32 devices in a mesh: ulysses: 4 (over z), blk: 8 (over y, x, core).
Axes of the slice: x: 2, y: 2, z: 4, core: 2. Of those that a mesh axis runs over, the one named last changes fastest.
Arguments:
- tokens: bfloat16 [4096, 1536], P(('ulysses', 'blk')), may hold values from -6 to 6
- lengths: int32 [3], replicated, may hold values from 1 to 2048, 4096 in all
- routes: int32 [4096, 8], P(('ulysses', 'blk')), may hold values from 0 to 15, all different within a row; in each aligned block of 128 rows (0 to 127, 128 to 255, ...) at most 96 rows name the same one
- gain_attn: bfloat16 [1536], P(('ulysses', 'blk')), may hold values from 0.5 to 1.5
- w_query: bfloat16 [1536, 1536], P(('ulysses', 'blk')), may hold values from -0.21875 to 0.21875
- key_projection: bfloat16 [1536, 512], P(('ulysses', 'blk')), may hold values from -0.15625 to 0.15625
- value_projection: bfloat16 [1536, 512], P(('ulysses', 'blk')), may hold values from -0.15625 to 0.15625
- w_output: bfloat16 [1536, 1536], P(('ulysses', 'blk')), may hold values from -2.5 to 2.5
- gain_moe: bfloat16 [1536], P(('ulysses', 'blk')), may hold values from 0.5 to 1.5
- w_router: bfloat16 [1536, 16], P(('ulysses', 'blk')), may hold values from -0.078125 to 0.078125
- w_inner: bfloat16 [16, 1536, 1024], P('blk', 'ulysses'), may hold values from -0.15625 to 0.15625
- w_outer: bfloat16 [16, 512, 1536], P('blk', None, 'ulysses'), may hold values from -1 to 1
- cotangent: bfloat16 [4096, 1536], P(('ulysses', 'blk')), may hold values from -6 to 6
Outputs:
- out: float32 [4096, 1536], P(('ulysses', 'blk'))
- d_tokens: float32 [4096, 1536], P(('ulysses', 'blk'))
- d_gain_attn: float32 [1536], P(('ulysses', 'blk'))
- d_w_query: float32 [1536, 1536], P(('ulysses', 'blk'))
- d_w_key: float32 [1536, 512], P(('ulysses', 'blk'))
- d_w_value: float32 [1536, 512], P(('ulysses', 'blk'))
- d_w_output: float32 [1536, 1536], P(('ulysses', 'blk'))
- d_gain_moe: float32 [1536], P(('ulysses', 'blk'))
- d_w_router: float32 [1536, 16], P(('ulysses', 'blk'))
- d_w_inner: float32 [16, 1536, 1024], P('blk', 'ulysses')
- d_w_outer: float32 [16, 512, 1536], P('blk', None, 'ulysses')
The draws below stay inside these ranges and needn't reach their ends.
Inputs may be any that keep to these rules, and one draw needn't show every extreme that they name: `lengths`: the 3 sequences fill the 4096 rows in order; the longest has exactly 2048 rows. `routes`: A row names 8 different experts; among the rows of one device no expert is named by more than 96 rows, and some expert reaches 96.
All inputs are finite; a program needn't handle non-finite values.
Results may differ from the reference program's by a relative error of at most 0.04.
Values may be sent and summed in bfloat16 or wider, within the bound.
A program may use at most 192 MiB of HBM per device.

```python
import math
from functools import partial
import jax
import jax.numpy as jnp
import numpy as np
from jax import lax

MODEL_WIDTH = 1536
QUERY_HEADS = 24
KEY_VALUE_HEADS = 8
HEAD_WIDTH = 64
FF = 512
TOPK = 8
TOK_DEV = 128
EXPERTS = 16
TOKENS = 4096
LONGEST_LENGTH = 2048
SEQS = 3
CAP = 96


def block_levels(rng, dims, cuts, smallest, top_value):
    factor_of = 1.0
    for axis_at, parts in cuts:
        heights = jax.random.uniform(jax.random.fold_in(jax.random.fold_in(rng, 6), axis_at), (parts,), jnp.float32, smallest / len(cuts), top_value / len(cuts))
        factor_of = factor_of * jnp.repeat(jnp.exp(heights), dims[axis_at] // parts).reshape((-1,) + (1,) * (len(dims) - 1 - axis_at))
    return factor_of


def length_profile(count, total, limit, lean):
    loads = [(1 << 20) // math.isqrt(grade ** lean) + 1 for grade in range(2, count + 1)]
    surplus, holding = total - limit - (count - 1), [1] * (count - 1)
    while surplus > 0:
        candidates = [i for i in range(count - 1) if holding[i] < limit]
        pool, left = sum([loads[i] for i in candidates]), surplus
        for i in candidates:
            addition = min(limit - holding[i], max(1, left * loads[i] // pool), surplus)
            holding[i] = holding[i] + addition
            surplus = surplus - addition
    return np.array([limit] + holding)


def uneven(stream_key, number_of, total, most, lean):
    if number_of == 2:
        one = jax.random.randint(stream_key, (), max(1, total - most), min(most, total - 1) + 1)
        return jnp.stack([one, total - one])
    sizes = jnp.asarray(length_profile(number_of, total, most, lean), jnp.int32)
    twos = (number_of - 1) // 2
    source_of, sink = sizes[1:1 + 2 * twos:2], sizes[2:2 + 2 * twos:2]
    margin = jnp.minimum(source_of - 1, most - sink)
    moved = jax.random.randint(jax.random.fold_in(stream_key, 1), (twos,), 0, 1 << 20) % (margin + 1)
    sizes = sizes.at[1:1 + 2 * twos:2].set(source_of - moved).at[2:2 + 2 * twos:2].set(sink + moved)
    return sizes[jax.random.permutation(jax.random.fold_in(stream_key, 2), number_of)]


def routed_block(rng, own, number, rows, amount, top, most, skew):
    order = jax.random.permutation(rng, amount)
    packed, ordinary = load_shares(amount, rows * top, most, skew, True), load_shares(amount, rows * top, most, skew, False)
    places = jnp.arange(amount)

    def named(sizes, turn):
        used = int((sizes > 0).sum())
        fixed = max(1, used // 4)
        shifted = fixed + (places - fixed + turn * (used - fixed)) % max(1, amount - fixed)
        return jnp.zeros((amount,), jnp.int32).at[order[jnp.where(places < fixed, places, shifted)]].set(jnp.asarray(sizes, jnp.int32))

    sizes = jnp.where(number % 4 == 0, named(packed, number // 4), named(ordinary, number - number // 4 - 1))
    mixed = jax.random.permutation(jax.random.fold_in(own, 3), amount)
    donor, receiver = mixed[0:amount // 2 * 2:2], mixed[1:amount // 2 * 2:2]
    margin = jnp.minimum(sizes[donor] - 1, most - sizes[receiver]) // 2
    margin = jnp.where((donor == order[0]) | (receiver == order[0]) | (sizes[receiver] == 0), 0, jnp.maximum(margin, 0))
    shifted = jax.random.randint(jax.random.fold_in(own, 4), (amount // 2,), 0, 1 << 20) % (margin + 1)
    sizes = sizes.at[donor].add(-shifted).at[receiver].add(shifted)
    members = jnp.searchsorted(jnp.cumsum(sizes), jnp.arange(rows * top), side="right").astype(jnp.int32)
    grid = members.reshape(top, rows).T
    grid = grid[jax.random.permutation(jax.random.fold_in(own, 1), rows)]
    turn = jax.random.randint(jax.random.fold_in(own, 2), (rows, 1), 0, top)
    return jnp.take_along_axis(grid, (jnp.arange(top)[None, :] + turn) % top, axis=1)


def load_shares(number_of, total, most, skew, full):
    loads = [(1 << 20) // math.isqrt(standing ** skew) + 1 for standing in range(1, number_of + 1)]
    largest = most if full else min(most, max(-(-total // number_of), total * loads[0] // sum(loads)))
    least = 1 if total - largest >= number_of - 1 else 0
    given, surplus = [largest] + [least] * (number_of - 1), total - largest - least * (number_of - 1)
    while surplus > 0:
        movable = [i for i in range(1, number_of) if given[i] < largest] or [i for i in range(1, number_of) if given[i] < most]
        mass, left = sum([loads[i] for i in movable]), surplus
        for i in movable:
            addition = min(most - given[i], max(1, left * loads[i] // mass), surplus)
            given[i] = given[i] + addition
            surplus = surplus - addition
    return np.array(given)


def scatter_about(own_key, extent, scale, limit, split=(), kind=jnp.bfloat16):
    values = scale * jax.random.normal(own_key, extent, jnp.float32)
    if split:
        values = values * block_levels(own_key, extent, split, -0.22, 0.18)
    return jnp.clip(values, -limit, limit).astype(kind)


def setup_inputs(seed: int = 0) -> dict:
    keys = jax.random.split(jax.random.key(seed), 14)
    tokens = scatter_about(keys[0], (TOKENS, MODEL_WIDTH), 1.0, 6.0, ((0, 32),))
    lengths = uneven(keys[1], SEQS, TOKENS, LONGEST_LENGTH, 2).astype(jnp.int32)
    routes_keys = jax.random.split(jax.random.fold_in(keys[2], 1), TOKENS // TOK_DEV)
    routes_turns = jax.random.permutation(jax.random.fold_in(keys[2], 3), TOKENS // TOK_DEV)
    routes = jax.vmap(lambda own, number: routed_block(jax.random.fold_in(keys[2], 2), own, number, TOK_DEV, EXPERTS, TOPK, CAP, 1))(routes_keys, routes_turns).reshape((TOKENS, TOPK))
    gain_attn = jnp.clip(1.0 + 0.1 * jax.random.normal(keys[3], (MODEL_WIDTH,), jnp.float32), 0.5, 1.5).astype(jnp.bfloat16)
    w_query = scatter_about(keys[4], (MODEL_WIDTH, QUERY_HEADS * HEAD_WIDTH), (MODEL_WIDTH // 2) ** -0.5, 0.21875, ((0, 32),))
    key_projection = scatter_about(keys[5], (MODEL_WIDTH, KEY_VALUE_HEADS * HEAD_WIDTH), MODEL_WIDTH ** -0.5, 0.15625, ((0, 32),))
    value_projection = scatter_about(keys[6], (MODEL_WIDTH, KEY_VALUE_HEADS * HEAD_WIDTH), MODEL_WIDTH ** -0.5, 0.15625, ((0, 32),))
    w_output = scatter_about(keys[7], (QUERY_HEADS * HEAD_WIDTH, MODEL_WIDTH), (QUERY_HEADS * HEAD_WIDTH // 256) ** -0.5, 2.5, ((0, 32),))
    gain_moe = jnp.clip(1.0 + 0.1 * jax.random.normal(keys[8], (MODEL_WIDTH,), jnp.float32), 0.5, 1.5).astype(jnp.bfloat16)
    w_router = scatter_about(keys[9], (MODEL_WIDTH, EXPERTS), (4 * MODEL_WIDTH) ** -0.5, 0.078125, ((0, 32),))
    w_inner = scatter_about(keys[10], (EXPERTS, MODEL_WIDTH, 2 * FF), MODEL_WIDTH ** -0.5, 0.15625, ((0, 8), (1, 4)))
    w_outer = scatter_about(keys[11], (EXPERTS, FF, MODEL_WIDTH), (FF // 16) ** -0.5, 1.0, ((0, 8), (2, 4)))
    cotangent = scatter_about(keys[12], (TOKENS, MODEL_WIDTH), 1.0, 6.0, ((0, 32),))
    return dict(tokens=tokens, lengths=lengths, routes=routes, gain_attn=gain_attn, w_query=w_query, key_projection=key_projection, value_projection=value_projection, w_output=w_output, gain_moe=gain_moe, w_router=w_router, w_inner=w_inner, w_outer=w_outer, cotangent=cotangent)


@jax.custom_vjp
def low(v):
    return lax.optimization_barrier(v.astype(jnp.bfloat16)).astype(jnp.float32)

@jax.custom_vjp
def low_back(v):
    return v

def low_keep(v):
    return (low(v), None)

def low_pass(kept, grad):
    return (grad,)

def back_keep(v):
    return (v, None)

def back_low(kept, grad):
    return (low(grad),)
low.defvjp(low_keep, low_pass)
low_back.defvjp(back_keep, back_low)
EPSILON = 1e-05
THETA = 10000.0
NEGATIVE = -1e+30
FULL_PRECISION = lax.Precision.HIGHEST

def locate(global_rows, lengths):
    ends = jnp.cumsum(lengths)
    passed = global_rows[..., None] >= ends
    segment = lax.optimization_barrier(jnp.sum(passed.astype(jnp.int32), axis=-1))
    opening = lax.optimization_barrier(jnp.sum(jnp.where(passed, lengths, 0), axis=-1))
    return (segment, global_rows - opening)

def rope_tables(positions, head_size):
    halves = head_size // 2
    frequency = THETA ** (-(jnp.arange(halves, dtype=jnp.float32) * 2.0 / head_size))
    angles = positions.astype(jnp.float32)[:, None] * frequency[None, :]
    return (jnp.cos(angles), jnp.sin(angles))

def rotate(value_tensor, cosine, sine_table):
    halves = value_tensor.shape[-1] // 2
    leading = value_tensor[..., :halves]
    trailing = value_tensor[..., halves:]
    cosine_rows = cosine[:, None, :]
    sine_rows = sine_table[:, None, :]
    return jnp.concatenate([leading * cosine_rows - trailing * sine_rows, trailing * cosine_rows + leading * sine_rows], axis=-1)

def norm_rows(value_tensor, gain):
    return value_tensor * lax.rsqrt(lax.optimization_barrier(jnp.mean(value_tensor * value_tensor, axis=-1, keepdims=True)) + EPSILON) * gain

def dispatch(route_rows, experts, capacity):
    flat_routes = route_rows.reshape(-1)
    onehot = (flat_routes[:, None] == jnp.arange(experts, dtype=jnp.int32)[None, :]).astype(jnp.int32)
    ranking = lax.optimization_barrier(jnp.sum(jnp.cumsum(onehot, axis=0) * onehot, axis=1)) - 1
    slot_place = flat_routes * capacity + ranking
    slot_count = flat_routes.shape[0]
    slot_of_row = jnp.full((experts * capacity,), slot_count, jnp.int32).at[slot_place].set(jnp.arange(slot_count, dtype=jnp.int32))
    return (slot_place, slot_of_row)

def attention(query_tensor, key_tensor, value_tensor, segments):
    rows_overall = query_tensor.shape[0]
    block_slice = min(512, rows_overall)
    span = LONGEST_LENGTH + block_slice
    heads_per_group = QUERY_HEADS // KEY_VALUE_HEADS
    scale = 1.0 / math.sqrt(HEAD_WIDTH)
    padded_keys = jnp.concatenate([jnp.zeros((LONGEST_LENGTH, KEY_VALUE_HEADS, HEAD_WIDTH), jnp.float32), key_tensor], axis=0)
    padded_values = jnp.concatenate([jnp.zeros((LONGEST_LENGTH, KEY_VALUE_HEADS, HEAD_WIDTH), jnp.float32), value_tensor], axis=0)
    segment_padded = jnp.concatenate([jnp.full((LONGEST_LENGTH,), -1, jnp.int32), segments], axis=0)

    def one_block(start_offset):
        query_rows = start_offset + jnp.arange(block_slice, dtype=jnp.int32)
        key_rows = start_offset - LONGEST_LENGTH + jnp.arange(span, dtype=jnp.int32)
        query_tile = lax.dynamic_slice_in_dim(query_tensor, start_offset, block_slice, 0).reshape(block_slice, KEY_VALUE_HEADS, heads_per_group, HEAD_WIDTH)
        key_block = lax.dynamic_slice_in_dim(padded_keys, start_offset, span, 0)
        value_block = lax.dynamic_slice_in_dim(padded_values, start_offset, span, 0)
        query_segs = lax.dynamic_slice_in_dim(segments, start_offset, block_slice, 0)
        key_segs = lax.dynamic_slice_in_dim(segment_padded, start_offset, span, 0)
        scores = low_back(jnp.einsum('qhgd,khd->qhgk', query_tile, key_block, precision=FULL_PRECISION) * scale)
        visible = (key_rows[None, :] <= query_rows[:, None]) & (key_segs[None, :] == query_segs[:, None])
        scores = jnp.where(visible[:, None, None, :], scores, NEGATIVE)
        probs = low(jax.nn.softmax(scores, axis=-1))
        mixed = jnp.einsum('qhgk,khd->qhgd', probs, value_block, precision=FULL_PRECISION)
        return mixed.reshape(block_slice, QUERY_HEADS, HEAD_WIDTH)
    starts = jnp.arange(rows_overall // block_slice, dtype=jnp.int32) * block_slice
    blocks = lax.map(jax.checkpoint(one_block), starts)
    return blocks.reshape(rows_overall, QUERY_HEADS, HEAD_WIDTH)

def reference(tokens, lengths, routes, gain_attn, w_query, key_projection, value_projection, w_output, gain_moe, w_router, w_inner, w_outer, cotangent):
    rows_overall = tokens.shape[0]
    expert_count = w_router.shape[1]
    capacity = 3 * TOK_DEV * TOPK // (2 * expert_count)
    global_rows = jnp.arange(rows_overall, dtype=jnp.int32)
    segments, positions = locate(global_rows, lengths)
    cosine, sine_table = rope_tables(positions, HEAD_WIDTH)
    block_count = rows_overall // TOK_DEV
    slot_place, slot_of_row = jax.vmap(partial(dispatch, experts=expert_count, capacity=capacity))(routes.reshape(block_count, TOK_DEV, TOPK))
    per_expert = jnp.transpose(slot_of_row.reshape(block_count, expert_count, capacity), (1, 0, 2))
    block_base = jnp.arange(block_count, dtype=jnp.int32)[None, :, None]
    filled = per_expert < TOK_DEV * TOPK
    token_index = jnp.where(filled, block_base * TOK_DEV + per_expert // TOPK, rows_overall).reshape(expert_count, block_count * capacity)
    gate_index = jnp.where(filled, block_base * TOK_DEV * TOPK + per_expert, rows_overall * TOPK).reshape(expert_count, block_count * capacity)

    def forward(params):
        inputs, attn_gain, query_weight, key_matrix, value_matrix, output_weight, moe_gain, router_weight, inner_weight, outer_weight = params
        first_hidden = low(norm_rows(inputs, attn_gain))
        query_lin = low_back(jnp.dot(first_hidden, query_weight, precision=FULL_PRECISION)).reshape(rows_overall, QUERY_HEADS, HEAD_WIDTH)
        key_linear = low_back(jnp.dot(first_hidden, key_matrix, precision=FULL_PRECISION)).reshape(rows_overall, KEY_VALUE_HEADS, HEAD_WIDTH)
        rows_of_value = low(low_back(jnp.dot(first_hidden, value_matrix, precision=FULL_PRECISION))).reshape(rows_overall, KEY_VALUE_HEADS, HEAD_WIDTH)
        query_rot = low(low_back(rotate(query_lin, cosine, sine_table)))
        key_rot = low(low_back(rotate(key_linear, cosine, sine_table)))
        mixed = low(low_back(attention(query_rot, key_rot, rows_of_value, segments)))
        attn_out = low_back(jnp.dot(mixed.reshape(rows_overall, QUERY_HEADS * HEAD_WIDTH), output_weight, precision=FULL_PRECISION))
        residual = inputs + attn_out
        hidden_two = low(norm_rows(residual, moe_gain))
        logits = low_back(jnp.dot(hidden_two, router_weight, precision=FULL_PRECISION))
        chosen = jnp.take_along_axis(logits, routes, axis=1)
        gates = jax.nn.softmax(chosen, axis=1)
        gates_flat = jnp.concatenate([gates.reshape(-1), jnp.zeros((1,), jnp.float32)])
        padded_hidden = jnp.concatenate([hidden_two, jnp.zeros((1, MODEL_WIDTH), jnp.float32)], axis=0)

        def expert_step(accumulated, pieces):
            inner_piece, outer_piece, token_piece, gate_piece = pieces
            expert_in = low_back(jnp.take(padded_hidden, token_piece, axis=0))
            gate_up = low_back(jnp.dot(expert_in, inner_piece, precision=FULL_PRECISION))
            activation = low(jax.nn.silu(gate_up[:, :FF]) * gate_up[:, FF:])
            expert_out = low(low_back(jnp.dot(activation, outer_piece, precision=FULL_PRECISION)))
            weight_rows = jnp.take(gates_flat, gate_piece)
            return (accumulated.at[token_piece].add(weight_rows[:, None] * expert_out), None)
        starting = jnp.zeros((rows_overall + 1, MODEL_WIDTH), jnp.float32)
        accumulated, _ = lax.scan(jax.checkpoint(expert_step), starting, (inner_weight, outer_weight, token_index, gate_index))
        return residual + accumulated[:rows_overall]
    params = (tokens.astype(jnp.float32), gain_attn.astype(jnp.float32), w_query.astype(jnp.float32), key_projection.astype(jnp.float32), value_projection.astype(jnp.float32), w_output.astype(jnp.float32), gain_moe.astype(jnp.float32), w_router.astype(jnp.float32), w_inner.astype(jnp.float32), w_outer.astype(jnp.float32))
    result, pullback = jax.vjp(forward, params)
    grads = pullback(cotangent.astype(jnp.float32))[0]
    return (result, grads[0], grads[1], grads[2], grads[3], grads[4], grads[5], grads[6], grads[7], grads[8], grads[9])
```

```python
import functools
import math

import jax
import jax.numpy as jnp
from jax import lax
from jax.experimental import pallas as pl
from jax.experimental.pallas import tpu as pltpu
from jax.sharding import PartitionSpec as P

D = 1536
HEADS = 24
KV = 8
HW = 64
GROUP = HEADS // KV
FF = 512
TOPK = 8
EXP_DEV = 2
LENMAX = 4096
EPS = 1e-05
THETA = 10000.0
NEG = -1e30
LANES = 128
AUX = 384
ROUTER_AT = 320
QCOLS = GROUP * HW

f32 = jnp.float32
bf16 = jnp.bfloat16
MESH = pl.DeviceIdType.MESH
ANY = pl.BlockSpec(memory_space=pl.ANY)
VMEM = pl.BlockSpec(memory_space=pltpu.VMEM)
DMA = pltpu.SemaphoreType.DMA
MIB = 1 << 20


def dev(u, b):
    return {"ulysses": u, "blk": b}


def remote(src, dst, ss, rs, u, b):
    return pltpu.make_async_remote_copy(
        src_ref=src, dst_ref=dst, send_sem=ss, recv_sem=rs,
        device_id=dev(u, b), device_id_type=MESH,
    )


def signal(sem, u, b):
    pl.semaphore_signal(sem, inc=1, device_id=dev(u, b), device_id_type=MESH)


class Layer:
    def __init__(self, nb):
        self.u = lax.axis_index("ulysses")
        self.b = lax.axis_index("blk")
        self.nb = nb
        self.nc = nb // 2
        self.chip = self.b // 2
        self.core = lax.rem(self.b, 2)
        self.sib = self.chip * 2 + 1 - self.core

    def peer(self, i):
        return lax.rem(self.chip + i, self.nc) * 2 + self.core

    def behind(self, i):
        return lax.rem(self.chip + self.nc - i, self.nc) * 2 + self.core

    def enter(self):
        bar = pltpu.get_barrier_semaphore()
        for i in range(1, self.nc):
            signal(bar, self.u, self.peer(i))
        signal(bar, self.u, self.sib)
        pl.semaphore_wait(bar, self.nc)


def gather_start(me, src, dst, ss, rs, fs, frs):
    sends = []
    for i in range(1, me.nc):
        c = remote(src, dst.at[me.b], ss.at[i], rs.at[i], me.u, me.peer(i))
        c.start()
        sends.append(c)
    c = remote(src, dst.at[me.b], fs.at[0], frs.at[0], me.u, me.sib)
    c.start()
    own = pltpu.make_async_copy(src, dst.at[me.b], ss.at[0])
    own.start()
    return sends, [c], own


def gather_forward(me, dst, state, fs, frs):
    sends, passed, _ = state
    for i in range(1, me.nc):
        sends[i - 1].wait_recv()
        at = me.behind(i)
        c = remote(dst.at[at], dst.at[at], fs.at[i], frs.at[i], me.u, me.sib)
        c.start()
        passed.append(c)


def gather_finish(state):
    sends, passed, own = state
    for c in sends:
        c.wait_send()
    for c in passed:
        c.wait()
    own.wait()


def gather_layer(x, nb, cid):
    nc = nb // 2

    def kernel(x_ref, o_ref, ss, rs, fs, frs):
        me = Layer(nb)
        me.enter()
        state = gather_start(me, x_ref, o_ref, ss, rs, fs, frs)
        gather_forward(me, o_ref, state, fs, frs)
        gather_finish(state)

    return pl.pallas_call(
        kernel,
        out_shape=jax.ShapeDtypeStruct((nb,) + x.shape, x.dtype),
        in_specs=[ANY],
        out_specs=ANY,
        scratch_shapes=[DMA((nc,))] * 4,
        compiler_params=pltpu.CompilerParams(collective_id=cid, has_side_effects=True),
        name="gather_layer%d" % cid,
    )(x)


def gather_inputs(x, gm, pieces, wo, nz, nb, cid):
    n = nz * nb
    nc = nb // 2
    groups, shard, _ = pieces.shape
    rp = nb // groups
    n_o = QCOLS // shard

    def kernel(x_ref, g_ref, p_ref, w_ref, xo, go, po, wo_out, ss, rs, fs, frs, ps, pr, ws, wr, ls):
        me = Layer(nb)
        lin = me.u * nb + me.b
        bar = pltpu.get_barrier_semaphore()

        def place(i):
            t = lax.rem(lin + i, n)
            return t // nb, lax.rem(t, nb)

        @pl.loop(1, n)
        def _(i):
            tz, tb = place(i)
            signal(bar, tz, tb)

        pl.semaphore_wait(bar, n - 1)
        xs = gather_start(me, x_ref, xo, ss.at[0], rs.at[0], fs.at[0], frs.at[0])

        def piece(i):
            tz, tb = place(i)
            return remote(p_ref.at[tb // rp], po.at[lin], ps.at[i], pr.at[i], tz, tb)

        @pl.loop(1, n)
        def _(i):
            piece(i).start()

        own = pltpu.make_async_copy(p_ref.at[me.b // rp], po.at[lin], ls.at[0])
        own.start()
        hg = lin // n_o
        slot = lax.rem(lin, n_o)

        def weight(zo, p):
            tz, tb = lax.rem(me.u + zo, nz), hg * rp + p
            k = zo * rp + p
            return tb, remote(w_ref, wo_out.at[slot], ws.at[k], wr.at[slot], tz, tb)

        keep = pltpu.make_async_copy(w_ref, wo_out.at[slot], ls.at[1])
        for zo in range(nz):
            for p in range(rp):
                tb, c = weight(zo, p)
                if zo:
                    c.start()
                else:
                    pl.when(tb != me.b)(c.start)
                    pl.when(tb == me.b)(keep.start)
        gs = gather_start(me, g_ref, go, ss.at[1], rs.at[1], fs.at[1], frs.at[1])
        gather_forward(me, xo, xs, fs.at[0], frs.at[0])

        @pl.loop(1, n)
        def _(i):
            piece(i).wait()

        own.wait()
        for zo in range(nz):
            for p in range(rp):
                tb, c = weight(zo, p)
                if zo:
                    c.wait_send()
                else:
                    pl.when(tb != me.b)(c.wait_send)
                    pl.when(tb == me.b)(keep.wait)
        for j in range(n_o):
            src = (me.b // rp) * n_o + j
            c = remote(w_ref, wo_out.at[j], ws.at[0], wr.at[j], me.u, me.sib)
            pl.when(src != lin)(c.wait_recv)
        gather_forward(me, go, gs, fs.at[1], frs.at[1])
        gather_finish(xs)
        gather_finish(gs)

    sh = jax.ShapeDtypeStruct
    return pl.pallas_call(
        kernel,
        out_shape=(
            sh((nb,) + x.shape, x.dtype),
            sh((nb,) + gm.shape, gm.dtype),
            sh((n, shard, AUX), bf16),
            sh((n_o, shard, D), bf16),
        ),
        in_specs=[ANY] * 4,
        out_specs=(ANY,) * 4,
        scratch_shapes=[DMA((2, nc))] * 4
        + [DMA((n,))] * 2
        + [DMA((nz * rp,)), DMA((n_o,)), DMA((2,))],
        compiler_params=pltpu.CompilerParams(collective_id=cid, has_side_effects=True),
        name="gather_inputs",
    )(x, gm, pieces, wo)


def halo_forward(kv, nz, nb, back, cid):
    def kernel(x_ref, o_ref, ss, rs):
        u = lax.axis_index("ulysses")
        b = lax.axis_index("blk")
        bar = pltpu.get_barrier_semaphore()
        for d in range(1, nz):
            signal(bar, lax.rem(u + d, nz), b)
        pl.semaphore_wait(bar, nz - 1)

        def copy(d):
            return remote(x_ref, o_ref.at[d - 1], ss.at[d - 1], rs.at[d - 1], u + d, b)

        for d in range(1, back + 1):
            pl.when(u + d < nz)(lambda d=d: copy(d).start())
        for d in range(1, back + 1):
            pl.when(u + d < nz)(lambda d=d: copy(d).wait_send())
            pl.when(u >= d)(lambda d=d: copy(d).wait_recv())

    return pl.pallas_call(
        kernel,
        out_shape=jax.ShapeDtypeStruct((back,) + kv.shape, kv.dtype),
        in_specs=[ANY],
        out_specs=ANY,
        scratch_shapes=[DMA((back,))] * 2,
        compiler_params=pltpu.CompilerParams(collective_id=cid, has_side_effects=True),
        name="halo_forward",
    )(kv)


def reduce_blocks(me, block, sib_out, sib_in, snd, land, ss, rs, fs, frs):
    nc = me.nc
    passed = []
    for i in [*range(1, nc), 0]:
        to = lax.rem(me.chip + i, nc) * 2 + 1 - me.core
        sib_out[i] = block(to).astype(bf16)
        c = remote(sib_out.at[i], sib_in.at[i], fs.at[i], frs.at[i], me.u, me.sib)
        c.start()
        passed.append(c)
    sends = []
    for i in range(1, nc):
        mine = block(me.peer(i))
        passed[i - 1].wait_recv()
        snd[i] = (mine + sib_in[i].astype(f32)).astype(bf16)
        c = remote(snd.at[i], land.at[i], ss.at[i], rs.at[i], me.u, me.peer(i))
        c.start()
        sends.append(c)
    total = block(me.b)
    passed[nc - 1].wait_recv()
    total = total + sib_in[0].astype(f32)
    for i in range(1, nc):
        sends[i - 1].wait_recv()
        total = total + land[i].astype(f32)
    for c in passed + sends:
        c.wait_send()
    return total


def reduce_scratch(nb, rows, cols):
    nc = nb // 2
    return [pltpu.VMEM((nc, rows, cols), bf16)] * 4 + [DMA((nc,))] * 4


def reduce_product(lhs, rhs, nb, cid, transpose_rhs=False):
    rows = lhs.shape[0] // nb
    cols = rhs.shape[0] if transpose_rhs else rhs.shape[1]
    dims = (((1,), (1,)), ((), ())) if transpose_rhs else (((1,), (0,)), ((), ()))

    def kernel(l_ref, r_ref, o_ref, *scratch):
        me = Layer(nb)
        me.enter()

        def block(t):
            part = l_ref[pl.ds(pl.multiple_of(t * rows, rows), rows), :]
            return lax.dot_general(part, r_ref[...], dims, preferred_element_type=f32)

        o_ref[...] = reduce_blocks(me, block, *scratch)

    return pl.pallas_call(
        kernel,
        out_shape=jax.ShapeDtypeStruct((rows, cols), f32),
        in_specs=[VMEM, VMEM],
        out_specs=VMEM,
        scratch_shapes=reduce_scratch(nb, rows, cols),
        compiler_params=pltpu.CompilerParams(
            collective_id=cid, has_side_effects=True, vmem_limit_bytes=48 * MIB
        ),
        name="reduce_product%d" % cid,
    )(lhs, rhs)


def reduce_ready(part, nb, cid):
    _, rows, cols = part.shape

    def kernel(p_ref, o_ref, *scratch):
        me = Layer(nb)
        me.enter()

        def block(t):
            return p_ref[t].astype(f32)

        o_ref[...] = reduce_blocks(me, block, *scratch)

    return pl.pallas_call(
        kernel,
        out_shape=jax.ShapeDtypeStruct((rows, cols), f32),
        in_specs=[VMEM],
        out_specs=VMEM,
        scratch_shapes=reduce_scratch(nb, rows, cols),
        compiler_params=pltpu.CompilerParams(
            collective_id=cid, has_side_effects=True, vmem_limit_bytes=48 * MIB
        ),
        name="reduce_ready%d" % cid,
    )(part)


def halo_back(dkv, ypart, dwo, nz, nb, rp, back, cid):
    _, rows, cols = ypart.shape
    n_o, shard, _ = dwo.shape
    R = dkv.shape[1]

    def kernel(d_ref, y_ref, w_ref, kin, o_ref, win, *scratch):
        ks, kr, ws, wr, ls = scratch[:5]
        me = Layer(nb)
        lin = me.u * nb + me.b
        first = (me.b // rp) * rp
        part = lax.rem(me.b, rp)
        n = nz * nb
        bar = pltpu.get_barrier_semaphore()

        @pl.loop(1, n)
        def _(i):
            t = lax.rem(lin + i, n)
            signal(bar, t // nb, lax.rem(t, nb))

        pl.semaphore_wait(bar, n - 1)

        def copy(d, p):
            k = d * rp + p
            return remote(d_ref.at[d], kin.at[d * rp + part], ks.at[k], kr.at[d * rp + part], me.u - d, first + p)

        def arrival(d, p):
            k = d * rp + p
            return remote(d_ref.at[d], kin.at[k], ks.at[k], kr.at[k], me.u, me.sib)

        for d in range(back + 1):
            for p in range(rp):
                if d:
                    pl.when(me.u >= d)(lambda d=d, p=p: copy(d, p).start())
                elif rp > 1:
                    pl.when(part != p)(lambda d=d, p=p: copy(d, p).start())

        def weight(j):
            t = (me.b // rp) * n_o + j
            at = me.u * rp + part
            return t, remote(w_ref.at[j], win.at[at], ws.at[j], wr.at[at], t // nb, lax.rem(t, nb))

        for j in range(n_o):
            t, c = weight(j)
            keep = pltpu.make_async_copy(w_ref.at[j], win.at[me.u * rp + part], ls.at[0])
            pl.when(t != lin)(c.start)
            pl.when(t == lin)(keep.start)

        def block(t):
            return y_ref[t].astype(f32)

        o_ref[...] = reduce_blocks(me, block, *scratch[5:])

        for d in range(back + 1):
            for p in range(rp):
                if d:
                    pl.when(me.u >= d)(lambda d=d, p=p: copy(d, p).wait_send())
                    pl.when(me.u + d < nz)(lambda d=d, p=p: arrival(d, p).wait_recv())
                elif rp > 1:
                    pl.when(part != p)(lambda d=d, p=p: copy(d, p).wait_send())
                    pl.when(part != p)(lambda d=d, p=p: arrival(d, p).wait_recv())
        for j in range(n_o):
            t, c = weight(j)
            keep = pltpu.make_async_copy(w_ref.at[j], win.at[me.u * rp + part], ls.at[0])
            pl.when(t != lin)(c.wait_send)
            pl.when(t == lin)(keep.wait)
        hg = lin // n_o
        for z in range(nz):
            for p in range(rp):
                k = z * rp + p
                c = remote(w_ref.at[0], win.at[k], ws.at[0], wr.at[k], me.u, me.sib)
                pl.when(z * nb + hg * rp + p != lin)(c.wait_recv)

    sh = jax.ShapeDtypeStruct
    return pl.pallas_call(
        kernel,
        out_shape=(
            sh(((back + 1) * rp, R, LANES), bf16),
            sh((rows, cols), f32),
            sh((nz * rp, shard, D), bf16),
        ),
        in_specs=[ANY, VMEM, ANY],
        out_specs=(ANY, VMEM, ANY),
        scratch_shapes=[DMA(((back + 1) * rp,))] * 2
        + [DMA((n_o,)), DMA((nz * rp,)), DMA((1,))]
        + reduce_scratch(nb, rows, cols),
        compiler_params=pltpu.CompilerParams(
            collective_id=cid, has_side_effects=True, vmem_limit_bytes=48 * MIB
        ),
        name="halo_back",
    )(dkv, ypart, dwo)


def reduce_last(lhs, rhs, pieces, nz, nb, cid):
    rows = lhs.shape[0] // nb
    cols = rhs.shape[0]
    n, shard, width = pieces.shape

    def kernel(l_ref, r_ref, p_ref, o_ref, pin, *scratch):
        ps, pr, ls = scratch[:3]
        me = Layer(nb)
        lin = me.u * nb + me.b
        bar = pltpu.get_barrier_semaphore()

        def place(i):
            t = lax.rem(lin + i, n)
            return t, t // nb, lax.rem(t, nb)

        @pl.loop(1, n)
        def _(i):
            _, tz, tb = place(i)
            signal(bar, tz, tb)

        pl.semaphore_wait(bar, n - 1)

        def piece(i):
            t, tz, tb = place(i)
            return remote(p_ref.at[t], pin.at[lin], ps.at[i], pr.at[i], tz, tb)

        @pl.loop(1, n)
        def _(i):
            piece(i).start()

        own = pltpu.make_async_copy(p_ref.at[lin], pin.at[lin], ls.at[0])
        own.start()

        def block(t):
            part = l_ref[pl.ds(pl.multiple_of(t * rows, rows), rows), :]
            return lax.dot_general(
                part, r_ref[...], (((1,), (1,)), ((), ())), preferred_element_type=f32
            )

        o_ref[...] = reduce_blocks(me, block, *scratch[3:])

        @pl.loop(1, n)
        def _(i):
            piece(i).wait()

        own.wait()

    sh = jax.ShapeDtypeStruct
    return pl.pallas_call(
        kernel,
        out_shape=(sh((rows, cols), f32), sh((n, shard, width), bf16)),
        in_specs=[VMEM, VMEM, ANY],
        out_specs=(VMEM, ANY),
        scratch_shapes=[DMA((n,))] * 2 + [DMA((1,))] + reduce_scratch(nb, rows, cols),
        compiler_params=pltpu.CompilerParams(
            collective_id=cid, has_side_effects=True, vmem_limit_bytes=48 * MIB
        ),
        name="reduce_last",
    )(lhs, rhs, pieces)


def turn(a, c, s1, s2):
    return a * c + pltpu.roll(a, LANES - HW // 2, 1) * s1 + pltpu.roll(a, HW // 2, 1) * s2


def project(x, gain, wbig, c, s1, s2):
    R = x.shape[0]
    step = 256

    def kernel(x_ref, g_ref, w_ref, c_ref, a_ref, b_ref, q_ref, kv_ref, h_ref):
        v = x_ref[...].astype(f32)
        inv = lax.rsqrt(jnp.mean(v * v, axis=1, keepdims=True) + EPS)
        h = (v * inv * g_ref[...]).astype(bf16)
        h_ref[...] = h
        out = jnp.dot(h, w_ref[...], preferred_element_type=f32)
        tables = (c_ref[...], a_ref[...], b_ref[...])
        for k in range(GROUP):
            q = turn(out[:, k * LANES:(k + 1) * LANES], *tables)
            q_ref[k] = (q.astype(bf16).astype(f32) * (1.0 / math.sqrt(HW))).astype(bf16)
        kv_ref[...] = turn(out[:, GROUP * LANES:], *tables).astype(bf16)

    row = lambda w: pl.BlockSpec((step, w), lambda i: (i, 0))
    whole = lambda a: pl.BlockSpec(a.shape, lambda i: (0, 0))
    sh = jax.ShapeDtypeStruct
    return pl.pallas_call(
        kernel,
        grid=(R // step,),
        out_shape=(sh((GROUP, R, LANES), bf16), sh((R, LANES), bf16), sh((R, D), bf16)),
        in_specs=[row(D), whole(gain), whole(wbig), row(LANES), row(LANES), row(LANES)],
        out_specs=(pl.BlockSpec((GROUP, step, LANES), lambda i: (0, i, 0)), row(LANES), row(D)),
        compiler_params=pltpu.CompilerParams(vmem_limit_bytes=32 * MIB),
        name="project",
    )(x, gain, wbig, c, s1, s2)


BQ = 256
BK = 512


def seen(meta, st, i, kb, nq):
    qpos = meta[nq] + i * BQ + lax.broadcasted_iota(jnp.int32, (BQ, 1), 0)
    kpos = kb * BK + lax.broadcasted_iota(jnp.int32, (1, BK), 1)
    return ((kpos <= qpos) & (kpos >= st))[None]


NT = (((1,), (1,)), ((), ()))
NN = (((1,), (0,)), ((), ()))
TN = (((0,), (0,)), ((), ()))


def attend(q, kv, starts, meta):
    _, Rq, _ = q.shape
    nq = Rq // BQ
    M = GROUP * BQ

    def kernel(meta, q_ref, kv_ref, st_ref, o_ref, l_ref):
        i = pl.program_id(0)
        qv = q_ref[...].reshape(M, LANES)
        st = st_ref[...]
        last = (meta[nq] + i * BQ + BQ - 1) // BK + 1

        def step(kb, carry):
            m, l, acc = carry
            keys = kv_ref[pl.ds(pl.multiple_of(kb * BK, BK), BK), :]
            s = lax.dot_general(qv, keys, NT, preferred_element_type=f32).reshape(GROUP, BQ, BK)
            s = jnp.where(seen(meta, st, i, kb, nq), s, NEG)
            m2 = jnp.maximum(m, jnp.max(s, axis=2, keepdims=True))
            w = jnp.exp(s - m2)
            f = jnp.exp(m - m2)
            l = l * f + jnp.sum(w, axis=2, keepdims=True)
            pv = lax.dot_general(w.astype(bf16).reshape(M, BK), keys, NN, preferred_element_type=f32)
            return m2, l, acc * f + pv.reshape(GROUP, BQ, LANES)

        init = (
            jnp.full((GROUP, BQ, 1), NEG, f32),
            jnp.zeros((GROUP, BQ, 1), f32),
            jnp.zeros((GROUP, BQ, LANES), f32),
        )
        m, l, acc = lax.fori_loop(meta[i], last, step, init)
        lane = lax.broadcasted_iota(jnp.int32, (1, 1, LANES), 2)
        o_ref[...] = jnp.where(lane >= HW, acc / l, 0.0).astype(bf16)
        l_ref[...] = m + jnp.log(l)

    sh = jax.ShapeDtypeStruct
    blk = lambda w: pl.BlockSpec((GROUP, BQ, w), lambda i, m: (0, i, 0))
    return pl.pallas_call(
        kernel,
        grid_spec=pltpu.PrefetchScalarGridSpec(
            num_scalar_prefetch=1,
            grid=(nq,),
            in_specs=[
                blk(LANES),
                pl.BlockSpec(kv.shape, lambda i, m: (0, 0)),
                pl.BlockSpec((BQ, 1), lambda i, m: (i, 0)),
            ],
            out_specs=(blk(LANES), blk(1)),
        ),
        out_shape=(sh((GROUP, Rq, LANES), bf16), sh((GROUP, Rq, 1), f32)),
        compiler_params=pltpu.CompilerParams(vmem_limit_bytes=48 * MIB),
        name="attend",
    )(meta, q, kv, starts)


def attend_back(q, kv, starts, meta, lse, mixed, do):
    _, Rq, _ = q.shape
    nq = Rq // BQ
    M = GROUP * BQ
    K = kv.shape[0]

    def kernel(meta, q_ref, kv_ref, st_ref, l_ref, o_ref, g_ref, dq_ref, dkv_ref):
        i = pl.program_id(0)

        @pl.when(i == 0)
        def _():
            dkv_ref[...] = jnp.zeros_like(dkv_ref)

        qv = q_ref[...].reshape(M, LANES)
        do = g_ref[...].reshape(M, LANES)
        lse = l_ref[...]
        delta = jnp.sum(
            g_ref[...].astype(f32) * o_ref[...].astype(f32), axis=2, keepdims=True
        )
        st = st_ref[...]
        last = (meta[nq] + i * BQ + BQ - 1) // BK + 1

        def step(kb, dq):
            at = pl.ds(pl.multiple_of(kb * BK, BK), BK)
            keys = kv_ref[at, :]
            s = lax.dot_general(qv, keys, NT, preferred_element_type=f32).reshape(GROUP, BQ, BK)
            p = jnp.where(seen(meta, st, i, kb, nq), jnp.exp(s - lse), 0.0)
            dp = lax.dot_general(do, keys, NT, preferred_element_type=f32).reshape(GROUP, BQ, BK)
            ds = (p * (dp - delta)).astype(bf16).reshape(M, BK)
            pb = p.astype(bf16).reshape(M, BK)
            dkv_ref[at, :] += lax.dot_general(
                ds, qv, TN, preferred_element_type=f32
            ) + lax.dot_general(pb, do, TN, preferred_element_type=f32)
            return dq + lax.dot_general(ds, keys, NN, preferred_element_type=f32)

        dq = lax.fori_loop(meta[i], last, step, jnp.zeros((M, LANES), f32))
        lane = lax.broadcasted_iota(jnp.int32, (1, LANES), 1)
        dq = jnp.where(lane < HW, dq * (1.0 / math.sqrt(HW)), 0.0)
        dq_ref[...] = dq.astype(bf16).reshape(GROUP, BQ, LANES)

    sh = jax.ShapeDtypeStruct
    blk = lambda w: pl.BlockSpec((GROUP, BQ, w), lambda i, m: (0, i, 0))
    return pl.pallas_call(
        kernel,
        grid_spec=pltpu.PrefetchScalarGridSpec(
            num_scalar_prefetch=1,
            grid=(nq,),
            in_specs=[
                blk(LANES),
                pl.BlockSpec(kv.shape, lambda i, m: (0, 0)),
                pl.BlockSpec((BQ, 1), lambda i, m: (i, 0)),
                blk(1),
                blk(LANES),
                blk(LANES),
            ],
            out_specs=(blk(LANES), pl.BlockSpec((K, LANES), lambda i, m: (0, 0))),
        ),
        out_shape=(sh((GROUP, Rq, LANES), bf16), sh((K, LANES), f32)),
        compiler_params=pltpu.CompilerParams(vmem_limit_bytes=48 * MIB),
        name="attend_back",
    )(meta, q, kv, starts, lse, mixed, do)


def locate(rows, lengths):
    passed = rows[:, None] >= jnp.cumsum(lengths)
    return jnp.sum(jnp.where(passed, lengths, 0), axis=-1)


def norm_rows(v, gain):
    inverse = lax.rsqrt(jnp.mean(v * v, axis=-1, keepdims=True) + EPS)
    normed = v * inverse
    return normed, inverse, normed * gain


def norm_back(upstream, normed, inverse, gain):
    d_normed = upstream * gain
    d_gain = jnp.sum(upstream * normed, axis=0)
    d_values = inverse * (d_normed - normed * jnp.mean(d_normed * normed, axis=-1, keepdims=True))
    return d_values, d_gain


def dot(a, b):
    return jnp.dot(a, b, preferred_element_type=f32)


def rows_of(a, start, count):
    return a if a.shape[0] == count else lax.dynamic_slice_in_dim(a, start, count, 0)


def widen(a, start, count):
    if a.shape[0] == count:
        return a
    return lax.dynamic_update_slice_in_dim(jnp.zeros((count,) + a.shape[1:], a.dtype), a, start, 0)


def on_device(tokens, lengths, routes, gain_attn, w_query, w_key, w_value, w_output, gain_moe,
              w_router, w_inner, w_outer, cotangent):
    nz = lax.axis_size("ulysses")
    nb = lax.axis_size("blk")
    z = lax.axis_index("ulysses")
    b = lax.axis_index("blk")
    T = tokens.shape[0]
    R = nb * T
    rp = nb // KV
    Rq = R // rp
    part = b % rp
    at = part * Rq
    n = nz * nb
    S = D // n
    E = w_router.shape[1]
    longest = min(LENMAX, n * T // 2)
    back = min(nz - 1, (longest - 1 + R - 1) // R)
    n_o = QCOLS // S

    inner = [lax.all_gather(w_inner[e], "ulysses", axis=0, tiled=True) for e in range(EXP_DEV)]
    outer = [lax.all_gather(w_outer[e], "ulysses", axis=1, tiled=True) for e in range(EXP_DEV)]

    tail = jnp.concatenate(
        [w_router, gain_attn[:, None], gain_moe[:, None],
         jnp.zeros((S, AUX - ROUTER_AT - E - 2), bf16)], axis=1)
    pieces = jnp.stack([
        jnp.concatenate([
            w_query[:, h * QCOLS:(h + 1) * QCOLS], w_key[:, h * HW:(h + 1) * HW],
            w_value[:, h * HW:(h + 1) * HW], tail], axis=1)
        for h in range(KV)])
    lanes = jnp.arange(LANES, dtype=jnp.int32)
    named = jnp.any(routes[:, :, None] == lanes[None, None, :], axis=1)
    cot_mask = jnp.concatenate([cotangent, named.astype(bf16)], axis=1)
    xg, gg, packed, wo = gather_inputs(tokens, cot_mask, pieces, w_output, nz, nb, 0)
    xg = xg.reshape(R, D)
    gg = gg.reshape(R, D + LANES)
    packed = packed.reshape(D, AUX)
    wo = wo.reshape(QCOLS, D)
    router = packed[:, ROUTER_AT:ROUTER_AT + E]
    gains = packed[:, ROUTER_AT + E:ROUTER_AT + E + 2].astype(f32).T
    gain1, gain2 = gains[0:1], gains[1:2]
    gap = jnp.zeros((D, LANES - HW), bf16)
    wbig = jnp.concatenate(
        sum([[packed[:, h * HW:(h + 1) * HW], gap] for h in range(GROUP)], [])
        + [packed[:, QCOLS:ROUTER_AT]], axis=1)
    gap = jnp.zeros((HW, D), bf16)
    wo_wide = jnp.concatenate(
        sum([[gap, wo[h * HW:(h + 1) * HW]] for h in range(GROUP)], []), axis=0)

    rows = z * R + jnp.arange(R, dtype=jnp.int32)
    opening = locate(rows, lengths)
    frequency = THETA ** (-(jnp.arange(HW // 2, dtype=f32) * 2.0 / HW))
    angles = (rows - opening).astype(f32)[:, None] * frequency[None, :]
    cos, sin = jnp.cos(angles), jnp.sin(angles)
    none = jnp.zeros((R, HW // 2), f32)
    half = jnp.zeros((R, HW), f32)
    tc = jnp.concatenate([cos, cos, half + 1.0], axis=1)
    ts1 = jnp.concatenate([-sin, none, half], axis=1)
    ts2 = jnp.concatenate([none, sin, half], axis=1)

    q, kv, h1 = project(xg, gain1, wbig, tc, ts1, ts2)
    if rp > 1:
        q = lax.dynamic_slice_in_dim(q, at, Rq, 1)
    far = halo_forward(kv, nz, nb, back, 1)
    kv_all = jnp.concatenate([far[d - 1] for d in range(back, 0, -1)] + [kv], axis=0)
    base = (z - back) * R
    starts = rows_of(opening, at, Rq) - base
    meta = jnp.concatenate([starts[::BQ] // BK, (back * R + at)[None]]).astype(jnp.int32)
    starts = starts[:, None]
    mixed, lse = attend(q, kv_all, starts, meta)
    mixed_rows = jnp.concatenate([mixed[h] for h in range(GROUP)], axis=1)
    attn = reduce_product(widen(mixed_rows, at, R), wo_wide, nb, 2)

    x = tokens.astype(f32)
    resid = x + attn
    n2, inv2, scaled2 = norm_rows(resid, gain2)
    h2_own = scaled2.astype(bf16)
    h2 = gather_layer(h2_own, nb, 3).reshape(R, D)

    def gates_of(hidden, mask):
        logits = dot(hidden, router)
        mask = mask > 0
        top = jnp.max(jnp.where(mask, logits, NEG), axis=1, keepdims=True)
        w = jnp.where(mask, jnp.exp(jnp.where(mask, logits - top, 0.0)), 0.0)
        return w / jnp.sum(w, axis=1, keepdims=True)

    gates = gates_of(h2, gg[:, D:D + E])
    gates = lax.dynamic_slice_in_dim(gates, b * EXP_DEV, EXP_DEV, 1)
    g = gg[:, :D]

    y = 0.0
    dh2 = 0.0
    extra = jnp.zeros((R, LANES), f32)
    inner_grads, outer_grads = [], []
    for e in range(EXP_DEV):
        gate = gates[:, e:e + 1]
        gu = dot(h2, inner[e])
        a, up = gu[:, :FF], gu[:, FF:]
        sg = jax.nn.sigmoid(a)
        silu = a * sg
        act = (silu * up).astype(bf16)
        y = y + gate * dot(act, outer[e])
        raw = lax.dot_general(g, outer[e], NT, preferred_element_type=f32)
        dgate = jnp.sum(act.astype(f32) * raw, axis=1, keepdims=True)
        dact = gate * raw
        dgu = jnp.concatenate(
            [dact * up * (sg * (1.0 + a * (1.0 - sg))), dact * silu], axis=1).astype(bf16)
        dy = (gate * g.astype(f32)).astype(bf16)
        d_out = lax.dot_general(act, dy, TN, preferred_element_type=f32).astype(bf16)
        d_in = lax.dot_general(h2, dgu, TN, preferred_element_type=f32).astype(bf16)
        inner_grads.append(lax.psum_scatter(d_in, "ulysses", scatter_dimension=0, tiled=True))
        outer_grads.append(lax.psum_scatter(d_out, "ulysses", scatter_dimension=1, tiled=True))
        dh2 = dh2 + lax.dot_general(dgu, inner[e], NT, preferred_element_type=f32)
        hi = dgate.astype(bf16).astype(f32)
        place = b * EXP_DEV + e
        extra = extra + jnp.where(lanes[None, :] == place, hi, 0.0)
        extra = extra + jnp.where(lanes[None, :] == place + HW, dgate - hi, 0.0)
    back_rows = jnp.concatenate([dh2.astype(bf16), extra.astype(bf16)], axis=1)
    summed = reduce_ready(back_rows.reshape(nb, T, D + LANES), nb, 4)
    y = y.astype(bf16).reshape(nb, T, D)

    upstream = cotangent.astype(f32)
    dgates = summed[:, D:D + E] + summed[:, D + HW:D + HW + E]
    own_gates = gates_of(h2_own, named[:, :E].astype(bf16))
    dlogits = own_gates * (dgates - jnp.sum(own_gates * dgates, axis=1, keepdims=True))
    dlogits = dlogits.astype(bf16)
    d_router = lax.dot_general(h2_own, dlogits, TN, preferred_element_type=f32)
    dh2_own = summed[:, :D] + lax.dot_general(dlogits, router, NT, preferred_element_type=f32)
    d_norm2, d_gain2 = norm_back(dh2_own, n2, inv2, gain2)
    dresid = upstream + d_norm2
    dattn = gather_layer(dresid.astype(bf16), nb, 5).reshape(R, D)

    dattn = rows_of(dattn, at, Rq)
    dmixed = lax.dot_general(dattn, wo_wide, NT, preferred_element_type=f32).astype(bf16)
    dmixed = jnp.stack([dmixed[:, h * LANES:(h + 1) * LANES] for h in range(GROUP)])
    dwo = lax.dot_general(mixed_rows, dattn, TN, preferred_element_type=f32).astype(bf16)
    dwo = jnp.concatenate(
        [dwo[h * LANES + HW:(h + 1) * LANES] for h in range(GROUP)], axis=0)
    dq, dkv = attend_back(q, kv_all, starts, meta, lse, mixed, dmixed)
    dkv = dkv.reshape(back + 1, R, LANES)
    dkv_out = jnp.stack([dkv[back - d] for d in range(back + 1)]).astype(bf16)
    kin, ysum, win = halo_back(dkv_out, y, dwo.reshape(n_o, S, D), nz, nb, rp, back, 6)
    out = resid + ysum
    d_output = jnp.sum(win.astype(f32), axis=0)

    dkv_own = rows_of(dkv[back], at, Rq)
    for d in range(back + 1):
        for p in range(rp):
            if d:
                ok = z + d < nz
            elif rp > 1:
                ok = part != p
            else:
                continue
            dkv_own = dkv_own + jnp.where(ok, rows_of(kin[d * rp + p], at, Rq).astype(f32), 0.0)
    flat = jnp.concatenate([dq[h] for h in range(GROUP)] + [dkv_own.astype(bf16)], axis=1)
    flat = flat.astype(f32).reshape(Rq, GROUP + 1, LANES)
    mc, m1, m2 = (rows_of(t, at, Rq)[:, None, :] for t in (tc, ts1, ts2))
    turned = (flat * mc - jnp.roll(flat, -(HW // 2), 2) * m1 - jnp.roll(flat, HW // 2, 2) * m2)
    turned = turned.astype(bf16).reshape(Rq, (GROUP + 1) * LANES)
    dw = lax.dot_general(rows_of(h1, at, Rq), turned, TN, preferred_element_type=f32)
    n1, inv1, _ = norm_rows(x, gain1)
    d_gain1 = jnp.sum(dw * wbig.astype(f32), axis=1) / gain1[0]
    narrow = jnp.concatenate(
        [dw[:, h * LANES:h * LANES + HW] for h in range(GROUP)]
        + [dw[:, GROUP * LANES:], d_router, d_gain2[:, None], d_gain1[:, None],
           jnp.zeros((D, AUX - ROUTER_AT - E - 2), f32)], axis=1).astype(bf16)
    dh1, pin = reduce_last(widen(turned, at, R), wbig, narrow.reshape(n, S, AUX), nz, nb, 7)
    d_norm1, _ = norm_back(dh1, n1, inv1, gain1)
    d_tokens = dresid + d_norm1

    pin = pin.astype(f32)
    small = jnp.sum(pin[:, :, ROUTER_AT:], axis=0)
    dqkv = jnp.sum(pin.reshape(nz, KV, rp, S, AUX)[..., :ROUTER_AT], axis=(0, 2))
    lay = lambda a: jnp.transpose(a, (1, 0, 2)).reshape(S, -1)
    d_query = lay(dqkv[:, :, :QCOLS])
    d_key = lay(dqkv[:, :, QCOLS:QCOLS + HW])
    d_value = lay(dqkv[:, :, QCOLS + HW:])
    return (
        out, d_tokens, small[:, E + 1], d_query, d_key, d_value, d_output,
        small[:, E], small[:, :E],
        jnp.stack(inner_grads).astype(f32), jnp.stack(outer_grads).astype(f32),
    )


def solution(mesh):
    both = ("ulysses", "blk")
    rows = P(both, None)
    weights = (P(both), rows, rows, rows, rows, P(both), rows, P("blk", "ulysses", None), P("blk", None, "ulysses"))
    return jax.shard_map(
        on_device,
        mesh=mesh,
        in_specs=(rows, P(), rows) + weights + (rows,),
        out_specs=(rows, rows) + weights,
        check_vma=False,
    )
```

```python
import functools
import math

import jax
import jax.numpy as jnp
from jax import lax
from jax.experimental import pallas as pl
from jax.experimental.pallas import tpu as pltpu
from jax.sharding import PartitionSpec as P

D = 1536
HEADS = 24
KV = 8
HW = 64
GROUP = HEADS // KV
FF = 512
TOPK = 8
EXP_DEV = 2
LENMAX = 4096
EPS = 1e-05
THETA = 10000.0
NEG = -1e30
LANES = 128
AUX = 384
ROUTER_AT = 320
QCOLS = GROUP * HW

f32 = jnp.float32
bf16 = jnp.bfloat16
MESH = pl.DeviceIdType.MESH
ANY = pl.BlockSpec(memory_space=pl.ANY)
VMEM = pl.BlockSpec(memory_space=pltpu.VMEM)
DMA = pltpu.SemaphoreType.DMA
MIB = 1 << 20


def dev(u, b):
    return {"ulysses": u, "blk": b}


def remote(src, dst, ss, rs, u, b):
    return pltpu.make_async_remote_copy(
        src_ref=src, dst_ref=dst, send_sem=ss, recv_sem=rs,
        device_id=dev(u, b), device_id_type=MESH,
    )


def cost(us):
    return pl.CostEstimate(flops=us * 1_000_000_000, bytes_accessed=0, transcendentals=0)


def signal(sem, u, b):
    pl.semaphore_signal(sem, inc=1, device_id=dev(u, b), device_id_type=MESH)


class Layer:
    def __init__(self, nb):
        self.u = lax.axis_index("ulysses")
        self.b = lax.axis_index("blk")
        self.nb = nb
        self.nc = nb // 2
        self.chip = self.b // 2
        self.core = lax.rem(self.b, 2)
        self.sib = self.chip * 2 + 1 - self.core

    def peer(self, i):
        return lax.rem(self.chip + i, self.nc) * 2 + self.core

    def behind(self, i):
        return lax.rem(self.chip + self.nc - i, self.nc) * 2 + self.core

    def across(self, d):
        at = self.u
        for k in range(d.bit_length()):
            if (d >> k) & 1:
                at = at + (1 << k) - (2 << k) * lax.rem(self.u // (1 << k), 2)
        return at

    def enter(self, flips=()):
        bar = pltpu.get_barrier_semaphore()
        for i in range(1, self.nc):
            signal(bar, self.u, self.peer(i))
        signal(bar, self.u, self.sib)
        for d in flips:
            signal(bar, self.across(d), self.b)
        pl.semaphore_wait(bar, self.nc + len(flips))


class Swaps:
    def __init__(self, items):
        self.items = items
        self.flips = sorted({d for _, d in items})
        self.arrays = [a for a, _ in items]
        self.shapes = tuple(jax.ShapeDtypeStruct(a.shape[-2:], a.dtype) for a in self.arrays)
        self.n = len(items)
        self.specs = [ANY] * self.n
        self.scratch = [DMA((2, max(self.n, 1)))]

    def start(self, me, srcs, dsts, sems):
        copies = []
        for k, (src, dst, (_, d)) in enumerate(zip(srcs, dsts, self.items)):
            if len(src.shape) == 3:
                odd = lax.rem(me.u, 2)
                src = src.at[1 - odd if d % 2 else odd]
            c = remote(src, dst, sems.at[0, k], sems.at[1, k], me.across(d), me.b)
            c.start()
            copies.append(c)
        return copies


def both(flips, *more):
    return sorted(set(flips) | set(more))


def gather_start(me, src, dst, ss, rs, fs, frs):
    sends = []
    for i in range(1, me.nc):
        c = remote(src, dst.at[me.b], ss.at[i], rs.at[i], me.u, me.peer(i))
        c.start()
        sends.append(c)
    c = remote(src, dst.at[me.b], fs.at[0], frs.at[0], me.u, me.sib)
    c.start()
    return sends, [c]


def gather_keep(me, src, dst, sem):
    c = pltpu.make_async_copy(src, dst.at[me.b], sem)
    c.start()
    return c


def gather_forward(me, dst, state, fs, frs):
    sends, passed = state
    for i in range(1, me.nc):
        sends[i - 1].wait_recv()
        at = me.behind(i)
        c = remote(dst.at[at], dst.at[at], fs.at[i], frs.at[i], me.u, me.sib)
        c.start()
        passed.append(c)


def gather_finish(state):
    sends, passed = state
    for c in sends:
        c.wait_send()
    for c in passed:
        c.wait()


def gather_layer(x, nb, cid, swaps):
    nc = nb // 2
    m = swaps.n

    def kernel(x_ref, *rest):
        srcs, o_ref, dsts = rest[:m], rest[m], rest[m + 1:2 * m + 1]
        ss, rs, fs, frs, ls, ws = rest[2 * m + 1:]
        me = Layer(nb)
        me.enter(swaps.flips)
        state = gather_start(me, x_ref, o_ref, ss, rs, fs, frs)
        moved = swaps.start(me, srcs, dsts, ws)
        own = gather_keep(me, x_ref, o_ref, ls)
        gather_forward(me, o_ref, state, fs, frs)
        gather_finish(state)
        own.wait()
        for c in moved:
            c.wait()

    return pl.pallas_call(
        kernel,
        out_shape=(jax.ShapeDtypeStruct((nb,) + x.shape, x.dtype),) + swaps.shapes,
        in_specs=[ANY] + swaps.specs,
        out_specs=(ANY,) + tuple(swaps.specs),
        scratch_shapes=[DMA((nc,))] * 4 + [DMA] + swaps.scratch,
        compiler_params=pltpu.CompilerParams(collective_id=cid, has_side_effects=True),
        cost_estimate=cost(22),
        name="gather_layer%d" % cid,
    )(x, *swaps.arrays)


def gather_pair(x, nb, cid, swaps):
    nc = nb // 2
    m = swaps.n

    def kernel(x_ref, *rest):
        srcs, o_ref, dsts = rest[:m], rest[m], rest[m + 1:2 * m + 1]
        ss, rs, fs, frs, zs, ls, ws = rest[2 * m + 1:]
        me = Layer(nb)
        me.enter(both(swaps.flips, 1))
        own, oth = o_ref.at[0], o_ref.at[1]
        mate = remote(x_ref, oth.at[me.b], zs.at[0], zs.at[1], me.across(1), me.b)
        mate.start()
        s0 = gather_start(me, x_ref, own, ss.at[0], rs.at[0], fs.at[0], frs.at[0])
        moved = swaps.start(me, srcs, dsts, ws)
        keep = gather_keep(me, x_ref, own, ls)
        mate.wait_recv()
        s1 = gather_start(me, oth.at[me.b], oth, ss.at[1], rs.at[1], fs.at[1], frs.at[1])
        gather_forward(me, own, s0, fs.at[0], frs.at[0])
        gather_forward(me, oth, s1, fs.at[1], frs.at[1])
        gather_finish(s0)
        gather_finish(s1)
        mate.wait_send()
        keep.wait()
        for c in moved:
            c.wait()

    return pl.pallas_call(
        kernel,
        out_shape=(jax.ShapeDtypeStruct((2, nb) + x.shape, x.dtype),) + swaps.shapes,
        in_specs=[ANY] + swaps.specs,
        out_specs=(ANY,) + tuple(swaps.specs),
        scratch_shapes=[DMA((2, nc))] * 4 + [DMA((2,)), DMA] + swaps.scratch,
        compiler_params=pltpu.CompilerParams(collective_id=cid, has_side_effects=True),
        cost_estimate=cost(38),
        name="gather_pair%d" % cid,
    )(x, *swaps.arrays)


def gather_inputs(x, gm, pieces, wo, nz, nb, cid, swaps):
    n = nz * nb
    nc = nb // 2
    groups, shard, _ = pieces.shape
    rp = nb // groups
    n_o = QCOLS // shard
    m = swaps.n

    def kernel(x_ref, g_ref, p_ref, w_ref, *rest):
        srcs = rest[:m]
        xo, go, gx, po, wo_out = rest[m:m + 5]
        dsts = rest[m + 5:2 * m + 5]
        ss, rs, fs, frs, ps, pr, zs, ws, wr, ls, sw = rest[2 * m + 5:]
        me = Layer(nb)
        lin = me.u * nb + me.b
        bar = pltpu.get_barrier_semaphore()

        def place(i):
            t = lax.rem(lin + i, n)
            return t // nb, lax.rem(t, nb)

        @pl.loop(1, n)
        def _(i):
            tz, tb = place(i)
            signal(bar, tz, tb)

        pl.semaphore_wait(bar, n - 1)

        def piece(i):
            tb = lax.rem(me.b + i, nb)
            return remote(p_ref.at[tb // rp], po.at[me.u, me.b], ps.at[i], pr.at[i], me.u, tb)

        for i in range(1, nb):
            piece(i).start()
        own = pltpu.make_async_copy(p_ref.at[me.b // rp], po.at[me.u, me.b], ls.at[0])
        own.start()
        xs = gather_start(me, x_ref, xo, ss.at[0], rs.at[0], fs.at[0], frs.at[0])
        for i in range(1, nb):
            piece(i).wait()
        own.wait()
        slabs = []
        for zo in range(1, nz):
            c = remote(po.at[me.u], po.at[me.u], zs.at[0, zo], zs.at[1, zo], lax.rem(me.u + zo, nz), me.b)
            c.start()
            slabs.append(c)
        hg = lin // n_o
        slot = lax.rem(lin, n_o)

        def weight(zo, p):
            tz, tb = lax.rem(me.u + zo, nz), hg * rp + p
            k = zo * rp + p
            return tb, remote(w_ref, wo_out.at[slot], ws.at[k], wr.at[slot], tz, tb)

        mate = remote(g_ref, gx, ls.at[2], ls.at[3], me.across(1), me.b)
        mate.start()
        keep = pltpu.make_async_copy(w_ref, wo_out.at[slot], ls.at[1])
        for zo in range(nz):
            for p in range(rp):
                tb, c = weight(zo, p)
                if zo:
                    c.start()
                else:
                    pl.when(tb != me.b)(c.start)
                    pl.when(tb == me.b)(keep.start)
        gs = gather_start(me, g_ref, go, ss.at[1], rs.at[1], fs.at[1], frs.at[1])
        moved = swaps.start(me, srcs, dsts, sw)
        xk = gather_keep(me, x_ref, xo, ls.at[4])
        gk = gather_keep(me, g_ref, go, ls.at[5])
        gather_forward(me, xo, xs, fs.at[0], frs.at[0])
        gather_forward(me, go, gs, fs.at[1], frs.at[1])
        for zo in range(nz):
            for p in range(rp):
                tb, c = weight(zo, p)
                if zo:
                    c.wait_send()
                else:
                    pl.when(tb != me.b)(c.wait_send)
                    pl.when(tb == me.b)(keep.wait)
        for j in range(n_o):
            src = (me.b // rp) * n_o + j
            c = remote(w_ref, wo_out.at[j], ws.at[0], wr.at[j], me.u, me.sib)
            pl.when(src != lin)(c.wait_recv)
        gather_finish(xs)
        gather_finish(gs)
        for c in slabs + moved:
            c.wait()
        mate.wait()
        xk.wait()
        gk.wait()

    sh = jax.ShapeDtypeStruct
    return pl.pallas_call(
        kernel,
        out_shape=(
            sh((nb,) + x.shape, x.dtype),
            sh((nb,) + gm.shape, gm.dtype),
            sh(gm.shape, gm.dtype),
            sh((nz, nb, shard, AUX), bf16),
            sh((n_o, shard, D), bf16),
        )
        + swaps.shapes,
        in_specs=[ANY] * (4 + m),
        out_specs=(ANY,) * (5 + m),
        scratch_shapes=[DMA((2, nc))] * 4
        + [DMA((nb,))] * 2
        + [DMA((2, nz)), DMA((nz * rp,)), DMA((n_o,)), DMA((6,))]
        + swaps.scratch,
        compiler_params=pltpu.CompilerParams(collective_id=cid, has_side_effects=True),
        cost_estimate=cost(50),
        name="gather_inputs",
    )(x, gm, pieces, wo, *swaps.arrays)


def halo_forward(kv, gx, nz, nb, back, cid, swaps):
    nc = nb // 2
    m = swaps.n

    def kernel(x_ref, g_ref, *rest):
        srcs = rest[:m]
        o_ref, go = rest[m:m + 2]
        dsts = rest[m + 2:2 * m + 2]
        ks, kr, ss, rs, fs, frs, ls, ws = rest[2 * m + 2:]
        me = Layer(nb)
        u, b = me.u, me.b
        bar = pltpu.get_barrier_semaphore()
        for d in range(1, nz):
            signal(bar, lax.rem(u + d, nz), b)
        for i in range(1, nc):
            signal(bar, u, me.peer(i))
        signal(bar, u, me.sib)
        pl.semaphore_wait(bar, nz - 1 + nc)

        def copy(d):
            return remote(x_ref, o_ref.at[d - 1], ks.at[d - 1], kr.at[d - 1], u + d, b)

        for d in range(1, back + 1):
            pl.when(u + d < nz)(lambda d=d: copy(d).start())
        state = gather_start(me, g_ref, go, ss, rs, fs, frs)
        moved = swaps.start(me, srcs, dsts, ws)
        keep = gather_keep(me, g_ref, go, ls)
        gather_forward(me, go, state, fs, frs)
        gather_finish(state)
        keep.wait()
        for c in moved:
            c.wait()
        for d in range(1, back + 1):
            pl.when(u + d < nz)(lambda d=d: copy(d).wait_send())
            pl.when(u >= d)(lambda d=d: copy(d).wait_recv())

    sh = jax.ShapeDtypeStruct
    return pl.pallas_call(
        kernel,
        out_shape=(sh((back,) + kv.shape, kv.dtype), sh((nb,) + gx.shape, gx.dtype)) + swaps.shapes,
        in_specs=[ANY] * (2 + m),
        out_specs=(ANY,) * (2 + m),
        scratch_shapes=[DMA((back,))] * 2 + [DMA((nc,))] * 4 + [DMA] + swaps.scratch,
        compiler_params=pltpu.CompilerParams(collective_id=cid, has_side_effects=True),
        cost_estimate=cost(20),
        name="halo_forward",
    )(kv, gx, *swaps.arrays)


def reduce_start(me, source, sib_in, fs, frs):
    passed = []
    for i in [*range(1, me.nc), 0]:
        to = lax.rem(me.chip + i, me.nc) * 2 + 1 - me.core
        c = remote(source(i, to), sib_in.at[i], fs.at[i], frs.at[i], me.u, me.sib)
        c.start()
        passed.append(c)
    return passed


def reduce_rest(me, block, passed, sib_in, snd, land, ss, rs):
    nc = me.nc
    sends = []
    for i in range(1, nc):
        mine = block(me.peer(i))
        passed[i - 1].wait_recv()
        snd[i] = (mine + sib_in[i].astype(f32)).astype(bf16)
        c = remote(snd.at[i], land.at[i], ss.at[i], rs.at[i], me.u, me.peer(i))
        c.start()
        sends.append(c)
    total = block(me.b)
    passed[nc - 1].wait_recv()
    return total + sib_in[0].astype(f32), sends


def reduce_end(me, total, passed, sends, land):
    for i in range(1, me.nc):
        sends[i - 1].wait_recv()
        total = total + land[i].astype(f32)
    for c in passed + sends:
        c.wait_send()
    return total


def reduce_made(me, block, sib_out, sib_in, snd, land, ss, rs, fs, frs):
    def source(i, to):
        sib_out[i] = block(to).astype(bf16)
        return sib_out.at[i]

    passed = reduce_start(me, source, sib_in, fs, frs)
    total, sends = reduce_rest(me, block, passed, sib_in, snd, land, ss, rs)
    return reduce_end(me, total, passed, sends, land)


def reduce_scratch(nb, rows, cols):
    nc = nb // 2
    return [pltpu.VMEM((nc, rows, cols), bf16)] * 4 + [DMA((nc,))] * 4


def reduce_pair_body(me, p_ref, sib_in, snd, land, zbuf, ss, rs, fs, frs, zs):
    block = lambda h: (lambda t: p_ref[h, t].astype(f32))
    source = lambda h: (lambda i, to: p_ref.at[h, to])
    p1 = reduce_start(me, source(1), sib_in.at[1], fs.at[1], frs.at[1])
    p0 = reduce_start(me, source(0), sib_in.at[0], fs.at[0], frs.at[0])
    t1, s1 = reduce_rest(me, block(1), p1, sib_in.at[1], snd.at[1], land.at[1], ss.at[1], rs.at[1])
    zbuf[0] = reduce_end(me, t1, p1, s1, land.at[1]).astype(bf16)
    across = remote(zbuf.at[0], zbuf.at[1], zs.at[0], zs.at[1], me.across(1), me.b)
    across.start()
    t0, s0 = reduce_rest(me, block(0), p0, sib_in.at[0], snd.at[0], land.at[0], ss.at[0], rs.at[0])
    t0 = reduce_end(me, t0, p0, s0, land.at[0])
    across.wait()
    return t0 + zbuf[1].astype(f32)


def reduce_pair_scratch(nb, rows, cols):
    nc = nb // 2
    return (
        [pltpu.VMEM((2, nc, rows, cols), bf16)] * 3
        + [pltpu.VMEM((2, rows, cols), bf16)]
        + [DMA((2, nc))] * 4
        + [DMA((2,))]
    )


def reduce_product(lhs, rhs, nb, cid, swaps):
    rows = lhs.shape[0] // nb
    cols = rhs.shape[1]
    m = swaps.n

    def kernel(l_ref, r_ref, *rest):
        srcs, o_ref, dsts = rest[:m], rest[m], rest[m + 1:2 * m + 1]
        ws, *scratch = rest[2 * m + 1:]
        me = Layer(nb)
        me.enter(swaps.flips)
        moved = swaps.start(me, srcs, dsts, ws)

        def block(t):
            part = l_ref[pl.ds(pl.multiple_of(t * rows, rows), rows), :]
            return jnp.dot(part, r_ref[...], preferred_element_type=f32)

        o_ref[...] = reduce_made(me, block, *scratch)
        for c in moved:
            c.wait()

    return pl.pallas_call(
        kernel,
        out_shape=(jax.ShapeDtypeStruct((rows, cols), f32),) + swaps.shapes,
        in_specs=[VMEM, VMEM] + swaps.specs,
        out_specs=(VMEM,) + tuple(swaps.specs),
        scratch_shapes=swaps.scratch + reduce_scratch(nb, rows, cols),
        compiler_params=pltpu.CompilerParams(
            collective_id=cid, has_side_effects=True, vmem_limit_bytes=48 * MIB
        ),
        cost_estimate=cost(23),
        name="reduce_product%d" % cid,
    )(lhs, rhs, *swaps.arrays)


def reduce_pair(part, nb, cid, swaps):
    _, _, rows, cols = part.shape
    m = swaps.n

    def kernel(p_ref, *rest):
        srcs, o_ref, dsts = rest[:m], rest[m], rest[m + 1:2 * m + 1]
        ws, *scratch = rest[2 * m + 1:]
        me = Layer(nb)
        me.enter(both(swaps.flips, 1))
        moved = swaps.start(me, srcs, dsts, ws)
        o_ref[...] = reduce_pair_body(me, p_ref, *scratch)
        for c in moved:
            c.wait()

    return pl.pallas_call(
        kernel,
        out_shape=(jax.ShapeDtypeStruct((rows, cols), f32),) + swaps.shapes,
        in_specs=[VMEM] + swaps.specs,
        out_specs=(VMEM,) + tuple(swaps.specs),
        scratch_shapes=swaps.scratch + reduce_pair_scratch(nb, rows, cols),
        compiler_params=pltpu.CompilerParams(
            collective_id=cid, has_side_effects=True, vmem_limit_bytes=56 * MIB
        ),
        cost_estimate=cost(48),
        name="reduce_pair%d" % cid,
    )(part, *swaps.arrays)


def halo_back(dkv, ypart, dwo, nz, nb, rp, back, cid):
    _, _, rows, cols = ypart.shape
    n_o, shard, _ = dwo.shape
    R = dkv.shape[1]

    def kernel(d_ref, y_ref, w_ref, kin, o_ref, win, *scratch):
        ks, kr, ws, wr, ls = scratch[:5]
        me = Layer(nb)
        lin = me.u * nb + me.b
        first = (me.b // rp) * rp
        part = lax.rem(me.b, rp)
        n = nz * nb
        bar = pltpu.get_barrier_semaphore()

        @pl.loop(1, n)
        def _(i):
            t = lax.rem(lin + i, n)
            signal(bar, t // nb, lax.rem(t, nb))

        pl.semaphore_wait(bar, n - 1)

        def copy(d, p):
            k = d * rp + p
            return remote(d_ref.at[d], kin.at[d * rp + part], ks.at[k], kr.at[d * rp + part], me.u - d, first + p)

        def arrival(d, p):
            k = d * rp + p
            return remote(d_ref.at[d], kin.at[k], ks.at[k], kr.at[k], me.u, me.sib)

        for d in range(back + 1):
            for p in range(rp):
                if d:
                    pl.when(me.u >= d)(lambda d=d, p=p: copy(d, p).start())
                elif rp > 1:
                    pl.when(part != p)(lambda d=d, p=p: copy(d, p).start())

        def weight(j):
            t = (me.b // rp) * n_o + j
            at = me.u * rp + part
            return t, remote(w_ref.at[j], win.at[at], ws.at[j], wr.at[at], t // nb, lax.rem(t, nb))

        for j in range(n_o):
            t, c = weight(j)
            keep = pltpu.make_async_copy(w_ref.at[j], win.at[me.u * rp + part], ls.at[0])
            pl.when(t != lin)(c.start)
            pl.when(t == lin)(keep.start)

        o_ref[...] = reduce_pair_body(me, y_ref, *scratch[5:])

        for d in range(back + 1):
            for p in range(rp):
                if d:
                    pl.when(me.u >= d)(lambda d=d, p=p: copy(d, p).wait_send())
                    pl.when(me.u + d < nz)(lambda d=d, p=p: arrival(d, p).wait_recv())
                elif rp > 1:
                    pl.when(part != p)(lambda d=d, p=p: copy(d, p).wait_send())
                    pl.when(part != p)(lambda d=d, p=p: arrival(d, p).wait_recv())
        for j in range(n_o):
            t, c = weight(j)
            keep = pltpu.make_async_copy(w_ref.at[j], win.at[me.u * rp + part], ls.at[0])
            pl.when(t != lin)(c.wait_send)
            pl.when(t == lin)(keep.wait)
        hg = lin // n_o
        for z in range(nz):
            for p in range(rp):
                k = z * rp + p
                c = remote(w_ref.at[0], win.at[k], ws.at[0], wr.at[k], me.u, me.sib)
                pl.when(z * nb + hg * rp + p != lin)(c.wait_recv)

    sh = jax.ShapeDtypeStruct
    return pl.pallas_call(
        kernel,
        out_shape=(
            sh(((back + 1) * rp, R, LANES), bf16),
            sh((rows, cols), f32),
            sh((nz * rp, shard, D), bf16),
        ),
        in_specs=[ANY, VMEM, ANY],
        out_specs=(ANY, VMEM, ANY),
        scratch_shapes=[DMA(((back + 1) * rp,))] * 2
        + [DMA((n_o,)), DMA((nz * rp,)), DMA((1,))]
        + reduce_pair_scratch(nb, rows, cols),
        compiler_params=pltpu.CompilerParams(
            collective_id=cid, has_side_effects=True, vmem_limit_bytes=56 * MIB
        ),
        cost_estimate=cost(45),
        name="halo_back",
    )(dkv, ypart, dwo)


def reduce_last(lhs, rhs, pieces, nz, nb, cid):
    rows = lhs.shape[0] // nb
    cols = rhs.shape[0]
    _, _, shard, width = pieces.shape

    def kernel(l_ref, r_ref, p_ref, o_ref, pin, slab, total, zs, zr, ps, pr, ls, *scratch):
        me = Layer(nb)
        bar = pltpu.get_barrier_semaphore()
        for i in range(1, nb):
            signal(bar, me.u, lax.rem(me.b + i, nb))
        for i in range(1, nz):
            signal(bar, lax.rem(me.u + i, nz), me.b)
        pl.semaphore_wait(bar, nb + nz - 2)
        across = []
        for i in range(1, nz):
            to = lax.rem(me.u + i, nz)
            c = remote(p_ref.at[to], slab.at[i], zs.at[i], zr.at[i], to, me.b)
            c.start()
            across.append(c)

        def block(t):
            part = l_ref[pl.ds(pl.multiple_of(t * rows, rows), rows), :]
            return lax.dot_general(part, r_ref[...], NT, preferred_element_type=f32)

        sib_out, sib_in, snd, land, ss, rs, fs, frs = scratch

        def source(i, to):
            sib_out[i] = block(to).astype(bf16)
            return sib_out.at[i]

        passed = reduce_start(me, source, sib_in, fs, frs)
        mine, sends = reduce_rest(me, block, passed, sib_in, snd, land, ss, rs)
        for c in across:
            c.wait_recv()
        out = []
        for t in range(nb):
            tile = p_ref[me.u, t].astype(f32)
            for i in range(1, nz):
                tile = tile + slab[i, t].astype(f32)
            total[t] = tile.astype(bf16)
        for i in range(1, nb):
            t = lax.rem(me.b + i, nb)
            c = remote(total.at[t], pin.at[me.b], ps.at[i], pr.at[i], me.u, t)
            c.start()
            out.append(c)
        own = pltpu.make_async_copy(total.at[me.b], pin.at[me.b], ls.at[0])
        own.start()
        o_ref[...] = reduce_end(me, mine, passed, sends, land)
        for c in across:
            c.wait_send()
        for c in out:
            c.wait()
        own.wait()

    sh = jax.ShapeDtypeStruct
    return pl.pallas_call(
        kernel,
        out_shape=(sh((rows, cols), f32), sh((nb, shard, width), bf16)),
        in_specs=[VMEM, VMEM, VMEM],
        out_specs=(VMEM, ANY),
        scratch_shapes=[pltpu.VMEM((nz, nb, shard, width), bf16), pltpu.VMEM((nb, shard, width), bf16)]
        + [DMA((nz,))] * 2
        + [DMA((nb,))] * 2
        + [DMA((1,))]
        + reduce_scratch(nb, rows, cols),
        compiler_params=pltpu.CompilerParams(
            collective_id=cid, has_side_effects=True, vmem_limit_bytes=56 * MIB
        ),
        cost_estimate=cost(37),
        name="reduce_last",
    )(lhs, rhs, pieces)


def turn(a, c, s1, s2):
    return a * c + pltpu.roll(a, LANES - HW // 2, 1) * s1 + pltpu.roll(a, HW // 2, 1) * s2


def turn_back(a, c, s1, s2):
    return a * c - pltpu.roll(a, LANES - HW // 2, 1) * s1 - pltpu.roll(a, HW // 2, 1) * s2


def swap(a):
    return pltpu.roll(a, HW, 1)


def low_half():
    return lax.broadcasted_iota(jnp.int32, (1, LANES), 1) < HW


def row_block(step, width):
    return pl.BlockSpec((step, width), lambda i: (i, 0))


def whole_block(a):
    zeros = (0,) * a.ndim
    return pl.BlockSpec(a.shape, lambda i: zeros)


def project(x, gain, packed, c, s1, s2):
    R = x.shape[0]
    step = 256

    def kernel(x_ref, g_ref, w_ref, c_ref, a_ref, b_ref, q_ref, kv_ref, h_ref):
        v = x_ref[...].astype(f32)
        inv = lax.rsqrt(jnp.mean(v * v, axis=1, keepdims=True) + EPS)
        h = (v * inv * g_ref[...]).astype(bf16)
        h_ref[...] = h
        out = jnp.dot(h, w_ref[...], preferred_element_type=f32)
        tables = (c_ref[...], a_ref[...], b_ref[...])
        low = low_half()
        t0 = turn(out[:, :LANES], *tables)
        t1 = turn(out[:, LANES:2 * LANES], *tables)
        scale = lambda a: (jnp.where(low, a, 0.0) * (1.0 / math.sqrt(HW))).astype(bf16)
        q_ref[0] = scale(t0)
        q_ref[1] = scale(swap(t0))
        q_ref[2] = scale(t1)
        kv_ref[...] = jnp.where(low, swap(t1), swap(out[:, 2 * LANES:])).astype(bf16)

    sh = jax.ShapeDtypeStruct
    return pl.pallas_call(
        kernel,
        grid=(R // step,),
        out_shape=(sh((GROUP, R, LANES), bf16), sh((R, LANES), bf16), sh((R, D), bf16)),
        in_specs=[row_block(step, D), whole_block(gain), whole_block(packed)] + [row_block(step, LANES)] * 3,
        out_specs=(
            pl.BlockSpec((GROUP, step, LANES), lambda i: (0, i, 0)),
            row_block(step, LANES),
            row_block(step, D),
        ),
        compiler_params=pltpu.CompilerParams(vmem_limit_bytes=32 * MIB),
        cost_estimate=cost(4),
        name="project",
    )(x, gain, packed, c, s1, s2)


BQ = 256
BK = 512
NT = (((1,), (1,)), ((), ()))
NN = (((1,), (0,)), ((), ()))
TN = (((0,), (0,)), ((), ()))


def mm(a, b, dims=NN):
    return lax.dot_general(a, b, dims, preferred_element_type=f32)


def seen(meta, st, i, kb, nq):
    qpos = meta[nq] + i * BQ + lax.broadcasted_iota(jnp.int32, (BQ, 1), 0)
    kpos = kb * BK + lax.broadcasted_iota(jnp.int32, (1, BK), 1)
    return ((kpos <= qpos) & (kpos >= st))[None]


def attend(q, kv, starts, meta):
    _, Rq, _ = q.shape
    nq = Rq // BQ
    M = GROUP * BQ

    def kernel(meta, q_ref, kv_ref, st_ref, o_ref, l_ref):
        i = pl.program_id(0)
        qv = q_ref[...].reshape(M, LANES)
        st = st_ref[...]
        last = (meta[nq] + i * BQ + BQ - 1) // BK + 1

        def step(kb, carry):
            m, l, acc = carry
            keys = kv_ref[pl.ds(pl.multiple_of(kb * BK, BK), BK), :]
            s = mm(qv, keys, NT).reshape(GROUP, BQ, BK)
            s = jnp.where(seen(meta, st, i, kb, nq), s, NEG)
            m2 = jnp.maximum(m, jnp.max(s, axis=2, keepdims=True))
            w = jnp.exp(s - m2)
            f = jnp.exp(m - m2)
            l = l * f + jnp.sum(w, axis=2, keepdims=True)
            pv = mm(w.astype(bf16).reshape(M, BK), keys)
            return m2, l, acc * f + pv.reshape(GROUP, BQ, LANES)

        init = (
            jnp.full((GROUP, BQ, 1), NEG, f32),
            jnp.zeros((GROUP, BQ, 1), f32),
            jnp.zeros((GROUP, BQ, LANES), f32),
        )
        m, l, acc = lax.fori_loop(meta[i], last, step, init)
        o = acc / l
        o_ref[:, :LANES] = jnp.where(low_half(), swap(o[0]), o[1]).astype(bf16)
        o_ref[:, LANES:] = swap(o[2])[:, :HW].astype(bf16)
        l_ref[...] = m + jnp.log(l)

    sh = jax.ShapeDtypeStruct
    blk = lambda w: pl.BlockSpec((GROUP, BQ, w), lambda i, m: (0, i, 0))
    return pl.pallas_call(
        kernel,
        grid_spec=pltpu.PrefetchScalarGridSpec(
            num_scalar_prefetch=1,
            grid=(nq,),
            in_specs=[
                blk(LANES),
                pl.BlockSpec(kv.shape, lambda i, m: (0, 0)),
                pl.BlockSpec((BQ, 1), lambda i, m: (i, 0)),
            ],
            out_specs=(pl.BlockSpec((BQ, QCOLS), lambda i, m: (i, 0)), blk(1)),
        ),
        out_shape=(sh((Rq, QCOLS), bf16), sh((GROUP, Rq, 1), f32)),
        compiler_params=pltpu.CompilerParams(vmem_limit_bytes=48 * MIB),
        cost_estimate=cost(17),
        name="attend",
    )(meta, q, kv, starts)


def attend_back(q, kv, starts, meta, lse, mixed, dattn, wo):
    _, Rq, _ = q.shape
    nq = Rq // BQ
    M = GROUP * BQ
    K = kv.shape[0]

    def kernel(meta, q_ref, kv_ref, st_ref, l_ref, o_ref, g_ref, w_ref, dq_ref, dkv_ref, dw_ref):
        i = pl.program_id(0)

        @pl.when(i == 0)
        def _():
            dkv_ref[...] = jnp.zeros_like(dkv_ref)
            dw_ref[...] = jnp.zeros_like(dw_ref)

        g = g_ref[...]
        mixed = o_ref[...]
        dm = mm(g, w_ref[...], NT).astype(bf16).astype(f32)
        dw_ref[...] += mm(mixed, g, TN)
        low = low_half()
        d0 = dm[:, :LANES]
        d1 = jnp.concatenate([dm[:, LANES:], jnp.zeros((BQ, LANES - HW), f32)], axis=1)
        m0 = mixed[:, :LANES].astype(f32)
        m1 = jnp.concatenate([mixed[:, LANES:].astype(f32), jnp.zeros((BQ, LANES - HW), f32)], axis=1)
        total = lambda a: jnp.sum(a, axis=1, keepdims=True)
        e0, e1 = d0 * m0, d1 * m1
        first = total(jnp.where(low, e0, 0.0))
        delta = jnp.stack([first, total(jnp.where(low, 0.0, e0)), total(e1)])
        high = lambda a: jnp.where(low, 0.0, a).astype(bf16)
        do = jnp.concatenate([high(swap(d0)), high(d0), high(swap(d1))], axis=0)
        qv = q_ref[...].reshape(M, LANES)
        lse = l_ref[...]
        st = st_ref[...]
        last = (meta[nq] + i * BQ + BQ - 1) // BK + 1

        def step(kb, dq):
            at = pl.ds(pl.multiple_of(kb * BK, BK), BK)
            keys = kv_ref[at, :]
            s = mm(qv, keys, NT).reshape(GROUP, BQ, BK)
            p = jnp.where(seen(meta, st, i, kb, nq), jnp.exp(s - lse), 0.0)
            dp = mm(do, keys, NT).reshape(GROUP, BQ, BK)
            ds = (p * (dp - delta)).astype(bf16).reshape(M, BK)
            pb = p.astype(bf16).reshape(M, BK)
            dkv_ref[at, :] += mm(ds, qv, TN) + mm(pb, do, TN)
            return dq + mm(ds, keys)

        dq = lax.fori_loop(meta[i], last, step, jnp.zeros((M, LANES), f32))
        dq_ref[...] = (dq * (1.0 / math.sqrt(HW))).astype(bf16).reshape(GROUP, BQ, LANES)

    sh = jax.ShapeDtypeStruct
    blk = lambda w: pl.BlockSpec((GROUP, BQ, w), lambda i, m: (0, i, 0))
    rows = lambda w: pl.BlockSpec((BQ, w), lambda i, m: (i, 0))
    full = lambda *shape: pl.BlockSpec(shape, lambda i, m: (0, 0))
    return pl.pallas_call(
        kernel,
        grid_spec=pltpu.PrefetchScalarGridSpec(
            num_scalar_prefetch=1,
            grid=(nq,),
            in_specs=[
                blk(LANES), full(*kv.shape), rows(1), blk(1), rows(QCOLS), rows(D), full(QCOLS, D),
            ],
            out_specs=(blk(LANES), full(K, LANES), full(QCOLS, D)),
        ),
        out_shape=(sh((GROUP, Rq, LANES), bf16), sh((K, LANES), f32), sh((QCOLS, D), f32)),
        compiler_params=pltpu.CompilerParams(vmem_limit_bytes=48 * MIB),
        cost_estimate=cost(27),
        name="attend_back",
    )(meta, q, kv, starts, lse, mixed, dattn, wo)


def weight_grads(dq, dkv, kin, ok, tables, h1, packed, tail):
    _, Rq, _ = dq.shape
    step = 256
    arrivals = kin.shape[0]

    def kernel(ok_ref, dq_ref, dkv_ref, kin_ref, c_ref, a_ref, b_ref, h_ref, w_ref, t_ref, o_ref, p_ref, acc):
        i = pl.program_id(0)

        @pl.when(i == 0)
        def _():
            acc[...] = jnp.zeros_like(acc)

        kv = dkv_ref[...]
        for k in range(arrivals):
            kv = kv + jnp.where(ok_ref[k] > 0, kin_ref[k].astype(f32), 0.0)
        kv = kv.astype(bf16).astype(f32)
        low = low_half()
        tables = (c_ref[...], a_ref[...], b_ref[...])
        q = [dq_ref[h].astype(f32) for h in range(GROUP)]
        kv = swap(kv)
        t0 = turn_back(jnp.where(low, q[0], swap(q[1])), *tables)
        t1 = turn_back(jnp.where(low, q[2], kv), *tables)
        out = jnp.concatenate([t0, t1, jnp.where(low, kv, 0.0)], axis=1).astype(bf16)
        o_ref[...] = out
        acc[...] += mm(h_ref[...], out, TN)

        @pl.when(i == Rq // step - 1)
        def _():
            w = w_ref[...].astype(f32)
            dw = acc[...]
            t = t_ref[...]
            lane = lax.broadcasted_iota(jnp.int32, (1, LANES), 1)
            gain = jnp.sum(jnp.where(lane == ok_ref[arrivals], w[:, 2 * LANES:], 0.0), axis=1, keepdims=True)
            d_gain = jnp.sum(w * dw, axis=1, keepdims=True) / gain
            t = t + jnp.where(lane == ok_ref[arrivals] + 1, d_gain, 0.0)
            p_ref[:, :2 * LANES] = dw[:, :2 * LANES].astype(bf16)
            p_ref[:, 2 * LANES:] = jnp.where(low, dw[:, 2 * LANES:], t).astype(bf16)

    sh = jax.ShapeDtypeStruct
    heads = lambda n: pl.BlockSpec((n, step, LANES), lambda i: (0, i, 0))
    return pl.pallas_call(
        kernel,
        grid=(Rq // step,),
        out_shape=(sh((Rq, AUX), bf16), sh((D, AUX), bf16)),
        in_specs=[pl.BlockSpec(memory_space=pltpu.SMEM), heads(GROUP), row_block(step, LANES), heads(arrivals)]
        + [row_block(step, LANES)] * 3
        + [row_block(step, D), whole_block(packed), whole_block(tail)],
        out_specs=(row_block(step, AUX), pl.BlockSpec((D, AUX), lambda i: (0, 0))),
        scratch_shapes=[pltpu.VMEM((D, AUX), f32)],
        compiler_params=pltpu.CompilerParams(vmem_limit_bytes=48 * MIB),
        cost_estimate=cost(7),
        name="weight_grads",
    )(ok, dq, dkv, kin, *tables, h1, packed, tail)


def experts(h2, g_own, g_oth, router, hot, inner, outer, nz):
    rows2 = h2.shape[0]
    step = 256
    steps = rows2 // step
    half = steps // 2
    dz = D // nz
    nw = len(outer)
    dw = D // nw
    C = D + LANES

    def kernel(h_ref, g0_ref, g1_ref, r_ref, e_ref, *rest):
        win, wout = rest[:nz], rest[nz:nz + nw]
        y_ref, d_ref = rest[nz + nw:nz + nw + 2]
        outs = rest[nz + nw + 2:]
        din, dout = outs[:nz], outs[nz:nz + nw]
        wi, wo, ai, ao, sem = outs[nz + nw:]
        i = pl.program_id(0)
        z = lax.axis_index("ulysses")

        @pl.when(i == 0)
        def _():
            cps = [
                pltpu.make_async_copy(win[d], wi.at[pl.ds(pl.multiple_of((z ^ d) * dz, dz), dz)], sem.at[d])
                for d in range(nz)
            ] + [
                pltpu.make_async_copy(wout[d], wo.at[z ^ d if nw > 1 else 0], sem.at[nz + d])
                for d in range(nw)
            ]
            for c in cps:
                c.start()
            ai[...] = jnp.zeros_like(ai)
            ao[...] = jnp.zeros_like(ao)
            for c in cps:
                c.wait()

        h = h_ref[...]
        gm = jnp.where(i < half, g0_ref[...], g1_ref[...])
        g = gm[:, :D]
        hot = e_ref[...]
        mask = gm[:, D:].astype(f32) > 0
        logits = mm(h, r_ref[...])
        top = jnp.max(jnp.where(mask, logits, NEG), axis=1, keepdims=True)
        w = jnp.where(mask, jnp.exp(jnp.where(mask, logits - top, 0.0)), 0.0)
        gate = jnp.sum(w * hot, axis=1, keepdims=True) / jnp.sum(w, axis=1, keepdims=True)

        gu = mm(h, wi[...])
        a, up = gu[:, :FF], gu[:, FF:]
        sg = jax.nn.sigmoid(a)
        silu = a * sg
        act = (silu * up).astype(bf16)
        raw = 0.0
        dy = (gate * g.astype(f32)).astype(bf16)
        for k in range(nw):
            cols = slice(k * dw, (k + 1) * dw)
            y_ref[:, cols] = (gate * mm(act, wo[k])).astype(bf16)
            raw = raw + mm(g[:, cols], wo[k], NT)
            ao[k] += mm(act, dy[:, cols], TN)
        dgate = jnp.sum(act.astype(f32) * raw, axis=1, keepdims=True)
        dact = gate * raw
        dgu = jnp.concatenate(
            [dact * up * (sg * (1.0 + a * (1.0 - sg))), dact * silu], axis=1).astype(bf16)
        ai[...] += mm(h, dgu, TN)
        d_ref[:, :D] = mm(dgu, wi[...], NT).astype(bf16)
        hi = dgate.astype(bf16).astype(f32)
        d_ref[:, D:] = (hi * hot + swap((dgate - hi) * hot)).astype(bf16)

        @pl.when(i == steps - 1)
        def _():
            for d in range(nz):
                din[d][...] = ai[pl.ds(pl.multiple_of((z ^ d) * dz, dz), dz), :].astype(bf16)
            for d in range(nw):
                dout[d][...] = ao[z ^ d if nw > 1 else 0].astype(bf16)

    sh = jax.ShapeDtypeStruct
    full = lambda *shape: pl.BlockSpec(shape, lambda i: (0, 0))
    return pl.pallas_call(
        kernel,
        grid=(steps,),
        out_shape=(sh((rows2, D), bf16), sh((rows2, C), bf16))
        + (sh((dz, 2 * FF), bf16),) * nz
        + (sh((FF, dw), bf16),) * nw,
        in_specs=[
            row_block(step, D),
            pl.BlockSpec((step, C), lambda i: (jnp.minimum(i, half - 1), 0)),
            pl.BlockSpec((step, C), lambda i: (jnp.maximum(i - half, 0), 0)),
            whole_block(router),
            whole_block(hot),
        ]
        + [ANY] * (nz + nw),
        out_specs=(row_block(step, D), row_block(step, C)) + (full(dz, 2 * FF),) * nz + (full(FF, dw),) * nw,
        scratch_shapes=[
            pltpu.VMEM((D, 2 * FF), bf16), pltpu.VMEM((nw, FF, dw), bf16),
            pltpu.VMEM((D, 2 * FF), f32), pltpu.VMEM((nw, FF, dw), f32), DMA((nz + nw,)),
        ],
        compiler_params=pltpu.CompilerParams(vmem_limit_bytes=58 * MIB),
        cost_estimate=cost(45),
        name="experts",
    )(h2, g_own, g_oth, router, hot, *inner, *outer)


def finish(dh1, x, gain, dresid, pin, win, resid, ysum):
    T = x.shape[0]
    groups, rp, S, _ = pin.shape
    senders = win.shape[0]

    def kernel(d_ref, x_ref, g_ref, r_ref, p_ref, w_ref, s_ref, y_ref, t_ref, q_ref, k_ref, v_ref, m_ref, o_ref, out_ref):
        v = x_ref[...].astype(f32)
        inv = lax.rsqrt(jnp.mean(v * v, axis=1, keepdims=True) + EPS)
        n = v * inv
        w = d_ref[...] * g_ref[...]
        t_ref[...] = r_ref[...] + inv * (w - n * jnp.mean(w * n, axis=1, keepdims=True))
        out_ref[...] = s_ref[...] + y_ref[...]
        o_ref[...] = functools.reduce(lambda a, b: a + b, [w_ref[k].astype(f32) for k in range(senders)])
        small = 0.0
        for h in range(groups):
            row = 0.0
            for p in range(rp):
                row = row + p_ref[h, p].astype(f32)
            q_ref[:, h * QCOLS:(h + 1) * QCOLS] = row[:, :QCOLS]
            k_ref[:, h * HW:(h + 1) * HW] = row[:, QCOLS:QCOLS + HW]
            v_ref[:, h * HW:(h + 1) * HW] = row[:, QCOLS + HW:ROUTER_AT]
            small = small + row[:, 2 * LANES:]
        m_ref[...] = small

    sh = lambda *shape: jax.ShapeDtypeStruct(shape, f32)
    return pl.pallas_call(
        kernel,
        out_shape=(sh(T, D), sh(S, HEADS * HW), sh(S, KV * HW), sh(S, KV * HW), sh(S, LANES), sh(S, D), sh(T, D)),
        in_specs=[VMEM] * 8,
        out_specs=(VMEM,) * 7,
        compiler_params=pltpu.CompilerParams(vmem_limit_bytes=32 * MIB),
        cost_estimate=cost(2),
        name="finish",
    )(dh1, x, gain, dresid, pin, win, resid, ysum)


def locate(rows, lengths):
    passed = rows[:, None] >= jnp.cumsum(lengths)
    return jnp.sum(jnp.where(passed, lengths, 0), axis=-1)


def norm_rows(v, gain):
    inverse = lax.rsqrt(jnp.mean(v * v, axis=-1, keepdims=True) + EPS)
    normed = v * inverse
    return normed, inverse, normed * gain


def norm_back(upstream, normed, inverse, gain):
    d_normed = upstream * gain
    d_gain = jnp.sum(upstream * normed, axis=0)
    d_values = inverse * (d_normed - normed * jnp.mean(d_normed * normed, axis=-1, keepdims=True))
    return d_values, d_gain


def rows_of(a, start, count):
    return a if a.shape[0] == count else lax.dynamic_slice_in_dim(a, start, count, 0)


def widen(a, start, count):
    if a.shape[0] == count:
        return a
    return lax.dynamic_update_slice_in_dim(jnp.zeros((count,) + a.shape[1:], a.dtype), a, start, 0)


def on_device(tokens, lengths, routes, gain_attn, w_query, w_key, w_value, w_output, gain_moe,
              w_router, w_inner, w_outer, cotangent):
    nz = lax.axis_size("ulysses")
    nb = lax.axis_size("blk")
    z = lax.axis_index("ulysses")
    b = lax.axis_index("blk")
    T = tokens.shape[0]
    R = nb * T
    rp = nb // KV
    Rq = R // rp
    part = b % rp
    at = part * Rq
    n = nz * nb
    S = D // n
    E = w_router.shape[1]
    longest = min(LENMAX, n * T // 2)
    back = min(nz - 1, (longest - 1 + R - 1) // R)
    n_o = QCOLS // S
    odd = z % 2

    tail = jnp.concatenate(
        [w_router, gain_attn[:, None], gain_moe[:, None],
         jnp.zeros((S, AUX - ROUTER_AT - E - 2), bf16)], axis=1)
    pieces = jnp.stack([
        jnp.concatenate([
            w_query[:, h * QCOLS:(h + 1) * QCOLS], w_key[:, h * HW:(h + 1) * HW],
            w_value[:, h * HW:(h + 1) * HW], tail], axis=1)
        for h in range(KV)])
    lanes = jnp.arange(LANES, dtype=jnp.int32)
    named = jnp.any(routes[:, :, None] + HW == lanes[None, None, :], axis=1)
    cot_mask = jnp.concatenate([cotangent, named.astype(bf16)], axis=1)
    take = lambda *items: Swaps([(w, d) for w, d in items if d < nz])
    inner, outer = {}, {}
    xg, g_own, g_far, packed, wo, inner[1], outer[1] = gather_inputs(
        tokens, cot_mask, pieces, w_output, nz, nb, 0, take((w_inner, 1), (w_outer, 1)))
    xg = xg.reshape(R, D)
    g_own = g_own.reshape(R, D + LANES)
    packed = packed.reshape(D, AUX)
    wo = wo.reshape(QCOLS, D)
    router = packed[:, 2 * LANES:]
    gains = packed[:, ROUTER_AT + E:ROUTER_AT + E + 2].astype(f32).T
    gain1, gain2 = gains[0:1], gains[1:2]

    rows = z * R + jnp.arange(R, dtype=jnp.int32)
    opening = locate(rows, lengths)
    pair = lanes % HW
    frequency = THETA ** (-((pair % (HW // 2)).astype(f32) * 2.0 / HW))
    angles = (rows - opening).astype(f32)[:, None] * frequency[None, :]
    cos, sin = jnp.cos(angles), jnp.sin(angles)
    tables = (cos, jnp.where(pair < HW // 2, -sin, 0.0), jnp.where(pair < HW // 2, 0.0, sin))

    q, kv, h1 = project(xg, gain1, packed, *tables)
    if rp > 1:
        q = lax.dynamic_slice_in_dim(q, at, Rq, 1)
    far, g_oth, *got = halo_forward(kv, g_far, nz, nb, back, 1, take((w_outer, 3)))
    outer.update(zip([3], got))
    g_oth = g_oth.reshape(R, D + LANES)
    flip = lambda d: [(k, k ^ d) for k in range(nz)]
    pick = lambda w, d: lax.dynamic_index_in_dim(w, odd ^ (d % 2), 0, keepdims=False)
    late, g_oth = lax.optimization_barrier((w_inner, g_oth))
    later, g_oth = lax.optimization_barrier((w_outer, g_oth))
    for d in range(2, nz):
        if d != 3:
            inner[d] = lax.ppermute(pick(late, d), "ulysses", flip(d))
        if d > 3:
            outer[d] = lax.ppermute(pick(later, d), "ulysses", flip(d))

    kv_all = jnp.concatenate([far[d - 1] for d in range(back, 0, -1)] + [kv], axis=0)
    base = (z - back) * R
    starts = rows_of(opening, at, Rq) - base
    meta = jnp.concatenate([starts[::BQ] // BK, (back * R + at)[None]]).astype(jnp.int32)
    starts = starts[:, None]
    mixed, lse = attend(q, kv_all, starts, meta)
    attn, *got = reduce_product(widen(mixed, at, R), wo, nb, 2, take((w_outer, 2)))
    outer.update(zip([2], got))

    resid = tokens.astype(f32) + attn
    n2, inv2, scaled2 = norm_rows(resid, gain2)
    h2_own = scaled2.astype(bf16)
    h2_own, inner[2] = lax.optimization_barrier((h2_own, inner[2]))
    h2, *got = gather_pair(h2_own, nb, 3, take((w_inner, 3)))
    inner.update(zip([3], got))
    h2 = h2.reshape(2 * R, D)
    inner[0], outer[0] = pick(w_inner, 0), pick(w_outer, 0)
    inner, outer = ([w[d] for d in range(nz)] for w in (inner, outer))
    aligned = (D // nz) % LANES == 0
    if not aligned:
        outer = lax.optimization_barrier(outer)
        by_owner = jnp.take(jnp.stack(outer), z ^ jnp.arange(nz), axis=0)
        outer = [jnp.transpose(by_owner, (1, 0, 2)).reshape(FF, D)]
    hot = (lanes == HW + b * EXP_DEV + odd).astype(f32)[None, :]
    y, back_rows, *grads = experts(h2, g_own, g_oth, router, hot, inner, outer, nz)
    d_inner, d_outer = grads[:nz], grads[nz:]
    if not aligned:
        by_owner = jnp.transpose(d_outer[0].reshape(FF, nz, D // nz), (1, 0, 2))
        by_owner = jnp.take(by_owner, z ^ jnp.arange(nz), axis=0)
        d_outer = [by_owner[d] for d in range(nz)]
    summed, d_inner[1], d_inner[2], d_outer[1], d_outer[2] = reduce_pair(
        back_rows.reshape(2, nb, T, D + LANES), nb, 4,
        take((d_inner[1], 1), (d_inner[2], 2), (d_outer[1], 1), (d_outer[2], 2)))

    upstream = cotangent.astype(f32)
    dgates = summed[:, D:] + jnp.roll(summed[:, D:], HW, 1)
    logits = mm(h2_own, router)
    top = jnp.max(jnp.where(named, logits, NEG), axis=1, keepdims=True)
    w = jnp.where(named, jnp.exp(jnp.where(named, logits - top, 0.0)), 0.0)
    gates = w / jnp.sum(w, axis=1, keepdims=True)
    dlogits = gates * (dgates - jnp.sum(gates * dgates, axis=1, keepdims=True))
    dlogits = dlogits.astype(bf16)
    dh2 = summed[:, :D] + mm(dlogits, router, NT)
    d_norm2, d_gain2 = norm_back(dh2, n2, inv2, gain2)
    dresid = upstream + d_norm2
    dattn, d_outer[3] = gather_layer(dresid.astype(bf16), nb, 5, take((d_outer[3], 3)))
    dattn, *rest = lax.optimization_barrier((dattn, *d_inner[3:], *d_outer[4:]))
    rest = [lax.ppermute(r, "ulysses", flip(d)) for r, d in zip(rest, [*range(3, nz), *range(4, nz)])]
    d_inner[3:], d_outer[4:] = rest[:nz - 3], rest[nz - 3:]
    dattn = dattn.reshape(R, D)
    tail = mm(h2_own, dlogits, TN) + jnp.where(lanes == HW + E, d_gain2[:, None], 0.0)

    dq, dkv, dwo = attend_back(q, kv_all, starts, meta, lse, mixed, rows_of(dattn, at, Rq), wo)
    dkv, d_inner, d_outer = lax.optimization_barrier((dkv, d_inner, d_outer))
    dkv = dkv.reshape(back + 1, R, LANES)
    dkv_out = jnp.stack([dkv[back - d] for d in range(back + 1)]).astype(bf16)
    y = y.reshape(2, nb, T, D)
    kin, ysum, win = halo_back(dkv_out, y, dwo.astype(bf16).reshape(n_o, S, D), nz, nb, rp, back, 6)
    ok = [(z + d < nz) if d else (part != p) for d in range(back + 1) for p in range(rp)]
    ok = jnp.stack([jnp.asarray(o).astype(jnp.int32) for o in ok] + [jnp.int32(HW + E)])
    if rp > 1:
        kin = lax.dynamic_slice_in_dim(kin, at, Rq, 1)
    turned, dw = weight_grads(
        dq, rows_of(dkv[back], at, Rq), kin, ok, [rows_of(t, at, Rq) for t in tables],
        rows_of(h1, at, Rq), packed, tail)
    dh1, pin = reduce_last(widen(turned, at, R), packed, dw.reshape(nz, nb, S, AUX), nz, nb, 7)
    d_tokens, d_query, d_key, d_value, small, d_output, out = finish(
        dh1, tokens, gain1, dresid, pin.reshape(KV, rp, S, AUX), win, resid, ysum)

    def settle(parts):
        same = sum(p.astype(f32) for p in parts[0::2])
        other = sum(p.astype(f32) for p in parts[1::2])
        return jnp.where(odd == 0, jnp.stack([same, other]), jnp.stack([other, same]))

    return (
        out, d_tokens, small[:, HW + E + 1], d_query, d_key, d_value, d_output,
        small[:, HW + E], small[:, HW:HW + E], settle(d_inner), settle(d_outer),
    )


def solution(mesh):
    both = ("ulysses", "blk")
    rows = P(both, None)
    weights = (P(both), rows, rows, rows, rows, P(both), rows, P("blk", "ulysses", None), P("blk", None, "ulysses"))
    return jax.shard_map(
        on_device,
        mesh=mesh,
        in_specs=(rows, P(), rows) + weights + (rows,),
        out_specs=(rows, rows) + weights,
        check_vma=False,
    )
```

```python
import functools
import math

import jax
import jax.numpy as jnp
from jax import lax
from jax.experimental import pallas as pl
from jax.experimental.pallas import tpu as pltpu
from jax.sharding import PartitionSpec as P

D = 1536
HEADS = 24
KV = 8
HW = 64
GROUP = HEADS // KV
FF = 512
TOPK = 8
EXP_DEV = 2
LENMAX = 4096
EPS = 1e-05
THETA = 10000.0
NEG = -1e30
LANES = 128
AUX = 384
ROUTER_AT = 320
QCOLS = GROUP * HW

f32 = jnp.float32
bf16 = jnp.bfloat16
MESH = pl.DeviceIdType.MESH
ANY = pl.BlockSpec(memory_space=pl.ANY)
VMEM = pl.BlockSpec(memory_space=pltpu.VMEM)
DMA = pltpu.SemaphoreType.DMA
MIB = 1 << 20


def dev(u, b):
    return {"ulysses": u, "blk": b}


def remote(src, dst, ss, rs, u, b):
    return pltpu.make_async_remote_copy(
        src_ref=src, dst_ref=dst, send_sem=ss, recv_sem=rs,
        device_id=dev(u, b), device_id_type=MESH,
    )


def cost(us):
    return pl.CostEstimate(flops=us * 1_000_000_000, bytes_accessed=0, transcendentals=0)


def signal(sem, u, b):
    pl.semaphore_signal(sem, inc=1, device_id=dev(u, b), device_id_type=MESH)


class Layer:
    def __init__(self, nb):
        self.u = lax.axis_index("ulysses")
        self.b = lax.axis_index("blk")
        self.nb = nb
        self.nc = nb // 2
        self.chip = self.b // 2
        self.core = lax.rem(self.b, 2)
        self.sib = self.chip * 2 + 1 - self.core

    def peer(self, i):
        return lax.rem(self.chip + i, self.nc) * 2 + self.core

    def unit(self, j):
        if self.nc != 4:
            return lax.rem(self.chip + self.nc - j, self.nc)
        x, y = lax.rem(self.chip, 2), self.chip // 2
        jx, jy = j % 2, j // 2
        return x + jx - 2 * x * jx + 2 * (y + jy - 2 * y * jy)

    def far(self, j):
        return self.unit(j) * 2 + self.core

    def across(self, d):
        at = self.u
        for k in range(d.bit_length()):
            if (d >> k) & 1:
                at = at + (1 << k) - (2 << k) * lax.rem(self.u // (1 << k), 2)
        return at

    def enter(self, flips=()):
        bar = pltpu.get_barrier_semaphore()
        for i in range(1, self.nc):
            signal(bar, self.u, self.peer(i))
        signal(bar, self.u, self.sib)
        for d in flips:
            signal(bar, self.across(d), self.b)
        pl.semaphore_wait(bar, self.nc + len(flips))


class Gather:
    def __init__(self, me, src, dst, sems):
        self.me, self.src, self.dst, self.sems = me, src, dst, sems
        self.quad = me.nc == 4
        half = dst.shape[1] // 2
        self.a, self.b = pl.ds(0, half), pl.ds(half, half)

    @staticmethod
    def scratch(nb, *lead):
        return DMA(lead + (2, 10 if nb == 8 else nb))

    def copy(self, k):
        me, src, dst = self.me, self.src, self.dst
        send = lambda s, d, to: remote(s, d, self.sems.at[0, k], self.sems.at[1, k], me.u, to)
        same = lambda at, to: send(dst.at[at], dst.at[at], to)
        part = lambda at, rows, to: send(dst.at[at, rows], dst.at[at, rows], to)
        if self.quad:
            if k < 4:
                rows = self.b if k % 2 else self.a
                return send(src.at[rows], dst.at[me.b, rows], me.far(1 + k // 2))
            if k < 6:
                return part(me.far(k - 3), self.b if k == 5 else self.a, me.far(6 - k))
            if k == 6:
                return send(src, dst.at[me.b], me.sib)
            return same(me.far(k - 6), me.sib)
        if k < me.nc:
            return send(src, dst.at[me.b], me.peer(k))
        if k == me.nc:
            return send(src, dst.at[me.b], me.sib)
        return same(me.far(k - me.nc), me.sib)

    def start(self):
        if self.quad:
            for k in (0, 3, 1, 2, 6):
                self.copy(k).start()
        else:
            for k in range(1, self.me.nc + 1):
                self.copy(k).start()

    def relay1(self):
        if self.quad:
            self.copy(0).wait_recv()
            self.copy(4).start()
            self.copy(3).wait_recv()
            self.copy(5).start()

    def relay2(self):
        if self.quad:
            self.copy(1).wait_recv()
            self.copy(7).start()
            self.copy(2).wait_recv()
            self.copy(8).start()
        else:
            for k in range(1, self.me.nc):
                self.copy(k).wait_recv()
                self.copy(self.me.nc + k).start()

    def relay3(self):
        if self.quad:
            self.copy(4).wait_recv()
            self.copy(5).wait_recv()
            self.copy(9).start()

    def passed(self, j):
        self.copy((6 if self.quad else self.me.nc) + j).wait_recv()

    def sent(self):
        for k in range(10) if self.quad else range(1, 2 * self.me.nc):
            self.copy(k).wait_send()

    def rest(self):
        self.relay1()
        self.relay2()
        self.relay3()

    def finish(self):
        for j in range(self.me.nc):
            self.passed(j)
        self.sent()


class Reduce:
    def __init__(self, me, get, source, sib_in, snd, land, sems):
        self.me, self.get, self.source = me, get, source
        self.sib_in, self.snd, self.land, self.sems = sib_in, snd, land, sems
        self.quad = me.nc == 4
        self.rows = sib_in.shape[1]
        half = self.rows // 2
        self.a, self.b = pl.ds(0, half), pl.ds(half, half)
        self.order = (3, 1, 2, 0) if self.quad else (*range(1, me.nc), 0)

    @staticmethod
    def scratch(nb, rows, cols, *lead):
        nc = nb // 2
        shape = lead + ((6, rows // 2, cols) if nc == 4 else (nc, rows, cols))
        return [
            pltpu.VMEM(lead + (nc, rows, cols), bf16), pltpu.VMEM(shape, bf16), pltpu.VMEM(shape, bf16),
            DMA(lead + (2, 10 if nc == 4 else 2 * nc)),
        ]

    def copy(self, k):
        me = self.me
        ss, rs = self.sems.at[0, k], self.sems.at[1, k]
        if k < me.nc:
            return remote(self.source(k), self.sib_in.at[k], ss, rs, me.u, me.sib)
        k = k - me.nc
        to = me.far((1, 1, 2, 2, 2, 1)[k] if self.quad else k)
        return remote(self.snd.at[k], self.land.at[k], ss, rs, me.u, to)

    def start(self, j):
        self.copy(j).start()

    def part(self, j, rows):
        return self.get(j, rows) + self.sib_in[j, rows].astype(f32)

    def send(self, k, value):
        self.snd[k] = value.astype(bf16)
        self.copy(self.me.nc + k).start()

    def phase1(self, j):
        self.copy(j).wait_recv()
        if not self.quad:
            self.send(j, self.part(j, pl.ds(0, self.rows)))
            return
        if j != 2:
            self.send(0 if j == 1 else 1, self.part(j, self.a))
        if j != 1:
            self.send(2 if j == 2 else 3, self.part(j, self.b))

    def landed(self, k):
        self.copy(self.me.nc + k).wait_recv()
        return self.land[k].astype(f32)

    def phase2(self):
        if self.quad:
            self.send(4, self.part(2, self.a) + self.landed(1))
            self.send(5, self.part(1, self.b) + self.landed(3))

    def end(self, write):
        self.copy(0).wait_recv()
        if self.quad:
            write(self.a, self.part(0, self.a) + self.landed(0) + self.landed(4))
            write(self.b, self.part(0, self.b) + self.landed(2) + self.landed(5))
        else:
            total = self.part(0, pl.ds(0, self.rows))
            for j in range(1, self.me.nc):
                total = total + self.landed(j)
            write(pl.ds(0, self.rows), total)

    def sent(self):
        for k in range(10) if self.quad else (*range(self.me.nc + 1), *range(self.me.nc + 1, 2 * self.me.nc)):
            if self.quad or k != self.me.nc:
                self.copy(k).wait_send()


def made(me, block, mine, sib_out, sib_in, snd, land, sems):
    red = Reduce(me, lambda j, rows: mine[j, rows], lambda j: sib_out.at[j], sib_in, snd, land, sems)
    for j in red.order:
        sib_out[j] = block(me.unit(j) * 2 + 1 - me.core).astype(bf16)
        red.start(j)
    for j in red.order:
        mine[j] = block(me.far(j))
        if j:
            red.phase1(j)
    return red


def made_scratch(nb, rows, cols):
    nc = nb // 2
    return [pltpu.VMEM((nc, rows, cols), f32), pltpu.VMEM((nc, rows, cols), bf16)] + Reduce.scratch(nb, rows, cols)


def keep(me, src, dst, sem):
    c = pltpu.make_async_copy(src, dst.at[me.b], sem)
    c.start()
    return c


def gather_inputs(x, pieces, nz, nb, cid):
    groups, shard, _ = pieces.shape
    rp = nb // groups

    def kernel(x_ref, p_ref, xo, po, gs, ps, pr, zs, ls):
        me = Layer(nb)
        bar = pltpu.get_barrier_semaphore()
        for i in range(1, nb):
            signal(bar, me.u, lax.rem(me.b + i, nb))
        for i in range(1, nz):
            signal(bar, lax.rem(me.u + i, nz), me.b)
        pl.semaphore_wait(bar, nb + nz - 2)

        def piece(i):
            tb = lax.rem(me.b + i, nb)
            return remote(p_ref.at[tb // rp], po.at[me.u, me.b], ps.at[i], pr.at[i], me.u, tb)

        for i in range(1, nb):
            piece(i).start()
        own = pltpu.make_async_copy(p_ref.at[me.b // rp], po.at[me.u, me.b], ls.at[0])
        own.start()
        g = Gather(me, x_ref, xo, gs)
        g.start()
        for i in range(1, nb):
            piece(i).wait()
        own.wait()
        slabs = []
        for zo in range(1, nz):
            c = remote(po.at[me.u], po.at[me.u], zs.at[0, zo], zs.at[1, zo], lax.rem(me.u + zo, nz), me.b)
            c.start()
            slabs.append(c)
        xk = keep(me, x_ref, xo, ls.at[1])
        g.rest()
        g.finish()
        for c in slabs:
            c.wait()
        xk.wait()

    sh = jax.ShapeDtypeStruct
    return pl.pallas_call(
        kernel,
        out_shape=(sh((nb,) + x.shape, x.dtype), sh((nz, nb, shard, AUX), bf16)),
        in_specs=[ANY] * 2,
        out_specs=(ANY,) * 2,
        scratch_shapes=[Gather.scratch(nb)] + [DMA((nb,))] * 2 + [DMA((2, nz)), DMA((2,))],
        compiler_params=pltpu.CompilerParams(collective_id=cid, has_side_effects=True),
        cost_estimate=cost(30),
        name="gather_inputs",
    )(x, pieces)


def halo_forward(kv, gm, wo, nz, nb, rp, back, cid):
    shard = wo.shape[0]
    n_o = QCOLS // shard
    n = nz * nb

    def kernel(x_ref, g_ref, w_ref, o_ref, go, gx, wo_out, ks, kr, gs, ws, wr, ls):
        me = Layer(nb)
        lin = me.u * nb + me.b
        u, b = me.u, me.b
        bar = pltpu.get_barrier_semaphore()

        @pl.loop(1, n)
        def _(i):
            t = lax.rem(lin + i, n)
            signal(bar, t // nb, lax.rem(t, nb))

        pl.semaphore_wait(bar, n - 1)

        def copy(d):
            return remote(x_ref, o_ref.at[d - 1], ks.at[d - 1], kr.at[d - 1], u + d, b)

        for d in range(1, back + 1):
            pl.when(u + d < nz)(lambda d=d: copy(d).start())
        hg = lin // n_o
        slot = lax.rem(lin, n_o)

        def weight(zo, p):
            tz, tb = lax.rem(me.u + zo, nz), hg * rp + p
            return tb, remote(w_ref, wo_out.at[slot], ws.at[zo * rp + p], wr.at[slot], tz, tb)

        stay = pltpu.make_async_copy(w_ref, wo_out.at[slot], ls.at[1])
        for zo in range(nz):
            for p in range(rp):
                tb, c = weight(zo, p)
                if zo:
                    c.start()
                else:
                    pl.when(tb != b)(c.start)
                    pl.when(tb == b)(stay.start)
        mate = remote(g_ref, gx, ls.at[2], ls.at[3], me.across(1), b)
        mate.start()
        g = Gather(me, g_ref, go, gs)
        g.start()
        own = keep(me, g_ref, go, ls.at[0])
        g.rest()
        g.finish()
        own.wait()
        for d in range(1, back + 1):
            pl.when(u + d < nz)(lambda d=d: copy(d).wait_send())
            pl.when(u >= d)(lambda d=d: copy(d).wait_recv())
        for zo in range(nz):
            for p in range(rp):
                tb, c = weight(zo, p)
                if zo:
                    c.wait_send()
                else:
                    pl.when(tb != b)(c.wait_send)
                    pl.when(tb == b)(stay.wait)
        for j in range(n_o):
            src = (b // rp) * n_o + j
            c = remote(w_ref, wo_out.at[j], ws.at[0], wr.at[j], u, me.sib)
            pl.when(src != lin)(c.wait_recv)
        mate.wait()

    sh = jax.ShapeDtypeStruct
    return pl.pallas_call(
        kernel,
        out_shape=(
            sh((back,) + kv.shape, kv.dtype), sh((nb,) + gm.shape, gm.dtype), sh(gm.shape, gm.dtype),
            sh((n_o, shard, D), bf16),
        ),
        in_specs=[ANY] * 3,
        out_specs=(ANY,) * 4,
        scratch_shapes=[DMA((back,))] * 2 + [Gather.scratch(nb), DMA((nz * rp,)), DMA((n_o,)), DMA((4,))],
        compiler_params=pltpu.CompilerParams(collective_id=cid, has_side_effects=True),
        cost_estimate=cost(30),
        name="halo_forward",
    )(kv, gm, wo)


def pair_of(me, p_ref, sib_in, snd, land, sems):
    def one(h):
        return Reduce(
            me, lambda j, rows: p_ref[h, me.far(j), rows].astype(f32),
            lambda j: p_ref.at[h, me.unit(j) * 2 + 1 - me.core],
            sib_in.at[h], snd.at[h], land.at[h], sems.at[h])
    return one(0), one(1)


def write_to(ref, *lead):
    def write(rows, value):
        ref[(*lead, rows)] = value.astype(ref.dtype)
    return write


def add_to(ref, other, at):
    def write(rows, value):
        ref[rows] = value + other[at, rows].astype(f32)
    return write


def reduce_product(lhs, rhs, gx, nb, cid):
    rows = lhs.shape[0] // nb
    cols = rhs.shape[1]

    def kernel(l_ref, r_ref, g_ref, o_ref, go, gs, ls, *scratch):
        me = Layer(nb)
        me.enter()

        def block(t):
            part = l_ref[pl.ds(pl.multiple_of(t * rows, rows), rows), :]
            return jnp.dot(part, r_ref[...], preferred_element_type=f32)

        red = made(me, block, *scratch)
        g = Gather(me, g_ref, go, gs)
        g.start()
        own = keep(me, g_ref, go, ls)
        red.phase2()
        g.rest()
        red.end(write_to(o_ref))
        red.sent()
        g.finish()
        own.wait()

    sh = jax.ShapeDtypeStruct
    return pl.pallas_call(
        kernel,
        out_shape=(sh((rows, cols), f32), sh((nb,) + gx.shape, gx.dtype)),
        in_specs=[VMEM, VMEM, ANY],
        out_specs=(VMEM, ANY),
        scratch_shapes=[Gather.scratch(nb), DMA] + made_scratch(nb, rows, cols),
        compiler_params=pltpu.CompilerParams(
            collective_id=cid, has_side_effects=True, vmem_limit_bytes=48 * MIB
        ),
        cost_estimate=cost(30),
        name="reduce_product",
    )(lhs, rhs, gx)


def middle(x, ypart, grads, nz, nb, cid):
    _, _, rows, cols = ypart.shape
    m = len(grads)

    def kernel(x_ref, y_ref, *rest):
        srcs, xo, o_ref, dsts = rest[:m], rest[m], rest[m + 1], rest[m + 2:2 * m + 2]
        gs, ls, ws, zs, zbuf, *pair = rest[2 * m + 2:]
        me = Layer(nb)
        me.enter(range(1, m + 1))
        g = Gather(me, x_ref, xo, gs)
        g.start()
        r0, r1 = pair_of(me, y_ref, *pair)
        for r in (r1, r0):
            for j in r.order:
                r.start(j)
        moved = [
            remote(srcs[k], dsts[k], ws.at[0, k], ws.at[1, k], me.across(k + 1), me.b) for k in range(m)
        ]
        for c in reversed(moved):
            c.start()
        own = keep(me, x_ref, xo, ls)
        g.rest()
        for r in (r1, r0):
            for j in r.order[:-1]:
                r.phase1(j)
        r1.phase2()
        r0.phase2()
        r1.end(write_to(zbuf, 0))
        mate = remote(zbuf.at[0], zbuf.at[1], zs.at[0], zs.at[1], me.across(1), me.b)
        mate.start()
        mate.wait_recv()
        r0.end(add_to(o_ref, zbuf, 1))
        mate.wait_send()
        r0.sent()
        r1.sent()
        g.finish()
        own.wait()
        for c in moved:
            c.wait()

    sh = jax.ShapeDtypeStruct
    return pl.pallas_call(
        kernel,
        out_shape=(sh((nb,) + x.shape, x.dtype), sh((rows, cols), f32))
        + tuple(sh(a.shape, a.dtype) for a in grads),
        in_specs=[ANY, VMEM] + [ANY] * m,
        out_specs=(ANY, VMEM) + (ANY,) * m,
        scratch_shapes=[Gather.scratch(nb), DMA, DMA((2, m)), DMA((2,)), pltpu.VMEM((2, rows, cols), bf16)]
        + Reduce.scratch(nb, rows, cols, 2),
        compiler_params=pltpu.CompilerParams(
            collective_id=cid, has_side_effects=True, vmem_limit_bytes=56 * MIB
        ),
        cost_estimate=cost(50),
        name="middle",
    )(x, ypart, *grads)


def halo_back(dkv, nz, nb, rp, back, cid):
    R = dkv.shape[1]

    def kernel(d_ref, kin, ks, kr):
        me = Layer(nb)
        first = (me.b // rp) * rp
        part = lax.rem(me.b, rp)
        bar = pltpu.get_barrier_semaphore()
        others = [(zo, p) for zo in range(nz) for p in range(rp) if zo or p]
        for zo, p in others:
            signal(bar, lax.rem(me.u + zo, nz), first + lax.rem(part + p, rp))
        pl.semaphore_wait(bar, len(others))

        def copy(d, p):
            k = d * rp + p
            return remote(d_ref.at[d], kin.at[d * rp + part], ks.at[k], kr.at[d * rp + part], me.u - d, first + p)

        def arrival(d, p):
            k = d * rp + p
            return remote(d_ref.at[d], kin.at[k], ks.at[k], kr.at[k], me.u, me.sib)

        for d in range(back + 1):
            for p in range(rp):
                if d:
                    pl.when(me.u >= d)(lambda d=d, p=p: copy(d, p).start())
                elif rp > 1:
                    pl.when(part != p)(lambda d=d, p=p: copy(d, p).start())
        for d in range(back + 1):
            for p in range(rp):
                if d:
                    pl.when(me.u >= d)(lambda d=d, p=p: copy(d, p).wait_send())
                    pl.when(me.u + d < nz)(lambda d=d, p=p: arrival(d, p).wait_recv())
                elif rp > 1:
                    pl.when(part != p)(lambda d=d, p=p: copy(d, p).wait_send())
                    pl.when(part != p)(lambda d=d, p=p: arrival(d, p).wait_recv())

    return pl.pallas_call(
        kernel,
        out_shape=jax.ShapeDtypeStruct(((back + 1) * rp, R, LANES), bf16),
        in_specs=[ANY],
        out_specs=ANY,
        scratch_shapes=[DMA(((back + 1) * rp,))] * 2,
        compiler_params=pltpu.CompilerParams(collective_id=cid, has_side_effects=True),
        cost_estimate=cost(25),
        name="halo_back",
    )(dkv)


def reduce_last(lhs, rhs, pieces, dwo, nz, nb, rp, cid):
    rows = lhs.shape[0] // nb
    cols = rhs.shape[0]
    _, _, shard, width = pieces.shape
    n_o = nz * rp
    n = nz * nb

    def kernel(l_ref, r_ref, p_ref, w_ref, o_ref, pin, win, slab, total, wslab, wtotal, zs, zr, ps, pr, ws, wr,
               ls, *scratch):
        me = Layer(nb)
        lin = me.u * nb + me.b
        part = lax.rem(me.b, rp)
        bar = pltpu.get_barrier_semaphore()

        @pl.loop(1, n)
        def _(i):
            t = lax.rem(lin + i, n)
            signal(bar, t // nb, lax.rem(t, nb))

        pl.semaphore_wait(bar, n - 1)

        def weight(p):
            t = (me.b // rp) * n_o + me.u * rp + p
            return t, remote(wtotal.at[p], win.at[part], ws.at[0, p], wr.at[0, part], t // nb, lax.rem(t, nb))

        across = []
        for i in range(1, nz):
            to = lax.rem(me.u + i, nz)
            c = remote(p_ref.at[to], slab.at[i], zs.at[i], zr.at[i], to, me.b)
            c.start()
            across.append(c)

        def block(t):
            part = l_ref[pl.ds(pl.multiple_of(t * rows, rows), rows), :]
            return lax.dot_general(part, r_ref[...], NT, preferred_element_type=f32)

        parts = []
        for i in range(1, nz):
            to = lax.rem(me.u + i, nz)
            c = remote(w_ref.at[to], wslab.at[i], ws.at[1, i], wr.at[1, i], to, me.b)
            c.start()
            parts.append(c)
        red = made(me, block, *scratch)
        red.phase2()
        for c in across:
            c.wait_recv()
        out = []
        for t in range(nb):
            tile = p_ref[me.u, t].astype(f32)
            for i in range(1, nz):
                tile = tile + slab[i, t].astype(f32)
            total[t] = tile.astype(bf16)
        for i in range(1, nb):
            t = lax.rem(me.b + i, nb)
            c = remote(total.at[t], pin.at[me.b], ps.at[i], pr.at[i], me.u, t)
            c.start()
            out.append(c)
        own = pltpu.make_async_copy(total.at[me.b], pin.at[me.b], ls.at[0])
        own.start()
        for c in parts:
            c.wait_recv()
        stay = lambda p: pltpu.make_async_copy(wtotal.at[p], win.at[part], ls.at[1])
        for p in range(rp):
            tile = w_ref[me.u, p].astype(f32)
            for i in range(1, nz):
                tile = tile + wslab[i, p].astype(f32)
            wtotal[p] = tile.astype(bf16)
            t, c = weight(p)
            pl.when(t != lin)(c.start)
            pl.when(t == lin)(stay(p).start)
        red.end(write_to(o_ref))
        red.sent()
        for c in across:
            c.wait_send()
        for c in out:
            c.wait()
        own.wait()
        for c in parts:
            c.wait_send()
        for p in range(rp):
            t, c = weight(p)
            pl.when(t != lin)(c.wait_send)
            pl.when(t == lin)(stay(p).wait)
        hg = lin // n_o
        layer = lax.rem(lin, n_o) // rp
        for p in range(rp):
            c = remote(wtotal.at[0], win.at[p], ws.at[0, 0], wr.at[0, p], me.u, me.sib)
            pl.when(layer * nb + hg * rp + p != lin)(c.wait_recv)

    sh = jax.ShapeDtypeStruct
    return pl.pallas_call(
        kernel,
        out_shape=(
            sh((rows, cols), f32), sh((nb, shard, width), bf16), sh((rp, shard, D), bf16),
        ),
        in_specs=[VMEM, VMEM, VMEM, VMEM],
        out_specs=(VMEM, ANY, ANY),
        scratch_shapes=[pltpu.VMEM((nz, nb, shard, width), bf16), pltpu.VMEM((nb, shard, width), bf16)]
        + [pltpu.VMEM((nz, rp, shard, D), bf16), pltpu.VMEM((rp, shard, D), bf16)]
        + [DMA((nz,))] * 2
        + [DMA((nb,))] * 2
        + [DMA((2, max(nz, rp)))] * 2
        + [DMA((2,))]
        + made_scratch(nb, rows, cols),
        compiler_params=pltpu.CompilerParams(
            collective_id=cid, has_side_effects=True, vmem_limit_bytes=56 * MIB
        ),
        cost_estimate=cost(2),
        name="reduce_last",
    )(lhs, rhs, pieces, dwo)


def turn(a, c, s1, s2):
    return a * c + pltpu.roll(a, LANES - HW // 2, 1) * s1 + pltpu.roll(a, HW // 2, 1) * s2


def turn_back(a, c, s1, s2):
    return a * c - pltpu.roll(a, LANES - HW // 2, 1) * s1 - pltpu.roll(a, HW // 2, 1) * s2


def swap(a):
    return pltpu.roll(a, HW, 1)


def low_half():
    return lax.broadcasted_iota(jnp.int32, (1, LANES), 1) < HW


def row_block(step, width):
    return pl.BlockSpec((step, width), lambda i: (i, 0))


def whole_block(a):
    zeros = (0,) * a.ndim
    return pl.BlockSpec(a.shape, lambda i: zeros)


def project(x, gain, packed, c, s1, s2):
    R = x.shape[0]
    step = 256

    def kernel(x_ref, g_ref, w_ref, c_ref, a_ref, b_ref, q_ref, kv_ref, h_ref):
        v = x_ref[...].astype(f32)
        inv = lax.rsqrt(jnp.mean(v * v, axis=1, keepdims=True) + EPS)
        h = (v * inv * g_ref[...]).astype(bf16)
        h_ref[...] = h
        out = jnp.dot(h, w_ref[...], preferred_element_type=f32)
        tables = (c_ref[...], a_ref[...], b_ref[...])
        low = low_half()
        t0 = turn(out[:, :LANES], *tables)
        t1 = turn(out[:, LANES:2 * LANES], *tables)
        scale = lambda a: (jnp.where(low, a, 0.0) * (1.0 / math.sqrt(HW))).astype(bf16)
        q_ref[0] = scale(t0)
        q_ref[1] = scale(swap(t0))
        q_ref[2] = scale(t1)
        kv_ref[...] = jnp.where(low, swap(t1), swap(out[:, 2 * LANES:])).astype(bf16)

    sh = jax.ShapeDtypeStruct
    return pl.pallas_call(
        kernel,
        grid=(R // step,),
        out_shape=(sh((GROUP, R, LANES), bf16), sh((R, LANES), bf16), sh((R, D), bf16)),
        in_specs=[row_block(step, D), whole_block(gain), whole_block(packed)] + [row_block(step, LANES)] * 3,
        out_specs=(
            pl.BlockSpec((GROUP, step, LANES), lambda i: (0, i, 0)),
            row_block(step, LANES),
            row_block(step, D),
        ),
        compiler_params=pltpu.CompilerParams(vmem_limit_bytes=32 * MIB),
        cost_estimate=cost(4),
        name="project",
    )(x, gain, packed, c, s1, s2)


BQ = 256
BK = 512
NT = (((1,), (1,)), ((), ()))
NN = (((1,), (0,)), ((), ()))
TN = (((0,), (0,)), ((), ()))


def mm(a, b, dims=NN):
    return lax.dot_general(a, b, dims, preferred_element_type=f32)


def seen(meta, st, i, kb, nq):
    qpos = meta[nq] + i * BQ + lax.broadcasted_iota(jnp.int32, (BQ, 1), 0)
    kpos = kb * BK + lax.broadcasted_iota(jnp.int32, (1, BK), 1)
    return ((kpos <= qpos) & (kpos >= st))[None]


def attend(q, kv, starts, meta):
    _, Rq, _ = q.shape
    nq = Rq // BQ
    M = GROUP * BQ

    def kernel(meta, q_ref, kv_ref, st_ref, o_ref, l_ref):
        i = pl.program_id(0)
        qv = q_ref[...].reshape(M, LANES)
        st = st_ref[...]
        last = (meta[nq] + i * BQ + BQ - 1) // BK + 1

        def step(kb, carry):
            m, l, acc = carry
            keys = kv_ref[pl.ds(pl.multiple_of(kb * BK, BK), BK), :]
            s = mm(qv, keys, NT).reshape(GROUP, BQ, BK)
            s = jnp.where(seen(meta, st, i, kb, nq), s, NEG)
            m2 = jnp.maximum(m, jnp.max(s, axis=2, keepdims=True))
            w = jnp.exp(s - m2)
            f = jnp.exp(m - m2)
            l = l * f + jnp.sum(w, axis=2, keepdims=True)
            pv = mm(w.astype(bf16).reshape(M, BK), keys)
            return m2, l, acc * f + pv.reshape(GROUP, BQ, LANES)

        init = (
            jnp.full((GROUP, BQ, 1), NEG, f32),
            jnp.zeros((GROUP, BQ, 1), f32),
            jnp.zeros((GROUP, BQ, LANES), f32),
        )
        m, l, acc = lax.fori_loop(meta[i], last, step, init)
        o = acc / l
        o_ref[:, :LANES] = jnp.where(low_half(), swap(o[0]), o[1]).astype(bf16)
        o_ref[:, LANES:] = swap(o[2])[:, :HW].astype(bf16)
        l_ref[...] = m + jnp.log(l)

    sh = jax.ShapeDtypeStruct
    blk = lambda w: pl.BlockSpec((GROUP, BQ, w), lambda i, m: (0, i, 0))
    return pl.pallas_call(
        kernel,
        grid_spec=pltpu.PrefetchScalarGridSpec(
            num_scalar_prefetch=1,
            grid=(nq,),
            in_specs=[
                blk(LANES),
                pl.BlockSpec(kv.shape, lambda i, m: (0, 0)),
                pl.BlockSpec((BQ, 1), lambda i, m: (i, 0)),
            ],
            out_specs=(pl.BlockSpec((BQ, QCOLS), lambda i, m: (i, 0)), blk(1)),
        ),
        out_shape=(sh((Rq, QCOLS), bf16), sh((GROUP, Rq, 1), f32)),
        compiler_params=pltpu.CompilerParams(vmem_limit_bytes=48 * MIB),
        cost_estimate=cost(17),
        name="attend",
    )(meta, q, kv, starts)


def attend_back(q, kv, starts, meta, lse, mixed, dattn, wo):
    _, Rq, _ = q.shape
    nq = Rq // BQ
    M = GROUP * BQ
    K = kv.shape[0]

    def kernel(meta, q_ref, kv_ref, st_ref, l_ref, o_ref, g_ref, w_ref, dq_ref, dkv_ref, dw_ref):
        i = pl.program_id(0)

        @pl.when(i == 0)
        def _():
            dkv_ref[...] = jnp.zeros_like(dkv_ref)
            dw_ref[...] = jnp.zeros_like(dw_ref)

        g = g_ref[...]
        mixed = o_ref[...]
        dm = mm(g, w_ref[...], NT).astype(bf16).astype(f32)
        dw_ref[...] += mm(mixed, g, TN)
        low = low_half()
        d0 = dm[:, :LANES]
        d1 = jnp.concatenate([dm[:, LANES:], jnp.zeros((BQ, LANES - HW), f32)], axis=1)
        m0 = mixed[:, :LANES].astype(f32)
        m1 = jnp.concatenate([mixed[:, LANES:].astype(f32), jnp.zeros((BQ, LANES - HW), f32)], axis=1)
        total = lambda a: jnp.sum(a, axis=1, keepdims=True)
        e0, e1 = d0 * m0, d1 * m1
        first = total(jnp.where(low, e0, 0.0))
        delta = jnp.stack([first, total(jnp.where(low, 0.0, e0)), total(e1)])
        high = lambda a: jnp.where(low, 0.0, a).astype(bf16)
        do = jnp.concatenate([high(swap(d0)), high(d0), high(swap(d1))], axis=0)
        qv = q_ref[...].reshape(M, LANES)
        lse = l_ref[...]
        st = st_ref[...]
        last = (meta[nq] + i * BQ + BQ - 1) // BK + 1

        def step(kb, dq):
            at = pl.ds(pl.multiple_of(kb * BK, BK), BK)
            keys = kv_ref[at, :]
            s = mm(qv, keys, NT).reshape(GROUP, BQ, BK)
            p = jnp.where(seen(meta, st, i, kb, nq), jnp.exp(s - lse), 0.0)
            dp = mm(do, keys, NT).reshape(GROUP, BQ, BK)
            ds = (p * (dp - delta)).astype(bf16).reshape(M, BK)
            pb = p.astype(bf16).reshape(M, BK)
            dkv_ref[at, :] += mm(ds, qv, TN) + mm(pb, do, TN)
            return dq + mm(ds, keys)

        dq = lax.fori_loop(meta[i], last, step, jnp.zeros((M, LANES), f32))
        dq_ref[...] = (dq * (1.0 / math.sqrt(HW))).astype(bf16).reshape(GROUP, BQ, LANES)

    sh = jax.ShapeDtypeStruct
    blk = lambda w: pl.BlockSpec((GROUP, BQ, w), lambda i, m: (0, i, 0))
    rows = lambda w: pl.BlockSpec((BQ, w), lambda i, m: (i, 0))
    full = lambda *shape: pl.BlockSpec(shape, lambda i, m: (0, 0))
    return pl.pallas_call(
        kernel,
        grid_spec=pltpu.PrefetchScalarGridSpec(
            num_scalar_prefetch=1,
            grid=(nq,),
            in_specs=[
                blk(LANES), full(*kv.shape), rows(1), blk(1), rows(QCOLS), rows(D), full(QCOLS, D),
            ],
            out_specs=(blk(LANES), full(K, LANES), full(QCOLS, D)),
        ),
        out_shape=(sh((GROUP, Rq, LANES), bf16), sh((K, LANES), f32), sh((QCOLS, D), f32)),
        compiler_params=pltpu.CompilerParams(vmem_limit_bytes=48 * MIB),
        cost_estimate=cost(2),
        name="attend_back",
    )(meta, q, kv, starts, lse, mixed, dattn, wo)


def weight_grads(dq, dkv, kin, ok, tables, h1, packed, tail):
    _, Rq, _ = dq.shape
    step = 256
    arrivals = kin.shape[0]

    def kernel(ok_ref, dq_ref, dkv_ref, kin_ref, c_ref, a_ref, b_ref, h_ref, w_ref, t_ref, o_ref, p_ref, acc):
        i = pl.program_id(0)

        @pl.when(i == 0)
        def _():
            acc[...] = jnp.zeros_like(acc)

        kv = dkv_ref[...]
        for k in range(arrivals):
            kv = kv + jnp.where(ok_ref[k] > 0, kin_ref[k].astype(f32), 0.0)
        kv = kv.astype(bf16).astype(f32)
        low = low_half()
        tables = (c_ref[...], a_ref[...], b_ref[...])
        q = [dq_ref[h].astype(f32) for h in range(GROUP)]
        kv = swap(kv)
        t0 = turn_back(jnp.where(low, q[0], swap(q[1])), *tables)
        t1 = turn_back(jnp.where(low, q[2], kv), *tables)
        out = jnp.concatenate([t0, t1, jnp.where(low, kv, 0.0)], axis=1).astype(bf16)
        o_ref[...] = out
        acc[...] += mm(h_ref[...], out, TN)

        @pl.when(i == Rq // step - 1)
        def _():
            w = w_ref[...].astype(f32)
            dw = acc[...]
            t = t_ref[...]
            lane = lax.broadcasted_iota(jnp.int32, (1, LANES), 1)
            gain = jnp.sum(jnp.where(lane == ok_ref[arrivals], w[:, 2 * LANES:], 0.0), axis=1, keepdims=True)
            d_gain = jnp.sum(w * dw, axis=1, keepdims=True) / gain
            t = t + jnp.where(lane == ok_ref[arrivals] + 1, d_gain, 0.0)
            p_ref[:, :2 * LANES] = dw[:, :2 * LANES].astype(bf16)
            p_ref[:, 2 * LANES:] = jnp.where(low, dw[:, 2 * LANES:], t).astype(bf16)

    sh = jax.ShapeDtypeStruct
    heads = lambda n: pl.BlockSpec((n, step, LANES), lambda i: (0, i, 0))
    return pl.pallas_call(
        kernel,
        grid=(Rq // step,),
        out_shape=(sh((Rq, AUX), bf16), sh((D, AUX), bf16)),
        in_specs=[pl.BlockSpec(memory_space=pltpu.SMEM), heads(GROUP), row_block(step, LANES), heads(arrivals)]
        + [row_block(step, LANES)] * 3
        + [row_block(step, D), whole_block(packed), whole_block(tail)],
        out_specs=(row_block(step, AUX), pl.BlockSpec((D, AUX), lambda i: (0, 0))),
        scratch_shapes=[pltpu.VMEM((D, AUX), f32)],
        compiler_params=pltpu.CompilerParams(vmem_limit_bytes=48 * MIB),
        cost_estimate=cost(2),
        name="weight_grads",
    )(ok, dq, dkv, kin, *tables, h1, packed, tail)


def experts(h2_own, g_own, g_oth, router, hot, weights, nz, nb, cid):
    T = h2_own.shape[0]
    nc = nb // 2
    step = 2 * T
    units = 2 * nc
    dz = D // nz
    C = D + LANES
    W = 3 * FF
    nw = len(weights)
    resident = nb <= 8

    def kernel(x_ref, g0_ref, g1_ref, r_ref, e_ref, *rest):
        win = rest[:nw]
        y_ref, s_ref = rest[nw:nw + 2]
        rest = rest[nw + 2:]
        din = rest[:nz]
        h_all, hbuf, part, gbuf, ybuf, wc, acc, zbuf, gs, zs, sem, gsem, ysem, *pair = rest[nz:]
        me = Layer(nb)
        me.enter((1,))
        own, oth = h_all.at[0], h_all.at[1]
        mate = remote(x_ref, oth.at[me.b], zs.at[0], zs.at[1], me.across(1), me.b)
        mate.start()
        ga = Gather(me, x_ref, own, gs.at[0])
        gb = Gather(me, oth.at[me.b], oth, gs.at[1])
        ga.start()
        mine = pltpu.make_async_copy(x_ref, own.at[me.b], zs.at[2])
        mine.start()
        rows_at = lambda d: pl.ds(pl.multiple_of(me.across(d) * dz, dz), dz)
        loads = [
            pltpu.make_async_copy(win[k], wc.at[rows_at(d), pl.ds(c, a.shape[1])], sem.at[k])
            for k, (a, d, c) in enumerate(weights)
        ]
        for c in loads:
            c.start()

        def place(u):
            other = (u >= 2) & (u < nc + 2)
            j = jnp.where(u < 2, u, jnp.where(other, u - 2, 2 * nc + 1 - u))
            return jnp.where(other, 1, 0), j

        def cot(u, h):
            _, j = place(u)
            rows = pl.ds(pl.multiple_of(me.unit(j) * step, step), step)
            slot = lax.rem(u, 2)
            return pltpu.make_async_copy((g1_ref if h else g0_ref).at[rows], gbuf.at[slot], gsem.at[slot])

        def cot_start(u):
            h, _ = place(u)
            pl.when(h == 0)(lambda: cot(u, 0).start())
            pl.when(h == 1)(lambda: cot(u, 1).start())

        def result(u):
            h, j = place(u)
            slot = lax.rem(u, 2)
            return pltpu.make_async_copy(
                ybuf.at[slot], y_ref.at[h, pl.ds(pl.multiple_of(me.unit(j) * 2, 2), 2)], ysem.at[slot])

        cot_start(jnp.int32(0))
        acc[...] = jnp.zeros_like(acc)
        ra, rb = pair_of(me, part, *pair)
        ga.relay1()
        for c in loads:
            c.wait()
        mine.wait()

        def at(k, f):
            def run(u):
                pl.when(u == k)(f)
            return run

        def arrive(u):
            def first():
                ga.relay2()
                mate.wait_recv()
                gb.start()

            def second():
                ga.relay3()
                gb.relay1()

            at(1, first)(u)
            at(2, second)(u)
            at(3, gb.relay2)(u)
            at(4, gb.relay3)(u)
            for k in range(units):
                h = 1 if 2 <= k < nc + 2 else 0
                j = k if k < 2 else (k - 2 if h else 2 * nc + 1 - k)
                at(k, lambda h=h, j=j: (gb if h else ga).passed(j))(u)

        def depart(u):
            for k in range(units):
                h = 1 if 2 <= k < nc + 2 else 0
                j = k if k < 2 else (k - 2 if h else 2 * nc + 1 - k)
                at(k, lambda h=h, j=j: (rb if h else ra).start(j))(u)

            def mates():
                for j in rb.order[:-1]:
                    rb.phase1(j)

            at(nc + 1, mates)(u)

            def ours():
                ra.phase1(3)
                ra.phase1(1)

            if nc == 4:
                at(nc + 2, ours)(u)

        @pl.loop(0, units)
        def _(u):
            h, j = place(u)
            slot = lax.rem(u, 2)
            pl.when(u + 1 < units)(lambda: cot_start(u + 1))
            arrive(u)
            cot(u, 0).wait()
            pl.when(u >= 2)(lambda: result(u - 2).wait())
            two = pl.ds(pl.multiple_of(me.unit(j) * 2, 2), 2)
            if resident:
                x = h_all[h, two].reshape(step, D)
            else:
                c = pltpu.make_async_copy(h_all.at[h, two], hbuf, zs.at[5])
                c.start()
                c.wait()
                x = hbuf[...].reshape(step, D)
            hot = e_ref[...]
            mask = gbuf[slot, :, D:].astype(f32) > 0
            logits = mm(x, r_ref[...])
            top = jnp.max(jnp.where(mask, logits, NEG), axis=1, keepdims=True)
            w = jnp.where(mask, jnp.exp(jnp.where(mask, logits - top, 0.0)), 0.0)
            gate = jnp.sum(w * hot, axis=1, keepdims=True) / jnp.sum(w, axis=1, keepdims=True)
            gu = mm(x, wc[:, :2 * FF])
            a, up = gu[:, :FF], gu[:, FF:]
            sg = jax.nn.sigmoid(a)
            silu = a * sg
            act = (silu * up).astype(bf16)
            g = gbuf[slot, :, :D]
            ybuf[slot] = (gate * mm(act, wc[:, 2 * FF:], NT)).astype(bf16).reshape(2, T, D)
            result(u).start()
            raw = mm(g, wc[:, 2 * FF:])
            acc[:, 2 * FF:] += mm((gate * g.astype(f32)).astype(bf16), act, TN)
            dgate = jnp.sum(act.astype(f32) * raw, axis=1, keepdims=True)
            dact = gate * raw
            dgu = jnp.concatenate(
                [dact * up * (sg * (1.0 + a * (1.0 - sg))), dact * silu], axis=1).astype(bf16)
            acc[:, :2 * FF] += mm(x, dgu, TN)
            part[h, two, :, :D] = mm(dgu, wc[:, :2 * FF], NT).astype(bf16).reshape(2, T, D)
            hi = dgate.astype(bf16).astype(f32)
            part[h, two, :, D:] = (hi * hot + swap((dgate - hi) * hot)).astype(bf16).reshape(2, T, LANES)
            depart(u)

        rb.phase2()
        for j in (2,) if nc == 4 else ra.order[:-1]:
            ra.phase1(j)
        wc[...] = acc[...].astype(bf16)
        saves = [pltpu.make_async_copy(wc.at[rows_at(d)], din[d], sem.at[d]) for d in range(nz)]
        for c in saves:
            c.start()
        rb.end(write_to(zbuf, 0))
        back = remote(zbuf.at[0], zbuf.at[1], zs.at[3], zs.at[4], me.across(1), me.b)
        back.start()
        ra.phase2()
        back.wait_recv()
        ra.end(add_to(s_ref, zbuf, 1))
        back.wait_send()
        mate.wait_send()
        for r in (ga, gb, ra, rb):
            r.sent()
        for c in saves:
            c.wait()
        result(jnp.int32(units - 2)).wait()
        result(jnp.int32(units - 1)).wait()

    sh = jax.ShapeDtypeStruct
    v = lambda shape, kind=bf16: pltpu.VMEM(shape, kind)
    return pl.pallas_call(
        kernel,
        out_shape=(sh((2, nb, T, D), bf16), sh((T, C), f32))
        + (sh((dz, W), bf16),) * nz
        + (() if resident else (sh((2, nb, T, D), bf16),)),
        in_specs=[ANY] * 3 + [VMEM] * 2 + [ANY] * nw,
        out_specs=(ANY, VMEM) + (ANY,) * (nz + int(not resident)),
        scratch_shapes=([v((2, nb, T, D))] if resident else [])
        + [
            v((2, T, D)), v((2, nb, T, C)), v((2, step, C)), v((2, 2, T, D)),
            v((D, W)), v((D, W), f32), v((2, T, C)),
            Gather.scratch(nb, 2), DMA((6,)), DMA((nw,)), DMA((2,)), DMA((2,)),
        ]
        + Reduce.scratch(nb, T, C, 2),
        compiler_params=pltpu.CompilerParams(
            collective_id=cid, has_side_effects=True, vmem_limit_bytes=60 * MIB
        ),
        cost_estimate=cost(70),
        name="experts",
    )(h2_own, g_own, g_oth, router, hot, *[a for a, _, _ in weights])


def finish(dh1, x, gain, dresid, pin, win, resid, ysum, grads):
    T = x.shape[0]
    groups, rp, S, _ = pin.shape
    senders = win.shape[0]
    m = len(grads)
    dz = grads[0].shape[0]

    def kernel(d_ref, x_ref, g_ref, r_ref, p_ref, w_ref, s_ref, y_ref, *rest):
        srcs = rest[:m]
        t_ref, q_ref, k_ref, v_ref, m_ref, o_ref, out_ref, in_ref, ex_ref = rest[m:]
        odd = lax.rem(lax.axis_index("ulysses"), 2)
        for e in range(2):
            total = functools.reduce(lambda a, b: a + b, [r[...].astype(f32) for r in srcs[e::2]])
            at = odd if e == 0 else 1 - odd
            in_ref[at] = total[:, :2 * FF]
            ex_ref[at] = total[:, 2 * FF:].T
        v = x_ref[...].astype(f32)
        inv = lax.rsqrt(jnp.mean(v * v, axis=1, keepdims=True) + EPS)
        n = v * inv
        w = d_ref[...] * g_ref[...]
        t_ref[...] = r_ref[...] + inv * (w - n * jnp.mean(w * n, axis=1, keepdims=True))
        out_ref[...] = s_ref[...] + y_ref[...]
        o_ref[...] = functools.reduce(lambda a, b: a + b, [w_ref[k].astype(f32) for k in range(senders)])
        small = 0.0
        for h in range(groups):
            row = 0.0
            for p in range(rp):
                row = row + p_ref[h, p].astype(f32)
            q_ref[:, h * QCOLS:(h + 1) * QCOLS] = row[:, :QCOLS]
            k_ref[:, h * HW:(h + 1) * HW] = row[:, QCOLS:QCOLS + HW]
            v_ref[:, h * HW:(h + 1) * HW] = row[:, QCOLS + HW:ROUTER_AT]
            small = small + row[:, 2 * LANES:]
        m_ref[...] = small

    sh = lambda *shape: jax.ShapeDtypeStruct(shape, f32)
    return pl.pallas_call(
        kernel,
        out_shape=(sh(T, D), sh(S, HEADS * HW), sh(S, KV * HW), sh(S, KV * HW), sh(S, LANES), sh(S, D), sh(T, D),
                   sh(2, dz, 2 * FF), sh(2, FF, dz)),
        in_specs=[VMEM] * (8 + m),
        out_specs=(VMEM,) * 9,
        compiler_params=pltpu.CompilerParams(vmem_limit_bytes=60 * MIB),
        cost_estimate=cost(2),
        name="finish",
    )(dh1, x, gain, dresid, pin, win, resid, ysum, *grads)


def locate(rows, lengths):
    passed = rows[:, None] >= jnp.cumsum(lengths)
    return jnp.sum(jnp.where(passed, lengths, 0), axis=-1)


def norm_rows(v, gain):
    inverse = lax.rsqrt(jnp.mean(v * v, axis=-1, keepdims=True) + EPS)
    normed = v * inverse
    return normed, inverse, normed * gain


def norm_back(upstream, normed, inverse, gain):
    d_normed = upstream * gain
    d_gain = jnp.sum(upstream * normed, axis=0)
    d_values = inverse * (d_normed - normed * jnp.mean(d_normed * normed, axis=-1, keepdims=True))
    return d_values, d_gain


def rows_of(a, start, count):
    return a if a.shape[0] == count else lax.dynamic_slice_in_dim(a, start, count, 0)


def widen(a, start, count):
    if a.shape[0] == count:
        return a
    return lax.dynamic_update_slice_in_dim(jnp.zeros((count,) + a.shape[1:], a.dtype), a, start, 0)


def on_device(tokens, lengths, routes, gain_attn, w_query, w_key, w_value, w_output, gain_moe,
              w_router, w_inner, w_outer, cotangent):
    nz = lax.axis_size("ulysses")
    nb = lax.axis_size("blk")
    z = lax.axis_index("ulysses")
    b = lax.axis_index("blk")
    T = tokens.shape[0]
    R = nb * T
    rp = nb // KV
    Rq = R // rp
    part = b % rp
    at = part * Rq
    n = nz * nb
    S = D // n
    E = w_router.shape[1]
    longest = min(LENMAX, n * T // 2)
    back = min(nz - 1, (longest - 1 + R - 1) // R)
    n_o = QCOLS // S
    odd = z % 2

    tail = jnp.concatenate(
        [w_router, gain_attn[:, None], gain_moe[:, None],
         jnp.zeros((S, AUX - ROUTER_AT - E - 2), bf16)], axis=1)
    pieces = jnp.stack([
        jnp.concatenate([
            w_query[:, h * QCOLS:(h + 1) * QCOLS], w_key[:, h * HW:(h + 1) * HW],
            w_value[:, h * HW:(h + 1) * HW], tail], axis=1)
        for h in range(KV)])
    lanes = jnp.arange(LANES, dtype=jnp.int32)
    named = jnp.any(routes[:, :, None] + HW == lanes[None, None, :], axis=1)
    cot_mask = jnp.concatenate([cotangent, named.astype(bf16)], axis=1)
    xg, packed = gather_inputs(tokens, pieces, nz, nb, 0)
    xg = xg.reshape(R, D)
    packed = packed.reshape(D, AUX)
    router = packed[:, 2 * LANES:]
    gains = packed[:, ROUTER_AT + E:ROUTER_AT + E + 2].astype(f32).T
    gain1, gain2 = gains[0:1], gains[1:2]

    experts_of = jnp.concatenate([w_inner, jnp.swapaxes(w_outer, 1, 2)], axis=2)
    flip = lambda d: [(k, k ^ d) for k in range(nz)]
    give = lambda w, d, lo, hi: lax.ppermute(
        lax.dynamic_index_in_dim(w, odd ^ (d % 2), 0, keepdims=False)[:, lo:hi], "ulysses", flip(d))
    W = 3 * FF
    experts_of, packed = lax.optimization_barrier((experts_of, packed))
    early = min(2, nz - 1)
    weights = [(lax.dynamic_index_in_dim(experts_of, odd, 0, keepdims=False), 0, 0),
               (give(experts_of, early, 0, W // 2), early, 0)]

    rows = z * R + jnp.arange(R, dtype=jnp.int32)
    opening = locate(rows, lengths)
    pair = lanes % HW
    frequency = THETA ** (-((pair % (HW // 2)).astype(f32) * 2.0 / HW))
    angles = (rows - opening).astype(f32)[:, None] * frequency[None, :]
    cos, sin = jnp.cos(angles), jnp.sin(angles)
    tables = (cos, jnp.where(pair < HW // 2, -sin, 0.0), jnp.where(pair < HW // 2, 0.0, sin))

    q, kv, h1 = project(xg, gain1, packed, *tables)
    if rp > 1:
        q = lax.dynamic_slice_in_dim(q, at, Rq, 1)
    array, *place = weights[1]
    kv, array = lax.optimization_barrier((kv, array))
    weights[1] = (array, *place)
    far, g_own, g_far, wo = halo_forward(kv, cot_mask, w_output, nz, nb, rp, back, 1)
    wo = wo.reshape(QCOLS, D)
    later, far = lax.optimization_barrier((experts_of, far))
    weights.append((give(later, early, W // 2, W), early, W // 2))
    weights += [(give(later, d, 0, W), d, 0) for d in range(1, nz) if d != early]
    kv_all = jnp.concatenate([far[d - 1] for d in range(back, 0, -1)] + [kv], axis=0)
    base = (z - back) * R
    starts = rows_of(opening, at, Rq) - base
    meta = jnp.concatenate([starts[::BQ] // BK, (back * R + at)[None]]).astype(jnp.int32)
    starts = starts[:, None]
    mixed, lse = attend(q, kv_all, starts, meta)
    attn, g_oth = reduce_product(widen(mixed, at, R), wo, g_far, nb, 2)
    g_own, g_oth = g_own.reshape(R, D + LANES), g_oth.reshape(R, D + LANES)

    resid = tokens.astype(f32) + attn
    n2, inv2, scaled2 = norm_rows(resid, gain2)
    h2_own = scaled2.astype(bf16)
    hot = (lanes == HW + b * EXP_DEV + odd).astype(f32)[None, :]
    y, summed, *grads = experts(h2_own, g_own, g_oth, router, hot, weights, nz, nb, 3)
    grads = grads[:nz]

    upstream = cotangent.astype(f32)
    dgates = summed[:, D:] + jnp.roll(summed[:, D:], HW, 1)
    logits = mm(h2_own, router)
    top = jnp.max(jnp.where(named, logits, NEG), axis=1, keepdims=True)
    w = jnp.where(named, jnp.exp(jnp.where(named, logits - top, 0.0)), 0.0)
    gates = w / jnp.sum(w, axis=1, keepdims=True)
    dlogits = gates * (dgates - jnp.sum(gates * dgates, axis=1, keepdims=True))
    dlogits = dlogits.astype(bf16)
    dh2 = summed[:, :D] + mm(dlogits, router, NT)
    d_norm2, d_gain2 = norm_back(dh2, n2, inv2, gain2)
    dresid = upstream + d_norm2
    split = min(3, nz)
    dattn, ysum, *grads[1:split] = middle(dresid.astype(bf16), y, grads[1:split], nz, nb, 5)
    dattn, *late = lax.optimization_barrier((dattn, *grads[split:]))
    grads[split:] = [lax.ppermute(a, "ulysses", flip(d)) for d, a in enumerate(late, split)]
    dattn = dattn.reshape(R, D)
    tail = mm(h2_own, dlogits, TN) + jnp.where(lanes == HW + E, d_gain2[:, None], 0.0)

    dq, dkv, dwo = attend_back(q, kv_all, starts, meta, lse, mixed, rows_of(dattn, at, Rq), wo)
    dkv, *late = lax.optimization_barrier((dkv, *grads[split:]))
    grads[split:] = late
    dkv = dkv.reshape(back + 1, R, LANES)
    dkv_out = jnp.stack([dkv[back - d] for d in range(back + 1)]).astype(bf16)
    kin = halo_back(dkv_out, nz, nb, rp, back, 6)
    ok = [(z + d < nz) if d else (part != p) for d in range(back + 1) for p in range(rp)]
    ok = jnp.stack([jnp.asarray(o).astype(jnp.int32) for o in ok] + [jnp.int32(HW + E)])
    if rp > 1:
        kin = lax.dynamic_slice_in_dim(kin, at, Rq, 1)
    turned, dw = weight_grads(
        dq, rows_of(dkv[back], at, Rq), kin, ok, [rows_of(t, at, Rq) for t in tables],
        rows_of(h1, at, Rq), packed, tail)
    dh1, pin, win = reduce_last(
        widen(turned, at, R), packed, dw.reshape(nz, nb, S, AUX),
        dwo.astype(bf16).reshape(nz, rp, S, D), nz, nb, rp, 7)
    d_tokens, d_query, d_key, d_value, small, d_output, out, d_inner, d_outer = finish(
        dh1, tokens, gain1, dresid, pin.reshape(KV, rp, S, AUX), win, resid, ysum, grads)
    return (
        out, d_tokens, small[:, HW + E + 1], d_query, d_key, d_value, d_output,
        small[:, HW + E], small[:, HW:HW + E], d_inner, d_outer,
    )


def solution(mesh):
    both = ("ulysses", "blk")
    rows = P(both, None)
    weights = (P(both), rows, rows, rows, rows, P(both), rows, P("blk", "ulysses", None), P("blk", None, "ulysses"))
    return jax.shard_map(
        on_device,
        mesh=mesh,
        in_specs=(rows, P(), rows) + weights + (rows,),
        out_specs=(rows, rows) + weights,
        check_vma=False,
    )
```

```python
import functools
import math

import jax
import jax.numpy as jnp
from jax import lax
from jax.experimental import pallas as pl
from jax.experimental.pallas import tpu as pltpu
from jax.sharding import PartitionSpec as P

D = 1536
HEADS = 24
KV = 8
HW = 64
GROUP = HEADS // KV
FF = 512
TOPK = 8
EXP_DEV = 2
LENMAX = 4096
EPS = 1e-05
THETA = 10000.0
NEG = -1e30
LANES = 128
AUX = 384
ROUTER_AT = 320
QCOLS = GROUP * HW

f32 = jnp.float32
bf16 = jnp.bfloat16
MESH = pl.DeviceIdType.MESH
ANY = pl.BlockSpec(memory_space=pl.ANY)
VMEM = pl.BlockSpec(memory_space=pltpu.VMEM)
DMA = pltpu.SemaphoreType.DMA
MIB = 1 << 20
NO_COST = pl.CostEstimate(flops=0, bytes_accessed=0, transcendentals=0)


def dev(u, b):
    return {"ulysses": u, "blk": b}


def remote(src, dst, ss, rs, u, b):
    return pltpu.make_async_remote_copy(
        src_ref=src, dst_ref=dst, send_sem=ss, recv_sem=rs,
        device_id=dev(u, b), device_id_type=MESH,
    )


def signal(sem, u, b):
    pl.semaphore_signal(sem, inc=1, device_id=dev(u, b), device_id_type=MESH)


class Layer:
    def __init__(self, nb):
        self.u = lax.axis_index("ulysses")
        self.b = lax.axis_index("blk")
        self.nb = nb
        self.nc = nb // 2
        self.chip = self.b // 2
        self.core = lax.rem(self.b, 2)
        self.sib = self.chip * 2 + 1 - self.core

    def peer(self, i):
        return lax.rem(self.chip + i, self.nc) * 2 + self.core

    def unit(self, j):
        if self.nc != 4:
            return lax.rem(self.chip + self.nc - j, self.nc)
        x, y = lax.rem(self.chip, 2), self.chip // 2
        jx, jy = j % 2, j // 2
        return x + jx - 2 * x * jx + 2 * (y + jy - 2 * y * jy)

    def far(self, j):
        return self.unit(j) * 2 + self.core

    def across(self, d):
        at = self.u
        for k in range(d.bit_length()):
            if (d >> k) & 1:
                at = at + (1 << k) - (2 << k) * lax.rem(self.u // (1 << k), 2)
        return at

    def enter(self, flips=()):
        bar = pltpu.get_barrier_semaphore()
        for i in range(1, self.nc):
            signal(bar, self.u, self.peer(i))
        signal(bar, self.u, self.sib)
        for d in flips:
            signal(bar, self.across(d), self.b)
        pl.semaphore_wait(bar, self.nc + len(flips))


class Gather:
    def __init__(self, me, src, dst, sems):
        self.me, self.src, self.dst, self.sems = me, src, dst, sems
        self.quad = me.nc == 4
        half = dst.shape[1] // 2
        self.a, self.b = pl.ds(0, half), pl.ds(half, half)

    @staticmethod
    def scratch(nb, *lead):
        return DMA(lead + (2, 10 if nb == 8 else nb))

    def copy(self, k):
        me, src, dst = self.me, self.src, self.dst
        send = lambda s, d, to: remote(s, d, self.sems.at[0, k], self.sems.at[1, k], me.u, to)
        same = lambda at, to: send(dst.at[at], dst.at[at], to)
        part = lambda at, rows, to: send(dst.at[at, rows], dst.at[at, rows], to)
        if self.quad:
            if k < 4:
                rows = self.b if k % 2 else self.a
                return send(src.at[rows], dst.at[me.b, rows], me.far(1 + k // 2))
            if k < 6:
                return part(me.far(k - 3), self.b if k == 5 else self.a, me.far(6 - k))
            if k == 6:
                return send(src, dst.at[me.b], me.sib)
            return same(me.far(k - 6), me.sib)
        if k < me.nc:
            return send(src, dst.at[me.b], me.peer(k))
        if k == me.nc:
            return send(src, dst.at[me.b], me.sib)
        return same(me.far(k - me.nc), me.sib)

    def start(self):
        if self.quad:
            for k in (0, 3, 1, 2, 6):
                self.copy(k).start()
        else:
            for k in range(1, self.me.nc + 1):
                self.copy(k).start()

    def relay1(self):
        if self.quad:
            self.copy(0).wait_recv()
            self.copy(4).start()
            self.copy(3).wait_recv()
            self.copy(5).start()

    def relay2(self):
        if self.quad:
            self.copy(1).wait_recv()
            self.copy(7).start()
            self.copy(2).wait_recv()
            self.copy(8).start()
        else:
            for k in range(1, self.me.nc):
                self.copy(k).wait_recv()
                self.copy(self.me.nc + k).start()

    def relay3(self):
        if self.quad:
            self.copy(4).wait_recv()
            self.copy(5).wait_recv()
            self.copy(9).start()

    def passed(self, j):
        self.copy((6 if self.quad else self.me.nc) + j).wait_recv()

    def sent(self):
        for k in range(10) if self.quad else range(1, 2 * self.me.nc):
            self.copy(k).wait_send()

    def rest(self):
        self.relay1()
        self.relay2()
        self.relay3()

    def finish(self):
        for j in range(self.me.nc):
            self.passed(j)
        self.sent()


class Reduce:
    def __init__(self, me, get, source, sib_in, snd, land, sems):
        self.me, self.get, self.source = me, get, source
        self.sib_in, self.snd, self.land, self.sems = sib_in, snd, land, sems
        self.quad = me.nc == 4
        self.rows = sib_in.shape[1]
        half = self.rows // 2
        self.a, self.b = pl.ds(0, half), pl.ds(half, half)
        self.order = (3, 1, 2, 0) if self.quad else (*range(1, me.nc), 0)

    @staticmethod
    def scratch(nb, rows, cols, *lead):
        nc = nb // 2
        shape = lead + ((6, rows // 2, cols) if nc == 4 else (nc, rows, cols))
        return [
            pltpu.VMEM(lead + (nc, rows, cols), bf16), pltpu.VMEM(shape, bf16), pltpu.VMEM(shape, bf16),
            DMA(lead + (2, 10 if nc == 4 else 2 * nc)),
        ]

    def copy(self, k):
        me = self.me
        ss, rs = self.sems.at[0, k], self.sems.at[1, k]
        if k < me.nc:
            return remote(self.source(k), self.sib_in.at[k], ss, rs, me.u, me.sib)
        k = k - me.nc
        to = me.far((1, 1, 2, 2, 2, 1)[k] if self.quad else k)
        return remote(self.snd.at[k], self.land.at[k], ss, rs, me.u, to)

    def start(self, j):
        self.copy(j).start()

    def part(self, j, rows):
        return self.get(j, rows) + self.sib_in[j, rows].astype(f32)

    def send(self, k, value):
        self.snd[k] = value.astype(bf16)
        self.copy(self.me.nc + k).start()

    def phase1(self, j):
        self.copy(j).wait_recv()
        if not self.quad:
            self.send(j, self.part(j, pl.ds(0, self.rows)))
            return
        if j != 2:
            self.send(0 if j == 1 else 1, self.part(j, self.a))
        if j != 1:
            self.send(2 if j == 2 else 3, self.part(j, self.b))

    def landed(self, k):
        self.copy(self.me.nc + k).wait_recv()
        return self.land[k].astype(f32)

    def phase2(self):
        if self.quad:
            self.send(4, self.part(2, self.a) + self.landed(1))
            self.send(5, self.part(1, self.b) + self.landed(3))

    def end(self, write):
        self.copy(0).wait_recv()
        if self.quad:
            write(self.a, self.part(0, self.a) + self.landed(0) + self.landed(4))
            write(self.b, self.part(0, self.b) + self.landed(2) + self.landed(5))
        else:
            total = self.part(0, pl.ds(0, self.rows))
            for j in range(1, self.me.nc):
                total = total + self.landed(j)
            write(pl.ds(0, self.rows), total)

    def sent(self):
        for k in range(10) if self.quad else (*range(self.me.nc + 1), *range(self.me.nc + 1, 2 * self.me.nc)):
            if self.quad or k != self.me.nc:
                self.copy(k).wait_send()


def made(me, block, mine, sib_out, sib_in, snd, land, sems, waits=True):
    red = Reduce(me, lambda j, rows: mine[j, rows], lambda j: sib_out.at[j], sib_in, snd, land, sems)
    for j in red.order:
        sib_out[j] = block(me.unit(j) * 2 + 1 - me.core).astype(bf16)
        red.start(j)
    for j in red.order:
        mine[j] = block(me.far(j))
        if j and waits:
            red.phase1(j)
    return red


def made_scratch(nb, rows, cols):
    nc = nb // 2
    return [pltpu.VMEM((nc, rows, cols), f32), pltpu.VMEM((nc, rows, cols), bf16)] + Reduce.scratch(nb, rows, cols)


def keep(me, src, dst, sem):
    c = pltpu.make_async_copy(src, dst.at[me.b], sem)
    c.start()
    return c


def gather_inputs(x, pieces, wo, gm, expert, swap_d, nz, nb, cid):
    groups, shard, _ = pieces.shape
    rp = nb // groups
    n_o = QCOLS // shard
    n = nz * nb

    def kernel(x_ref, p_ref, w_ref, g_ref, e_ref, xo, po, wo_out, go, gx, eo, gs, ps, pr, zs, zr, ws, wr, ls):
        me = Layer(nb)
        lin = me.u * nb + me.b
        u, b = me.u, me.b
        bar = pltpu.get_barrier_semaphore()

        @pl.loop(1, n)
        def _(i):
            t = lax.rem(lin + i, n)
            signal(bar, t // nb, lax.rem(t, nb))

        pl.semaphore_wait(bar, n - 1)

        def piece(i):
            tb = lax.rem(b + i, nb)
            return remote(p_ref.at[tb // rp], po.at[u, b], ps.at[i], pr.at[i], u, tb)

        for i in range(1, nb):
            piece(i).start()
        own = pltpu.make_async_copy(p_ref.at[b // rp], po.at[u, b], ls.at[0])
        own.start()
        g = Gather(me, x_ref, xo, gs.at[0])
        g.start()
        cot = Gather(me, g_ref, go, gs.at[1])
        for i in range(1, nb):
            piece(i).wait()
        own.wait()

        def up(k):
            o = u - k + 1
            return remote(po.at[o], po.at[o], zs.at[0, k], zr.at[0, k], u + 1, b)

        def down(k):
            o = u + k - 1
            return remote(po.at[o], po.at[o], zs.at[1, k], zr.at[1, k], u - 1, b)

        def here(way, k):
            remote(po.at[u], po.at[u], zs.at[way, k], zr.at[way, k], u, me.sib).wait_recv()

        def relay(k):
            if k > 1:
                pl.when(u >= k - 1)(lambda: here(0, k - 1))
                pl.when(u + k - 1 < nz)(lambda: here(1, k - 1))
            pl.when((u >= k - 1) & (u + 1 < nz))(lambda: up(k).start())
            pl.when((u + k - 1 < nz) & (u > 0))(lambda: down(k).start())

        relay(1)
        hg = lin // n_o
        slot = lax.rem(lin, n_o)

        def weight(zo, p):
            tz, tb = lax.rem(u + zo, nz), hg * rp + p
            return tb, remote(w_ref, wo_out.at[slot], ws.at[zo * rp + p], wr.at[slot], tz, tb)

        g.relay1()
        for k in range(2, nz):
            relay(k)
            if k == 2:
                g.relay2()
                cot.start()
        stay = pltpu.make_async_copy(w_ref, wo_out.at[slot], ls.at[1])
        for zo in range(nz):
            for p in range(rp):
                tb, c = weight(zo, p)
                if zo:
                    c.start()
                else:
                    pl.when(tb != b)(c.start)
                    pl.when(tb == b)(stay.start)
        mate = remote(g_ref, gx, ls.at[4], ls.at[5], me.across(1), b)
        mate.start()
        half = remote(e_ref, eo, ls.at[6], ls.at[7], me.across(swap_d), b)
        half.start()
        xk = keep(me, x_ref, xo, ls.at[2])
        gk = keep(me, g_ref, go, ls.at[3])
        g.relay3()
        cot.rest()
        g.finish()
        cot.finish()
        pl.when(u >= nz - 1)(lambda: here(0, nz - 1))
        pl.when(u + nz - 1 < nz)(lambda: here(1, nz - 1))
        for k in range(1, nz):
            pl.when((u >= k - 1) & (u + 1 < nz))(lambda k=k: up(k).wait_send())
            pl.when((u + k - 1 < nz) & (u > 0))(lambda k=k: down(k).wait_send())
        for zo in range(nz):
            for p in range(rp):
                tb, c = weight(zo, p)
                if zo:
                    c.wait_send()
                else:
                    pl.when(tb != b)(c.wait_send)
                    pl.when(tb == b)(stay.wait)
        for j in range(n_o):
            src = (b // rp) * n_o + j
            c = remote(w_ref, wo_out.at[j], ws.at[0], wr.at[j], u, me.sib)
            pl.when(src != lin)(c.wait_recv)
        for c in (mate, half, xk, gk):
            c.wait()

    sh = jax.ShapeDtypeStruct
    return pl.pallas_call(
        kernel,
        out_shape=(
            sh((nb,) + x.shape, x.dtype), sh((nz, nb, shard, AUX), bf16), sh((n_o, shard, D), bf16),
            sh((nb,) + gm.shape, gm.dtype), sh(gm.shape, gm.dtype), sh(expert.shape, bf16),
        ),
        in_specs=[ANY] * 5,
        out_specs=(ANY,) * 6,
        scratch_shapes=[Gather.scratch(nb, 2)]
        + [DMA((nb,))] * 2
        + [DMA((2, nz))] * 2
        + [DMA((nz * rp,)), DMA((n_o,)), DMA((8,))],
        compiler_params=pltpu.CompilerParams(collective_id=cid, has_side_effects=True),
        cost_estimate=NO_COST,
        name="gather_inputs",
    )(x, pieces, wo, gm, expert)


def halo_forward(kv, gx, nz, nb, back, cid):
    def kernel(x_ref, g_ref, o_ref, go, ks, kr, gs, ls):
        me = Layer(nb)
        u, b = me.u, me.b
        bar = pltpu.get_barrier_semaphore()
        for d in range(1, nz):
            signal(bar, lax.rem(u + d, nz), b)
        for i in range(1, me.nc):
            signal(bar, u, me.peer(i))
        signal(bar, u, me.sib)
        pl.semaphore_wait(bar, nz - 1 + me.nc)

        def copy(d):
            src = x_ref if d == 1 else o_ref.at[d - 2]
            return remote(src, o_ref.at[d - 1], ks.at[d - 1], kr.at[d - 1], u + 1, b)

        def relay(d):
            if d > 1:
                pl.when(u >= d - 1)(lambda: copy(d - 1).wait_recv())
            pl.when((u >= d - 1) & (u + 1 < nz))(lambda: copy(d).start())

        relay(1)
        g = Gather(me, g_ref, go, gs)
        g.start()
        own = keep(me, g_ref, go, ls)
        for d in range(2, back + 1):
            relay(d)
        g.rest()
        g.finish()
        own.wait()
        pl.when(u >= back)(lambda: copy(back).wait_recv())
        for d in range(1, back + 1):
            pl.when((u >= d - 1) & (u + 1 < nz))(lambda d=d: copy(d).wait_send())

    sh = jax.ShapeDtypeStruct
    return pl.pallas_call(
        kernel,
        out_shape=(sh((back,) + kv.shape, kv.dtype), sh((nb,) + gx.shape, gx.dtype)),
        in_specs=[ANY] * 2,
        out_specs=(ANY,) * 2,
        scratch_shapes=[DMA((back,))] * 2 + [Gather.scratch(nb), DMA],
        compiler_params=pltpu.CompilerParams(collective_id=cid, has_side_effects=True),
        cost_estimate=NO_COST,
        name="halo_forward",
    )(kv, gx)


def pair_of(me, p_ref, sib_in, snd, land, sems):
    def one(h):
        return Reduce(
            me, lambda j, rows: p_ref[h, me.far(j), rows].astype(f32),
            lambda j: p_ref.at[h, me.unit(j) * 2 + 1 - me.core],
            sib_in.at[h], snd.at[h], land.at[h], sems.at[h])
    return one(0), one(1)


def write_to(ref, *lead):
    def write(rows, value):
        ref[(*lead, rows)] = value.astype(ref.dtype)
    return write


def add_to(ref, other, at):
    def write(rows, value):
        ref[rows] = value + other[at, rows].astype(f32)
    return write


def reduce_product(lhs, rhs, nb, cid):
    rows = lhs.shape[0] // nb
    cols = rhs.shape[1]

    def kernel(l_ref, r_ref, o_ref, *scratch):
        me = Layer(nb)
        me.enter()

        def block(t):
            part = l_ref[pl.ds(pl.multiple_of(t * rows, rows), rows), :]
            return jnp.dot(part, r_ref[...], preferred_element_type=f32)

        red = made(me, block, *scratch)
        red.phase2()
        red.end(write_to(o_ref))
        red.sent()

    return pl.pallas_call(
        kernel,
        out_shape=jax.ShapeDtypeStruct((rows, cols), f32),
        in_specs=[VMEM, VMEM],
        out_specs=VMEM,
        scratch_shapes=made_scratch(nb, rows, cols),
        compiler_params=pltpu.CompilerParams(
            collective_id=cid, has_side_effects=True, vmem_limit_bytes=48 * MIB
        ),
        cost_estimate=NO_COST,
        name="reduce_product",
    )(lhs, rhs)


def middle(x, ypart, nb, cid):
    _, _, rows, cols = ypart.shape

    def kernel(x_ref, y_ref, xo, o_ref, z_ref, gs, ls, *pair):
        me = Layer(nb)
        me.enter()
        g = Gather(me, x_ref, xo, gs)
        g.start()
        r0, r1 = pair_of(me, y_ref, *pair)
        for r in (r1, r0):
            for j in r.order:
                r.start(j)
        own = keep(me, x_ref, xo, ls)
        for j in r1.order[:-1]:
            r1.phase1(j)
        g.rest()
        r1.phase2()
        for j in r0.order[:-1]:
            r0.phase1(j)
        r0.phase2()
        r1.end(write_to(z_ref))
        g.finish()
        r0.end(write_to(o_ref))
        r0.sent()
        r1.sent()
        own.wait()

    sh = jax.ShapeDtypeStruct
    return pl.pallas_call(
        kernel,
        out_shape=(sh((nb,) + x.shape, x.dtype), sh((rows, cols), f32), sh((rows, cols), bf16)),
        in_specs=[ANY, VMEM],
        out_specs=(ANY, VMEM, VMEM),
        scratch_shapes=[Gather.scratch(nb), DMA]
        + Reduce.scratch(nb, rows, cols, 2),
        compiler_params=pltpu.CompilerParams(
            collective_id=cid, has_side_effects=True, vmem_limit_bytes=56 * MIB
        ),
        cost_estimate=NO_COST,
        name="middle",
    )(x, ypart)


def halo_back(dkv, yfar, nz, nb, rp, back, cid):
    R = dkv.shape[1]

    def kernel(d_ref, y_ref, kin, yo, ks, kr, ys):
        me = Layer(nb)
        first = (me.b // rp) * rp
        part = lax.rem(me.b, rp)
        bar = pltpu.get_barrier_semaphore()
        others = [(zo, p) for zo in range(nz) for p in range(rp) if zo or p]
        for zo, p in others:
            signal(bar, lax.rem(me.u + zo, nz), first + lax.rem(part + p, rp))
        pl.semaphore_wait(bar, len(others))

        def copy(d, p):
            k = d * rp + p
            return remote(d_ref.at[d], kin.at[d * rp + part], ks.at[k], kr.at[d * rp + part], me.u - d, first + p)

        def arrival(d, p):
            k = d * rp + p
            return remote(d_ref.at[d], kin.at[k], ks.at[k], kr.at[k], me.u, me.sib)

        for d in range(back + 1):
            for p in range(rp):
                if d:
                    pl.when(me.u >= d)(lambda d=d, p=p: copy(d, p).start())
                elif rp > 1:
                    pl.when(part != p)(lambda d=d, p=p: copy(d, p).start())
        mate = remote(y_ref, yo, ys.at[0], ys.at[1], me.across(1), me.b)
        mate.start()
        for d in range(back + 1):
            for p in range(rp):
                if d:
                    pl.when(me.u >= d)(lambda d=d, p=p: copy(d, p).wait_send())
                    pl.when(me.u + d < nz)(lambda d=d, p=p: arrival(d, p).wait_recv())
                elif rp > 1:
                    pl.when(part != p)(lambda d=d, p=p: copy(d, p).wait_send())
                    pl.when(part != p)(lambda d=d, p=p: arrival(d, p).wait_recv())
        mate.wait()

    return pl.pallas_call(
        kernel,
        out_shape=(
            jax.ShapeDtypeStruct(((back + 1) * rp, R, LANES), bf16), jax.ShapeDtypeStruct(yfar.shape, bf16),
        ),
        in_specs=[ANY] * 2,
        out_specs=(ANY,) * 2,
        scratch_shapes=[DMA(((back + 1) * rp,))] * 2 + [DMA((2,))],
        compiler_params=pltpu.CompilerParams(collective_id=cid, has_side_effects=True),
        cost_estimate=NO_COST,
        name="halo_back",
    )(dkv, yfar)


def reduce_last(lhs, rhs, pieces, nz, nb, rp, cid):
    rows = lhs.shape[0] // nb
    cols = rhs.shape[0]
    _, count, shard, width = pieces.shape
    n_o = nz * rp
    wide = (count - nb) // rp
    n = nz * nb

    def kernel(l_ref, r_ref, p_ref, o_ref, pin, win, land, tmp, total, zs, zr, ps, pr, ws, wr, ls, *scratch):
        me = Layer(nb)
        u = me.u
        lin = u * nb + me.b
        part = lax.rem(me.b, rp)
        bar = pltpu.get_barrier_semaphore()

        @pl.loop(1, n)
        def _(i):
            t = lax.rem(lin + i, n)
            signal(bar, t // nb, lax.rem(t, nb))

        pl.semaphore_wait(bar, n - 1)

        def hop(way, o):
            to = u - 1 if way == 0 else u + 1
            return remote(tmp.at[way, o], land.at[way, o], zs.at[way, o], zr.at[way, o], to, me.b)

        def add(way, o):
            @pl.loop(0, count)
            def _(t):
                tmp[way, o, t] = (p_ref[o, t].astype(f32) + land[way, o, t].astype(f32)).astype(bf16)

        def ends(way, o):
            def run():
                tmp[way, o] = p_ref[o]
                hop(way, o).start()
            return run

        def passes(way, o):
            def run():
                hop(way, o).wait_recv()
                add(way, o)
                hop(way, o).start()
            return run

        def down(o):
            return u > o

        def up(o):
            return u < o

        ways = [(0, o) for o in range(nz - 1)], [(1, o) for o in range(nz - 1, 0, -1)]
        for pair in zip(*ways):
            for way, o in pair:
                pl.when(u == (0 if way else nz - 1))(ends(way, o))

        def relay(way, o):
            inner = (u > 0) & (u < nz - 1) & (up(o) if way else down(o))
            pl.when(inner)(passes(way, o))

        def block(t):
            rows_t = l_ref[pl.ds(pl.multiple_of(t * rows, rows), rows), :]
            return lax.dot_general(rows_t, r_ref[...], NT, preferred_element_type=f32)

        red = made(me, block, *scratch, waits=False)
        pairs = list(zip(*ways))
        for k, pair in enumerate(pairs):
            for way, o in pair:
                relay(way, o)
            if k == 0:
                for j in red.order[:-1]:
                    red.phase1(j)
            if k == len(pairs) - 2:
                red.phase2()

        def here(way):
            pl.when((u > 0) if way else (u < nz - 1))(
                lambda: remote(tmp.at[way, u], land.at[way, u], zs.at[way, u], zr.at[way, u], u, me.sib).wait_recv())

        here(0)
        here(1)

        @pl.loop(0, count)
        def _(t):
            tile = p_ref[u, t].astype(f32)
            tile = tile + jnp.where(u < nz - 1, land[0, u, t].astype(f32), 0.0)
            total[t] = (tile + jnp.where(u > 0, land[1, u, t].astype(f32), 0.0)).astype(bf16)

        out = []
        for i in range(1, nb):
            t = lax.rem(me.b + i, nb)
            c = remote(total.at[t], pin.at[me.b], ps.at[i], pr.at[i], u, t)
            c.start()
            out.append(c)
        own = pltpu.make_async_copy(total.at[me.b], pin.at[me.b], ls.at[0])
        own.start()

        def weight(p):
            t = (me.b // rp) * n_o + u * rp + p
            src = total.at[pl.ds(nb + p * wide, wide)]
            return t, remote(src, win.at[part], ws.at[p], wr.at[part], t // nb, lax.rem(t, nb))

        stay = lambda p: pltpu.make_async_copy(total.at[pl.ds(nb + p * wide, wide)], win.at[part], ls.at[1])
        for p in range(rp):
            t, c = weight(p)
            pl.when(t != lin)(c.start)
            pl.when(t == lin)(stay(p).start)
        red.end(write_to(o_ref))
        red.sent()
        for way, o in ways[0] + ways[1]:
            pl.when(up(o) if way else down(o))(lambda way=way, o=o: hop(way, o).wait_send())
        for c in out:
            c.wait()
        own.wait()
        for p in range(rp):
            t, c = weight(p)
            pl.when(t != lin)(c.wait_send)
            pl.when(t == lin)(stay(p).wait)
        hg = lin // n_o
        layer = lax.rem(lin, n_o) // rp
        for p in range(rp):
            c = remote(total.at[pl.ds(nb, wide)], win.at[p], ws.at[0], wr.at[p], u, me.sib)
            pl.when(layer * nb + hg * rp + p != lin)(c.wait_recv)

    sh = jax.ShapeDtypeStruct
    return pl.pallas_call(
        kernel,
        out_shape=(
            sh((rows, cols), f32), sh((nb, shard, width), bf16), sh((rp, wide, shard, width), bf16),
        ),
        in_specs=[VMEM, VMEM, VMEM],
        out_specs=(VMEM, ANY, ANY),
        scratch_shapes=[pltpu.VMEM((2, nz, count, shard, width), bf16)] * 2
        + [pltpu.VMEM((count, shard, width), bf16)]
        + [DMA((2, nz))] * 2
        + [DMA((nb,))] * 2
        + [DMA((rp,))] * 2
        + [DMA((2,))]
        + made_scratch(nb, rows, cols),
        compiler_params=pltpu.CompilerParams(
            collective_id=cid, has_side_effects=True, vmem_limit_bytes=56 * MIB
        ),
        cost_estimate=NO_COST,
        name="reduce_last",
    )(lhs, rhs, pieces)


def turn(a, c, s1, s2):
    return a * c + pltpu.roll(a, LANES - HW // 2, 1) * s1 + pltpu.roll(a, HW // 2, 1) * s2


def turn_back(a, c, s1, s2):
    return a * c - pltpu.roll(a, LANES - HW // 2, 1) * s1 - pltpu.roll(a, HW // 2, 1) * s2


def swap(a):
    return pltpu.roll(a, HW, 1)


def low_half():
    return lax.broadcasted_iota(jnp.int32, (1, LANES), 1) < HW


def row_block(step, width):
    return pl.BlockSpec((step, width), lambda i: (i, 0))


def whole_block(a):
    zeros = (0,) * a.ndim
    return pl.BlockSpec(a.shape, lambda i: zeros)


def prepare(w_query, w_key, w_value, extra, gains, w_inner, w_outer, cotangent, routes):
    S = w_query.shape[0]
    T = routes.shape[0]
    dz = w_inner.shape[1]
    W = 3 * FF
    half = W // 2

    def kernel(q_ref, k_ref, v_ref, x_ref, n_ref, i_ref, o_ref, c_ref, r_ref, p_ref, g_ref, a_ref, b_ref, f_ref):
        low = low_half()
        lane = lax.broadcasted_iota(jnp.int32, (1, LANES), 1)

        def low64(ref, at):
            a = ref[:, at // LANES * LANES:at // LANES * LANES + LANES].astype(f32)
            return swap(a) if at % LANES else a

        spread = lax.broadcasted_iota(jnp.int32, (S, S), 0) == lax.broadcasted_iota(jnp.int32, (S, S), 1)
        tail = x_ref[...].astype(f32)
        for i in range(2):
            column = jnp.sum(jnp.where(spread, n_ref[i:i + 1, :], 0.0), axis=1, keepdims=True)
            tail = jnp.where(lane == r_first + i, column, tail)
        for h in range(KV):
            at = h * QCOLS
            two = lambda a, b: jnp.where(low, a, swap(b)).astype(bf16)
            p_ref[h, :, :LANES] = two(low64(q_ref, at), low64(q_ref, at + HW))
            p_ref[h, :, LANES:2 * LANES] = two(low64(q_ref, at + 2 * HW), low64(k_ref, h * HW))
            p_ref[h, :, 2 * LANES:] = jnp.where(low, low64(v_ref, h * HW), tail).astype(bf16)
        g_ref[:, :D] = c_ref[...]
        named = r_ref[:, 0:1] + HW == lane
        for j in range(1, TOPK):
            named = named | (r_ref[:, j:j + 1] + HW == lane)
        g_ref[:, D:] = jnp.where(named, 1.0, 0.0).astype(bf16)
        odd = lax.rem(lax.axis_index("ulysses"), 2)
        same, outer = i_ref[odd], o_ref[odd].astype(f32).T.astype(bf16)
        a_ref[...] = same[:, :half]
        b_ref[:, :2 * FF - half] = same[:, half:]
        b_ref[:, 2 * FF - half:] = outer
        f_ref[:, :2 * FF] = i_ref[1 - odd]
        f_ref[:, 2 * FF:] = o_ref[1 - odd].astype(f32).T.astype(bf16)

    r_first = extra[1]
    sh = lambda *shape: jax.ShapeDtypeStruct(shape, bf16)
    return pl.pallas_call(
        kernel,
        out_shape=(sh(KV, S, AUX), sh(T, D + LANES), sh(dz, half), sh(dz, half), sh(dz, W)),
        in_specs=[VMEM] * 9,
        out_specs=(VMEM,) * 5,
        compiler_params=pltpu.CompilerParams(vmem_limit_bytes=48 * MIB),
        cost_estimate=NO_COST,
        name="prepare",
    )(w_query, w_key, w_value, extra[0], gains, w_inner, w_outer, cotangent, routes)


def project(x, gain, packed, c, s1, s2):
    R = x.shape[0]
    step = 256

    def kernel(x_ref, g_ref, w_ref, c_ref, a_ref, b_ref, q_ref, kv_ref, h_ref):
        v = x_ref[...].astype(f32)
        inv = lax.rsqrt(jnp.mean(v * v, axis=1, keepdims=True) + EPS)
        h = (v * inv * g_ref[...]).astype(bf16)
        h_ref[...] = h
        out = jnp.dot(h, w_ref[...], preferred_element_type=f32)
        tables = (c_ref[...], a_ref[...], b_ref[...])
        low = low_half()
        t0 = turn(out[:, :LANES], *tables)
        t1 = turn(out[:, LANES:2 * LANES], *tables)
        scale = lambda a: (jnp.where(low, a, 0.0) * (1.0 / math.sqrt(HW))).astype(bf16)
        q_ref[0] = scale(t0)
        q_ref[1] = scale(swap(t0))
        q_ref[2] = scale(t1)
        kv_ref[...] = jnp.where(low, swap(t1), swap(out[:, 2 * LANES:])).astype(bf16)

    sh = jax.ShapeDtypeStruct
    return pl.pallas_call(
        kernel,
        grid=(R // step,),
        out_shape=(sh((GROUP, R, LANES), bf16), sh((R, LANES), bf16), sh((R, D), bf16)),
        in_specs=[row_block(step, D), whole_block(gain), whole_block(packed)] + [row_block(step, LANES)] * 3,
        out_specs=(
            pl.BlockSpec((GROUP, step, LANES), lambda i: (0, i, 0)),
            row_block(step, LANES),
            row_block(step, D),
        ),
        compiler_params=pltpu.CompilerParams(vmem_limit_bytes=32 * MIB),
        cost_estimate=NO_COST,
        name="project",
    )(x, gain, packed, c, s1, s2)


BQ = 256
BK = 512
NT = (((1,), (1,)), ((), ()))
NN = (((1,), (0,)), ((), ()))
TN = (((0,), (0,)), ((), ()))


def mm(a, b, dims=NN):
    return lax.dot_general(a, b, dims, preferred_element_type=f32)


def seen(meta, st, i, kb, nq):
    qpos = meta[nq] + i * BQ + lax.broadcasted_iota(jnp.int32, (BQ, 1), 0)
    kpos = kb * BK + lax.broadcasted_iota(jnp.int32, (1, BK), 1)
    return ((kpos <= qpos) & (kpos >= st))[None]


def attend(q, kv, starts, meta):
    _, Rq, _ = q.shape
    nq = Rq // BQ
    M = GROUP * BQ

    def kernel(meta, q_ref, kv_ref, st_ref, o_ref, l_ref):
        i = pl.program_id(0)
        qv = q_ref[...].reshape(M, LANES)
        st = st_ref[...]
        last = (meta[nq] + i * BQ + BQ - 1) // BK + 1

        def step(kb, carry):
            m, l, acc = carry
            keys = kv_ref[pl.ds(pl.multiple_of(kb * BK, BK), BK), :]
            s = mm(qv, keys, NT).reshape(GROUP, BQ, BK)
            s = jnp.where(seen(meta, st, i, kb, nq), s, NEG)
            m2 = jnp.maximum(m, jnp.max(s, axis=2, keepdims=True))
            w = jnp.exp(s - m2)
            f = jnp.exp(m - m2)
            l = l * f + jnp.sum(w, axis=2, keepdims=True)
            pv = mm(w.astype(bf16).reshape(M, BK), keys)
            return m2, l, acc * f + pv.reshape(GROUP, BQ, LANES)

        init = (
            jnp.full((GROUP, BQ, 1), NEG, f32),
            jnp.zeros((GROUP, BQ, 1), f32),
            jnp.zeros((GROUP, BQ, LANES), f32),
        )
        m, l, acc = lax.fori_loop(meta[i], last, step, init)
        o = acc / l
        o_ref[:, :LANES] = jnp.where(low_half(), swap(o[0]), o[1]).astype(bf16)
        o_ref[:, LANES:] = swap(o[2])[:, :HW].astype(bf16)
        l_ref[...] = m + jnp.log(l)

    sh = jax.ShapeDtypeStruct
    blk = lambda w: pl.BlockSpec((GROUP, BQ, w), lambda i, m: (0, i, 0))
    return pl.pallas_call(
        kernel,
        grid_spec=pltpu.PrefetchScalarGridSpec(
            num_scalar_prefetch=1,
            grid=(nq,),
            in_specs=[
                blk(LANES),
                pl.BlockSpec(kv.shape, lambda i, m: (0, 0)),
                pl.BlockSpec((BQ, 1), lambda i, m: (i, 0)),
            ],
            out_specs=(pl.BlockSpec((BQ, QCOLS), lambda i, m: (i, 0)), blk(1)),
        ),
        out_shape=(sh((Rq, QCOLS), bf16), sh((GROUP, Rq, 1), f32)),
        compiler_params=pltpu.CompilerParams(vmem_limit_bytes=48 * MIB),
        cost_estimate=NO_COST,
        name="attend",
    )(meta, q, kv, starts)


def attend_back(q, kv, starts, meta, lse, mixed, dattn, wo):
    _, Rq, _ = q.shape
    nq = Rq // BQ
    M = GROUP * BQ
    K = kv.shape[0]

    def kernel(meta, q_ref, kv_ref, st_ref, l_ref, o_ref, g_ref, w_ref, dq_ref, dkv_ref, dw_ref):
        i = pl.program_id(0)

        @pl.when(i == 0)
        def _():
            dkv_ref[...] = jnp.zeros_like(dkv_ref)
            dw_ref[...] = jnp.zeros_like(dw_ref)

        g = g_ref[...]
        mixed = o_ref[...]
        dm = mm(g, w_ref[...], NT).astype(bf16).astype(f32)
        dw_ref[...] += mm(mixed, g, TN)
        low = low_half()
        d0 = dm[:, :LANES]
        d1 = jnp.concatenate([dm[:, LANES:], jnp.zeros((BQ, LANES - HW), f32)], axis=1)
        m0 = mixed[:, :LANES].astype(f32)
        m1 = jnp.concatenate([mixed[:, LANES:].astype(f32), jnp.zeros((BQ, LANES - HW), f32)], axis=1)
        total = lambda a: jnp.sum(a, axis=1, keepdims=True)
        e0, e1 = d0 * m0, d1 * m1
        first = total(jnp.where(low, e0, 0.0))
        delta = jnp.stack([first, total(jnp.where(low, 0.0, e0)), total(e1)])
        high = lambda a: jnp.where(low, 0.0, a).astype(bf16)
        do = jnp.concatenate([high(swap(d0)), high(d0), high(swap(d1))], axis=0)
        qv = q_ref[...].reshape(M, LANES)
        lse = l_ref[...]
        st = st_ref[...]
        last = (meta[nq] + i * BQ + BQ - 1) // BK + 1

        def step(kb, dq):
            at = pl.ds(pl.multiple_of(kb * BK, BK), BK)
            keys = kv_ref[at, :]
            s = mm(qv, keys, NT).reshape(GROUP, BQ, BK)
            p = jnp.where(seen(meta, st, i, kb, nq), jnp.exp(s - lse), 0.0)
            dp = mm(do, keys, NT).reshape(GROUP, BQ, BK)
            ds = (p * (dp - delta)).astype(bf16).reshape(M, BK)
            pb = p.astype(bf16).reshape(M, BK)
            dkv_ref[at, :] += mm(ds, qv, TN) + mm(pb, do, TN)
            return dq + mm(ds, keys)

        dq = lax.fori_loop(meta[i], last, step, jnp.zeros((M, LANES), f32))
        dq_ref[...] = (dq * (1.0 / math.sqrt(HW))).astype(bf16).reshape(GROUP, BQ, LANES)

    sh = jax.ShapeDtypeStruct
    blk = lambda w: pl.BlockSpec((GROUP, BQ, w), lambda i, m: (0, i, 0))
    rows = lambda w: pl.BlockSpec((BQ, w), lambda i, m: (i, 0))
    full = lambda *shape: pl.BlockSpec(shape, lambda i, m: (0, 0))
    return pl.pallas_call(
        kernel,
        grid_spec=pltpu.PrefetchScalarGridSpec(
            num_scalar_prefetch=1,
            grid=(nq,),
            in_specs=[
                blk(LANES), full(*kv.shape), rows(1), blk(1), rows(QCOLS), rows(D), full(QCOLS, D),
            ],
            out_specs=(blk(LANES), full(K, LANES), full(QCOLS, D)),
        ),
        out_shape=(sh((GROUP, Rq, LANES), bf16), sh((K, LANES), f32), sh((QCOLS, D), f32)),
        compiler_params=pltpu.CompilerParams(vmem_limit_bytes=48 * MIB),
        cost_estimate=NO_COST,
        name="attend_back",
    )(meta, q, kv, starts, lse, mixed, dattn, wo)


def weight_grads(dq, dkv, kin, ok, tables, h1, packed, tail):
    _, Rq, _ = dq.shape
    step = 256
    arrivals = kin.shape[0]

    def kernel(ok_ref, dq_ref, dkv_ref, kin_ref, c_ref, a_ref, b_ref, h_ref, w_ref, t_ref, o_ref, p_ref, acc):
        i = pl.program_id(0)

        @pl.when(i == 0)
        def _():
            acc[...] = jnp.zeros_like(acc)

        kv = dkv_ref[...]
        for k in range(arrivals):
            kv = kv + jnp.where(ok_ref[k] > 0, kin_ref[k].astype(f32), 0.0)
        kv = kv.astype(bf16).astype(f32)
        low = low_half()
        tables = (c_ref[...], a_ref[...], b_ref[...])
        q = [dq_ref[h].astype(f32) for h in range(GROUP)]
        kv = swap(kv)
        t0 = turn_back(jnp.where(low, q[0], swap(q[1])), *tables)
        t1 = turn_back(jnp.where(low, q[2], kv), *tables)
        out = jnp.concatenate([t0, t1, jnp.where(low, kv, 0.0)], axis=1).astype(bf16)
        o_ref[...] = out
        acc[...] += mm(h_ref[...], out, TN)

        @pl.when(i == Rq // step - 1)
        def _():
            w = w_ref[...].astype(f32)
            dw = acc[...]
            t = t_ref[...]
            lane = lax.broadcasted_iota(jnp.int32, (1, LANES), 1)
            gain = jnp.sum(jnp.where(lane == ok_ref[arrivals], w[:, 2 * LANES:], 0.0), axis=1, keepdims=True)
            d_gain = jnp.sum(w * dw, axis=1, keepdims=True) / gain
            t = t + jnp.where(lane == ok_ref[arrivals] + 1, d_gain, 0.0)
            p_ref[:, :2 * LANES] = dw[:, :2 * LANES].astype(bf16)
            p_ref[:, 2 * LANES:] = jnp.where(low, dw[:, 2 * LANES:], t).astype(bf16)

    sh = jax.ShapeDtypeStruct
    heads = lambda n: pl.BlockSpec((n, step, LANES), lambda i: (0, i, 0))
    return pl.pallas_call(
        kernel,
        grid=(Rq // step,),
        out_shape=(sh((Rq, AUX), bf16), sh((D, AUX), bf16)),
        in_specs=[pl.BlockSpec(memory_space=pltpu.SMEM), heads(GROUP), row_block(step, LANES), heads(arrivals)]
        + [row_block(step, LANES)] * 3
        + [row_block(step, D), whole_block(packed), whole_block(tail)],
        out_specs=(row_block(step, AUX), pl.BlockSpec((D, AUX), lambda i: (0, 0))),
        scratch_shapes=[pltpu.VMEM((D, AUX), f32)],
        compiler_params=pltpu.CompilerParams(vmem_limit_bytes=48 * MIB),
        cost_estimate=NO_COST,
        name="weight_grads",
    )(ok, dq, dkv, kin, *tables, h1, packed, tail)


def experts(h2_own, g_own, g_oth, router, hot, weights, sent, leave, nz, nb, cid):
    T = h2_own.shape[0]
    nc = nb // 2
    step = 2 * T
    units = 2 * nc
    dz = D // nz
    C = D + LANES
    W = 3 * FF
    nw = len(weights)
    ng = len(leave)
    resident = nb <= 8

    def kernel(x_ref, g0_ref, g1_ref, r_ref, e_ref, *rest):
        win = rest[:nw]
        y_ref, s_ref = rest[nw:nw + 2]
        rest = rest[nw + 2:]
        din, gin = rest[:ng], rest[ng]
        rest = rest[ng + 1:]
        h_all, hbuf, part, gbuf, ybuf, wc, acc, zbuf, gs, zs, sem, gsem, ysem, *pair = rest
        me = Layer(nb)
        me.enter(sorted({1, sent[0]}))
        own, oth = h_all.at[0], h_all.at[1]
        mate = remote(x_ref, oth.at[me.b], zs.at[0], zs.at[1], me.across(1), me.b)
        mate.start()
        ga = Gather(me, x_ref, own, gs.at[0])
        gb = Gather(me, oth.at[me.b], oth, gs.at[1])
        ga.start()
        mine = pltpu.make_async_copy(x_ref, own.at[me.b], zs.at[2])
        mine.start()
        rows_at = lambda d: pl.ds(pl.multiple_of(me.across(d) * dz, dz), dz)
        loads = [
            pltpu.make_async_copy(win[k], wc.at[rows_at(d), pl.ds(c, a.shape[1])], sem.at[k])
            for k, (a, d, c) in enumerate(weights)
        ]
        for c in loads:
            c.start()

        def place(u):
            other = (u >= 2) & (u < nc + 2)
            j = jnp.where(u < 2, u, jnp.where(other, u - 2, 2 * nc + 1 - u))
            return jnp.where(other, 1, 0), j

        def cot(u, h):
            _, j = place(u)
            rows = pl.ds(pl.multiple_of(me.unit(j) * step, step), step)
            slot = lax.rem(u, 2)
            return pltpu.make_async_copy((g1_ref if h else g0_ref).at[rows], gbuf.at[slot], gsem.at[slot])

        def cot_start(u):
            h, _ = place(u)
            pl.when(h == 0)(lambda: cot(u, 0).start())
            pl.when(h == 1)(lambda: cot(u, 1).start())

        def result(u):
            h, j = place(u)
            slot = lax.rem(u, 2)
            return pltpu.make_async_copy(
                ybuf.at[slot], y_ref.at[h, pl.ds(pl.multiple_of(me.unit(j) * 2, 2), 2)], ysem.at[slot])

        cot_start(jnp.int32(0))
        acc[...] = jnp.zeros_like(acc)
        ra, rb = pair_of(me, part, *pair)
        back = remote(zbuf.at[0], zbuf.at[1], zs.at[3], zs.at[4], me.across(1), me.b)
        ga.relay1()
        for c in loads:
            c.wait()
        mine.wait()

        def at(k, f):
            def run(u):
                pl.when(u == k)(f)
            return run

        def arrive(u):
            def first():
                ga.relay2()
                mate.wait_recv()
                gb.start()

            def second():
                ga.relay3()
                gb.relay1()

            at(1, first)(u)
            at(2, second)(u)
            at(3, gb.relay2)(u)
            at(4, gb.relay3)(u)
            for k in range(units):
                h = 1 if 2 <= k < nc + 2 else 0
                j = k if k < 2 else (k - 2 if h else 2 * nc + 1 - k)
                at(k, lambda h=h, j=j: (gb if h else ga).passed(j))(u)

        def depart(u):
            for k in range(units):
                h = 1 if 2 <= k < nc + 2 else 0
                j = k if k < 2 else (k - 2 if h else 2 * nc + 1 - k)
                at(k, lambda h=h, j=j: (rb if h else ra).start(j))(u)

            def mates():
                for j in rb.order[:-1]:
                    rb.phase1(j)

            at(nc + 1, mates)(u)

            def ours():
                rb.phase2()
                ra.phase1(3)
                ra.phase1(1)

            if nc == 4:
                at(nc + 2, ours)(u)

            def across():
                rb.end(write_to(zbuf, 0))
                back.start()

            at(units - 1, across)(u)

        @pl.loop(0, units)
        def _(u):
            h, j = place(u)
            slot = lax.rem(u, 2)
            pl.when(u + 1 < units)(lambda: cot_start(u + 1))
            arrive(u)
            cot(u, 0).wait()
            pl.when(u >= 2)(lambda: result(u - 2).wait())
            two = pl.ds(pl.multiple_of(me.unit(j) * 2, 2), 2)
            if resident:
                x = h_all[h, two].reshape(step, D)
            else:
                c = pltpu.make_async_copy(h_all.at[h, two], hbuf, zs.at[5])
                c.start()
                c.wait()
                x = hbuf[...].reshape(step, D)
            hot = e_ref[...]
            mask = gbuf[slot, :, D:].astype(f32) > 0
            logits = mm(x, r_ref[...])
            top = jnp.max(jnp.where(mask, logits, NEG), axis=1, keepdims=True)
            w = jnp.where(mask, jnp.exp(jnp.where(mask, logits - top, 0.0)), 0.0)
            gate = jnp.sum(w * hot, axis=1, keepdims=True) / jnp.sum(w, axis=1, keepdims=True)
            gu = mm(x, wc[:, :2 * FF])
            a, up = gu[:, :FF], gu[:, FF:]
            sg = jax.nn.sigmoid(a)
            silu = a * sg
            act = (silu * up).astype(bf16)
            g = gbuf[slot, :, :D]
            ybuf[slot] = (gate * mm(act, wc[:, 2 * FF:], NT)).astype(bf16).reshape(2, T, D)
            result(u).start()
            raw = mm(g, wc[:, 2 * FF:])
            acc[:, 2 * FF:] += mm((gate * g.astype(f32)).astype(bf16), act, TN)
            dgate = jnp.sum(act.astype(f32) * raw, axis=1, keepdims=True)
            dact = gate * raw
            dgu = jnp.concatenate(
                [dact * up * (sg * (1.0 + a * (1.0 - sg))), dact * silu], axis=1).astype(bf16)
            acc[:, :2 * FF] += mm(x, dgu, TN)
            part[h, two, :, :D] = mm(dgu, wc[:, :2 * FF], NT).astype(bf16).reshape(2, T, D)
            hi = dgate.astype(bf16).astype(f32)
            part[h, two, :, D:] = (hi * hot + swap((dgate - hi) * hot)).astype(bf16).reshape(2, T, LANES)
            depart(u)

        for j in (2,) if nc == 4 else ra.order[:-1]:
            ra.phase1(j)
        wc[...] = acc[...].astype(bf16)
        grad = lambda d, c, width: wc.at[rows_at(d), pl.ds(c, width)]
        going = remote(grad(*sent), gin, zs.at[6], zs.at[7], me.across(sent[0]), me.b)
        going.start()
        saves = [pltpu.make_async_copy(grad(*p), din[k], sem.at[k]) for k, p in enumerate(leave)]
        for c in saves:
            c.start()
        ra.phase2()
        back.wait_recv()
        ra.end(add_to(s_ref, zbuf, 1))
        back.wait_send()
        mate.wait_send()
        for r in (ga, gb, ra, rb):
            r.sent()
        for c in saves:
            c.wait()
        going.wait()
        result(jnp.int32(units - 2)).wait()
        result(jnp.int32(units - 1)).wait()

    sh = jax.ShapeDtypeStruct
    v = lambda shape, kind=bf16: pltpu.VMEM(shape, kind)
    return pl.pallas_call(
        kernel,
        out_shape=(sh((2, nb, T, D), bf16), sh((T, C), f32))
        + tuple(sh((dz, width), bf16) for _, _, width in leave)
        + (sh((dz, sent[2]), bf16),)
        + (() if resident else (sh((2, nb, T, D), bf16),)),
        in_specs=[ANY] * 3 + [VMEM] * 2 + [ANY] * nw,
        out_specs=(ANY, VMEM) + (ANY,) * (ng + 1 + int(not resident)),
        scratch_shapes=([v((2, nb, T, D))] if resident else [])
        + [
            v((2, T, D)), v((2, nb, T, C)), v((2, step, C)), v((2, 2, T, D)),
            v((D, W)), v((D, W), f32), v((2, T, C)),
            Gather.scratch(nb, 2), DMA((8,)), DMA((max(nw, ng),)), DMA((2,)), DMA((2,)),
        ]
        + Reduce.scratch(nb, T, C, 2),
        compiler_params=pltpu.CompilerParams(
            collective_id=cid, has_side_effects=True, vmem_limit_bytes=60 * MIB
        ),
        cost_estimate=NO_COST,
        name="experts",
    )(h2_own, g_own, g_oth, router, hot, *[a for a, _, _ in weights])


def finish(dh1, x, gain, dresid, pin, win, resid, ysum, yfar, grads, places):
    T = x.shape[0]
    groups, rp, S, _ = pin.shape
    senders = win.shape[0]
    m = len(grads)
    dz = grads[0].shape[0]

    def kernel(d_ref, x_ref, g_ref, r_ref, p_ref, w_ref, s_ref, y_ref, f_ref, *rest):
        srcs = rest[:m]
        t_ref, q_ref, k_ref, v_ref, m_ref, o_ref, out_ref, in_ref, ex_ref = rest[m:]
        odd = lax.rem(lax.axis_index("ulysses"), 2)
        for e in range(2):
            at = odd if e == 0 else 1 - odd
            for c in range(0, 3 * FF, FF // 2):
                total = 0.0
                for r, (d, lo, width) in zip(srcs, places):
                    if d % 2 == e and lo <= c < lo + width:
                        total = total + r[:, c - lo:c - lo + FF // 2].astype(f32)
                if c < 2 * FF:
                    in_ref[at, :, c:c + FF // 2] = total
                else:
                    ex_ref[at, c - 2 * FF:c - 2 * FF + FF // 2, :] = total.T
        v = x_ref[...].astype(f32)
        inv = lax.rsqrt(jnp.mean(v * v, axis=1, keepdims=True) + EPS)
        n = v * inv
        w = d_ref[...] * g_ref[...]
        t_ref[...] = r_ref[...] + inv * (w - n * jnp.mean(w * n, axis=1, keepdims=True))
        out_ref[...] = s_ref[...] + y_ref[...] + f_ref[...].astype(f32)
        for k in range(D // AUX):
            parts = [w_ref[p, k].astype(f32) for p in range(senders)]
            o_ref[:, k * AUX:(k + 1) * AUX] = functools.reduce(lambda a, b: a + b, parts)
        small = 0.0
        for h in range(groups):
            row = 0.0
            for p in range(rp):
                row = row + p_ref[h, p].astype(f32)
            q_ref[:, h * QCOLS:(h + 1) * QCOLS] = row[:, :QCOLS]
            k_ref[:, h * HW:(h + 1) * HW] = row[:, QCOLS:QCOLS + HW]
            v_ref[:, h * HW:(h + 1) * HW] = row[:, QCOLS + HW:ROUTER_AT]
            small = small + row[:, 2 * LANES:]
        m_ref[...] = small

    sh = lambda *shape: jax.ShapeDtypeStruct(shape, f32)
    return pl.pallas_call(
        kernel,
        out_shape=(sh(T, D), sh(S, HEADS * HW), sh(S, KV * HW), sh(S, KV * HW), sh(S, LANES), sh(S, D), sh(T, D),
                   sh(2, dz, 2 * FF), sh(2, FF, dz)),
        in_specs=[VMEM] * (9 + m),
        out_specs=(VMEM,) * 9,
        compiler_params=pltpu.CompilerParams(vmem_limit_bytes=60 * MIB),
        cost_estimate=NO_COST,
        name="finish",
    )(dh1, x, gain, dresid, pin, win, resid, ysum, yfar, *grads)


def locate(rows, lengths):
    passed = rows[:, None] >= jnp.cumsum(lengths)
    return jnp.sum(jnp.where(passed, lengths, 0), axis=-1)


def norm_rows(v, gain):
    inverse = lax.rsqrt(jnp.mean(v * v, axis=-1, keepdims=True) + EPS)
    normed = v * inverse
    return normed, inverse, normed * gain


def norm_back(upstream, normed, inverse, gain):
    d_normed = upstream * gain
    d_gain = jnp.sum(upstream * normed, axis=0)
    d_values = inverse * (d_normed - normed * jnp.mean(d_normed * normed, axis=-1, keepdims=True))
    return d_values, d_gain


def rows_of(a, start, count):
    return a if a.shape[0] == count else lax.dynamic_slice_in_dim(a, start, count, 0)


def widen(a, start, count):
    if a.shape[0] == count:
        return a
    return lax.dynamic_update_slice_in_dim(jnp.zeros((count,) + a.shape[1:], a.dtype), a, start, 0)


def on_device(tokens, lengths, routes, gain_attn, w_query, w_key, w_value, w_output, gain_moe,
              w_router, w_inner, w_outer, cotangent):
    nz = lax.axis_size("ulysses")
    nb = lax.axis_size("blk")
    z = lax.axis_index("ulysses")
    b = lax.axis_index("blk")
    T = tokens.shape[0]
    R = nb * T
    rp = nb // KV
    Rq = R // rp
    part = b % rp
    at = part * Rq
    n = nz * nb
    S = D // n
    E = w_router.shape[1]
    longest = min(LENMAX, n * T // 2)
    back = min(nz - 1, (longest - 1 + R - 1) // R)
    n_o = QCOLS // S
    odd = z % 2

    lanes = jnp.arange(LANES, dtype=jnp.int32)
    extra = (jnp.pad(w_router, ((0, 0), (HW, LANES - HW - E))), HW + E)
    gains = jnp.stack([gain_attn, gain_moe]).astype(f32)
    pieces, cot_mask, same_a, same_b, other = prepare(
        w_query, w_key, w_value, extra, gains, w_inner, w_outer, cotangent, routes)
    W = 3 * FF
    half = W // 2
    early = min(2, nz - 1)
    xg, packed, wo, g_own, g_far, first = gather_inputs(
        tokens, pieces, w_output, cot_mask, same_a if early % 2 == 0 else other[:, :half], early, nz, nb, 0)
    xg = xg.reshape(R, D)
    packed = packed.reshape(D, AUX)
    router = packed[:, 2 * LANES:]
    gains = packed[:, ROUTER_AT + E:ROUTER_AT + E + 2].astype(f32).T
    gain1, gain2 = gains[0:1], gains[1:2]

    flip = lambda d: [(k, k ^ d) for k in range(nz)]
    give = lambda w, d: lax.ppermute(w, "ulysses", flip(d))
    named = jnp.any(routes[:, :, None] + HW == lanes[None, None, :], axis=1)
    second, packed = lax.optimization_barrier((same_b if early % 2 == 0 else other[:, half:], packed))
    second = give(second, early)
    weights = [(same_a, 0, 0), (same_b, 0, half), (first, early, 0)]

    rows = z * R + jnp.arange(R, dtype=jnp.int32)
    opening = locate(rows, lengths)
    pair = lanes % HW
    frequency = THETA ** (-((pair % (HW // 2)).astype(f32) * 2.0 / HW))
    angles = (rows - opening).astype(f32)[:, None] * frequency[None, :]
    cos, sin = jnp.cos(angles), jnp.sin(angles)
    tables = (cos, jnp.where(pair < HW // 2, -sin, 0.0), jnp.where(pair < HW // 2, 0.0, sin))

    q, kv, h1 = project(xg, gain1, packed, *tables)
    if rp > 1:
        q = lax.dynamic_slice_in_dim(q, at, Rq, 1)
    kv, second = lax.optimization_barrier((kv, second))
    weights.append((second, early, half))
    far, g_oth = halo_forward(kv, g_far, nz, nb, back, 1)
    g_own, g_oth = g_own.reshape(R, D + LANES), g_oth.reshape(R, D + LANES)
    wo = wo.reshape(QCOLS, D)
    same_a, same_b, other, far = lax.optimization_barrier((same_a, same_b, other, far))
    for d in range(1, nz):
        if d % 2 and d != early:
            weights.append((give(other, d), d, 0))
        elif d != early:
            weights += [(give(same_a, d), d, 0), (give(same_b, d), d, half)]
    kv_all = jnp.concatenate([far[d - 1] for d in range(back, 0, -1)] + [kv], axis=0)
    base = (z - back) * R
    starts = rows_of(opening, at, Rq) - base
    meta = jnp.concatenate([starts[::BQ] // BK, (back * R + at)[None]]).astype(jnp.int32)
    starts = starts[:, None]
    mixed, lse = attend(q, kv_all, starts, meta)
    attn = reduce_product(widen(mixed, at, R), wo, nb, 2)

    resid = tokens.astype(f32) + attn
    n2, inv2, scaled2 = norm_rows(resid, gain2)
    h2_own = scaled2.astype(bf16)
    hot = (lanes == HW + b * EXP_DEV + odd).astype(f32)[None, :]
    sent = (early, 0, half)
    leave = [(0, 0, W), (early, half, half), (nz - 1, 0, half), (nz - 1, half, half)]
    leave += [(d, 0, W) for d in range(1, nz - 1) if d != early]
    y, summed, *grads = experts(h2_own, g_own, g_oth, router, hot, weights, sent, leave, nz, nb, 3)
    grads, got = grads[:len(leave)], grads[len(leave)]

    upstream = cotangent.astype(f32)
    dgates = summed[:, D:] + jnp.roll(summed[:, D:], HW, 1)
    logits = mm(h2_own, router)
    top = jnp.max(jnp.where(named, logits, NEG), axis=1, keepdims=True)
    w = jnp.where(named, jnp.exp(jnp.where(named, logits - top, 0.0)), 0.0)
    gates = w / jnp.sum(w, axis=1, keepdims=True)
    dlogits = gates * (dgates - jnp.sum(gates * dgates, axis=1, keepdims=True))
    dlogits = dlogits.astype(bf16)
    dh2 = summed[:, :D] + mm(dlogits, router, NT)
    d_norm2, d_gain2 = norm_back(dh2, n2, inv2, gain2)
    dresid = upstream + d_norm2
    grads = [grads[0]] + [give(a, d) for a, (d, _, _) in zip(grads[1:], leave[1:])]
    dattn, ysum, yfar = middle(dresid.astype(bf16), y, nb, 5)
    dattn = dattn.reshape(R, D)
    tail = mm(h2_own, dlogits, TN) + jnp.where(lanes == HW + E, d_gain2[:, None], 0.0)

    dq, dkv, dwo = attend_back(q, kv_all, starts, meta, lse, mixed, rows_of(dattn, at, Rq), wo)
    dkv, *grads = lax.optimization_barrier((dkv, *grads))
    dkv = dkv.reshape(back + 1, R, LANES)
    dkv_out = jnp.stack([dkv[back - d] for d in range(back + 1)]).astype(bf16)
    kin, yfar = halo_back(dkv_out, yfar, nz, nb, rp, back, 6)
    ok = [(z + d < nz) if d else (part != p) for d in range(back + 1) for p in range(rp)]
    ok = jnp.stack([jnp.asarray(o).astype(jnp.int32) for o in ok] + [jnp.int32(HW + E)])
    if rp > 1:
        kin = lax.dynamic_slice_in_dim(kin, at, Rq, 1)
    turned, dw = weight_grads(
        dq, rows_of(dkv[back], at, Rq), kin, ok, [rows_of(t, at, Rq) for t in tables],
        rows_of(h1, at, Rq), packed, tail)
    wide = D // AUX
    dwo = dwo.astype(bf16).reshape(nz, rp, S, wide, AUX)
    dwo = jnp.transpose(dwo, (0, 1, 3, 2, 4)).reshape(nz, rp * wide, S, AUX)
    last = jnp.concatenate([dw.reshape(nz, nb, S, AUX), dwo], axis=1)
    dh1, pin, win = reduce_last(widen(turned, at, R), packed, last, nz, nb, rp, 7)
    d_tokens, d_query, d_key, d_value, small, d_output, out, d_inner, d_outer = finish(
        dh1, tokens, gain1, dresid, pin.reshape(KV, rp, S, AUX), win, resid, ysum, yfar,
        grads + [got], leave + [sent])
    return (
        out, d_tokens, small[:, HW + E + 1], d_query, d_key, d_value, d_output,
        small[:, HW + E], small[:, HW:HW + E], d_inner, d_outer,
    )


def solution(mesh):
    both = ("ulysses", "blk")
    rows = P(both, None)
    weights = (P(both), rows, rows, rows, rows, P(both), rows, P("blk", "ulysses", None), P("blk", None, "ulysses"))
    return jax.shard_map(
        on_device,
        mesh=mesh,
        in_specs=(rows, P(), rows) + weights + (rows,),
        out_specs=(rows, rows) + weights,
        check_vma=False,
    )
```

```python
import functools
import math

import jax
import jax.numpy as jnp
from jax import lax
from jax.experimental import pallas as pl
from jax.experimental.pallas import tpu as pltpu
from jax.sharding import PartitionSpec as P

D = 1536
HEADS = 24
KV = 8
HW = 64
GROUP = HEADS // KV
FF = 512
TOPK = 8
EXP_DEV = 2
LENMAX = 4096
EPS = 1e-05
THETA = 10000.0
NEG = -1e30
LANES = 128
AUX = 384
ROUTER_AT = 320
QCOLS = GROUP * HW

f32 = jnp.float32
bf16 = jnp.bfloat16
MESH = pl.DeviceIdType.MESH
ANY = pl.BlockSpec(memory_space=pl.ANY)
VMEM = pl.BlockSpec(memory_space=pltpu.VMEM)
DMA = pltpu.SemaphoreType.DMA
MIB = 1 << 20
NO_COST = pl.CostEstimate(flops=0, bytes_accessed=0, transcendentals=0)


def dev(u, b):
    return {"ulysses": u, "blk": b}


def remote(src, dst, ss, rs, u, b):
    return pltpu.make_async_remote_copy(
        src_ref=src, dst_ref=dst, send_sem=ss, recv_sem=rs,
        device_id=dev(u, b), device_id_type=MESH,
    )


def signal(sem, u, b):
    pl.semaphore_signal(sem, inc=1, device_id=dev(u, b), device_id_type=MESH)


class Layer:
    def __init__(self, nb):
        self.u = lax.axis_index("ulysses")
        self.b = lax.axis_index("blk")
        self.nb = nb
        self.nc = nb // 2
        self.chip = self.b // 2
        self.core = lax.rem(self.b, 2)
        self.sib = self.chip * 2 + 1 - self.core

    def peer(self, i):
        return lax.rem(self.chip + i, self.nc) * 2 + self.core

    def unit(self, j):
        if self.nc != 4:
            return lax.rem(self.chip + self.nc - j, self.nc)
        x, y = lax.rem(self.chip, 2), self.chip // 2
        jx, jy = j % 2, j // 2
        return x + jx - 2 * x * jx + 2 * (y + jy - 2 * y * jy)

    def far(self, j):
        return self.unit(j) * 2 + self.core

    def across(self, d):
        at = self.u
        for k in range(d.bit_length()):
            if (d >> k) & 1:
                at = at + (1 << k) - (2 << k) * lax.rem(self.u // (1 << k), 2)
        return at

    def enter(self, flips=()):
        bar = pltpu.get_barrier_semaphore()
        for i in range(1, self.nc):
            signal(bar, self.u, self.peer(i))
        signal(bar, self.u, self.sib)
        for d in flips:
            signal(bar, self.across(d), self.b)
        pl.semaphore_wait(bar, self.nc + len(flips))


class Gather:
    def __init__(self, me, src, dst, sems):
        self.me, self.src, self.dst, self.sems = me, src, dst, sems
        self.quad = me.nc == 4
        half = dst.shape[1] // 2
        self.a, self.b = pl.ds(0, half), pl.ds(half, half)

    @staticmethod
    def scratch(nb, *lead):
        return DMA(lead + (2, 10 if nb == 8 else nb))

    def copy(self, k):
        me, src, dst = self.me, self.src, self.dst
        send = lambda s, d, to: remote(s, d, self.sems.at[0, k], self.sems.at[1, k], me.u, to)
        same = lambda at, to: send(dst.at[at], dst.at[at], to)
        part = lambda at, rows, to: send(dst.at[at, rows], dst.at[at, rows], to)
        if self.quad:
            if k < 4:
                rows = self.b if k % 2 else self.a
                return send(src.at[rows], dst.at[me.b, rows], me.far(1 + k // 2))
            if k < 6:
                return part(me.far(k - 3), self.b if k == 5 else self.a, me.far(6 - k))
            if k == 6:
                return send(src, dst.at[me.b], me.sib)
            return same(me.far(k - 6), me.sib)
        if k < me.nc:
            return send(src, dst.at[me.b], me.peer(k))
        if k == me.nc:
            return send(src, dst.at[me.b], me.sib)
        return same(me.far(k - me.nc), me.sib)

    def start(self):
        if self.quad:
            for k in (0, 3, 1, 2, 6):
                self.copy(k).start()
        else:
            for k in range(1, self.me.nc + 1):
                self.copy(k).start()

    def relay1(self):
        if self.quad:
            self.copy(0).wait_recv()
            self.copy(4).start()
            self.copy(3).wait_recv()
            self.copy(5).start()

    def relay2(self):
        if self.quad:
            self.copy(1).wait_recv()
            self.copy(7).start()
            self.copy(2).wait_recv()
            self.copy(8).start()
        else:
            for k in range(1, self.me.nc):
                self.copy(k).wait_recv()
                self.copy(self.me.nc + k).start()

    def relay3(self):
        if self.quad:
            self.copy(4).wait_recv()
            self.copy(5).wait_recv()
            self.copy(9).start()

    def passed(self, j):
        self.copy((6 if self.quad else self.me.nc) + j).wait_recv()

    def sent(self):
        for k in range(10) if self.quad else range(1, 2 * self.me.nc):
            self.copy(k).wait_send()

    def rest(self):
        self.relay1()
        self.relay2()
        self.relay3()

    def finish(self):
        for j in range(self.me.nc):
            self.passed(j)
        self.sent()


class Reduce:
    def __init__(self, me, get, source, sib_in, snd, land, sems):
        self.me, self.get, self.source = me, get, source
        self.sib_in, self.snd, self.land, self.sems = sib_in, snd, land, sems
        self.quad = me.nc == 4
        self.rows = sib_in.shape[1]
        half = self.rows // 2
        self.a, self.b = pl.ds(0, half), pl.ds(half, half)
        self.order = (3, 1, 2, 0) if self.quad else (*range(1, me.nc), 0)

    @staticmethod
    def scratch(nb, rows, cols, *lead):
        nc = nb // 2
        shape = lead + ((6, rows // 2, cols) if nc == 4 else (nc, rows, cols))
        return [
            pltpu.VMEM(lead + (nc, rows, cols), bf16), pltpu.VMEM(shape, bf16), pltpu.VMEM(shape, bf16),
            DMA(lead + (2, 10 if nc == 4 else 2 * nc)),
        ]

    def copy(self, k):
        me = self.me
        ss, rs = self.sems.at[0, k], self.sems.at[1, k]
        if k < me.nc:
            return remote(self.source(k), self.sib_in.at[k], ss, rs, me.u, me.sib)
        k = k - me.nc
        to = me.far((1, 1, 2, 2, 2, 1)[k] if self.quad else k)
        return remote(self.snd.at[k], self.land.at[k], ss, rs, me.u, to)

    def start(self, j):
        self.copy(j).start()

    def part(self, j, rows):
        return self.get(j, rows) + self.sib_in[j, rows].astype(f32)

    def send(self, k, value):
        self.snd[k] = value.astype(bf16)
        self.copy(self.me.nc + k).start()

    def phase1(self, j):
        self.copy(j).wait_recv()
        if not self.quad:
            self.send(j, self.part(j, pl.ds(0, self.rows)))
            return
        if j != 2:
            self.send(0 if j == 1 else 1, self.part(j, self.a))
        if j != 1:
            self.send(2 if j == 2 else 3, self.part(j, self.b))

    def landed(self, k):
        self.copy(self.me.nc + k).wait_recv()
        return self.land[k].astype(f32)

    def phase2(self):
        if self.quad:
            self.send(4, self.part(2, self.a) + self.landed(1))
            self.send(5, self.part(1, self.b) + self.landed(3))

    def end(self, write):
        self.copy(0).wait_recv()
        if self.quad:
            write(self.a, self.part(0, self.a) + self.landed(0) + self.landed(4))
            write(self.b, self.part(0, self.b) + self.landed(2) + self.landed(5))
        else:
            total = self.part(0, pl.ds(0, self.rows))
            for j in range(1, self.me.nc):
                total = total + self.landed(j)
            write(pl.ds(0, self.rows), total)

    def sent(self):
        for k in range(10) if self.quad else (*range(self.me.nc + 1), *range(self.me.nc + 1, 2 * self.me.nc)):
            if self.quad or k != self.me.nc:
                self.copy(k).wait_send()


def made(me, block, mine, sib_out, sib_in, snd, land, sems, waits=True):
    red = Reduce(me, lambda j, rows: mine[j, rows], lambda j: sib_out.at[j], sib_in, snd, land, sems)
    for j in red.order:
        sib_out[j] = block(me.unit(j) * 2 + 1 - me.core).astype(bf16)
        red.start(j)
    for j in red.order:
        mine[j] = block(me.far(j))
        if j and waits:
            red.phase1(j)
    return red


def made_scratch(nb, rows, cols):
    nc = nb // 2
    return [pltpu.VMEM((nc, rows, cols), f32), pltpu.VMEM((nc, rows, cols), bf16)] + Reduce.scratch(nb, rows, cols)


def keep(me, src, dst, sem):
    c = pltpu.make_async_copy(src, dst.at[me.b], sem)
    c.start()
    return c


def gather_inputs(x, pieces, wo, gm, expert, swap_d, nz, nb, cid):
    groups, shard, _ = pieces.shape
    rp = nb // groups
    n_o = QCOLS // shard
    n = nz * nb

    def kernel(x_ref, p_ref, w_ref, g_ref, e_ref, xo, po, wo_out, go, gx, eo, gs, ps, pr, zs, zr, ws, wr, ls):
        me = Layer(nb)
        lin = me.u * nb + me.b
        u, b = me.u, me.b
        bar = pltpu.get_barrier_semaphore()

        @pl.loop(1, n)
        def _(i):
            t = lax.rem(lin + i, n)
            signal(bar, t // nb, lax.rem(t, nb))

        pl.semaphore_wait(bar, n - 1)

        def piece(i):
            tb = lax.rem(b + i, nb)
            return remote(p_ref.at[tb // rp], po.at[u, b], ps.at[i], pr.at[i], u, tb)

        for i in range(1, nb):
            piece(i).start()
        own = pltpu.make_async_copy(p_ref.at[b // rp], po.at[u, b], ls.at[0])
        own.start()
        g = Gather(me, x_ref, xo, gs.at[0])
        g.start()
        cot = Gather(me, g_ref, go, gs.at[1])
        for i in range(1, nb):
            piece(i).wait()
        own.wait()

        def up(k):
            o = u - k + 1
            return remote(po.at[o], po.at[o], zs.at[0, k], zr.at[0, k], u + 1, b)

        def down(k):
            o = u + k - 1
            return remote(po.at[o], po.at[o], zs.at[1, k], zr.at[1, k], u - 1, b)

        def here(way, k):
            remote(po.at[u], po.at[u], zs.at[way, k], zr.at[way, k], u, me.sib).wait_recv()

        def relay(k):
            if k > 1:
                pl.when(u >= k - 1)(lambda: here(0, k - 1))
                pl.when(u + k - 1 < nz)(lambda: here(1, k - 1))
            pl.when((u >= k - 1) & (u + 1 < nz))(lambda: up(k).start())
            pl.when((u + k - 1 < nz) & (u > 0))(lambda: down(k).start())

        relay(1)
        hg = lin // n_o
        slot = lax.rem(lin, n_o)

        def weight(zo, p):
            tz, tb = lax.rem(u + zo, nz), hg * rp + p
            return tb, remote(w_ref, wo_out.at[slot], ws.at[zo * rp + p], wr.at[slot], tz, tb)

        g.relay1()
        for k in range(2, nz):
            relay(k)
            if k == 2:
                g.relay2()
                cot.start()
        stay = pltpu.make_async_copy(w_ref, wo_out.at[slot], ls.at[1])
        for zo in range(nz):
            for p in range(rp):
                tb, c = weight(zo, p)
                if zo:
                    c.start()
                else:
                    pl.when(tb != b)(c.start)
                    pl.when(tb == b)(stay.start)
        mate = remote(g_ref, gx, ls.at[4], ls.at[5], me.across(1), b)
        mate.start()
        half = remote(e_ref, eo, ls.at[6], ls.at[7], me.across(swap_d), b)
        half.start()
        xk = keep(me, x_ref, xo, ls.at[2])
        gk = keep(me, g_ref, go, ls.at[3])
        g.relay3()
        cot.rest()
        g.finish()
        cot.finish()
        pl.when(u >= nz - 1)(lambda: here(0, nz - 1))
        pl.when(u + nz - 1 < nz)(lambda: here(1, nz - 1))
        for k in range(1, nz):
            pl.when((u >= k - 1) & (u + 1 < nz))(lambda k=k: up(k).wait_send())
            pl.when((u + k - 1 < nz) & (u > 0))(lambda k=k: down(k).wait_send())
        for zo in range(nz):
            for p in range(rp):
                tb, c = weight(zo, p)
                if zo:
                    c.wait_send()
                else:
                    pl.when(tb != b)(c.wait_send)
                    pl.when(tb == b)(stay.wait)
        for j in range(n_o):
            src = (b // rp) * n_o + j
            c = remote(w_ref, wo_out.at[j], ws.at[0], wr.at[j], u, me.sib)
            pl.when(src != lin)(c.wait_recv)
        for c in (mate, half, xk, gk):
            c.wait()

    sh = jax.ShapeDtypeStruct
    return pl.pallas_call(
        kernel,
        out_shape=(
            sh((nb,) + x.shape, x.dtype), sh((nz, nb, shard, AUX), bf16), sh((n_o, shard, D), bf16),
            sh((nb,) + gm.shape, gm.dtype), sh(gm.shape, gm.dtype), sh(expert.shape, bf16),
        ),
        in_specs=[ANY] * 5,
        out_specs=(ANY,) * 6,
        scratch_shapes=[Gather.scratch(nb, 2)]
        + [DMA((nb,))] * 2
        + [DMA((2, nz))] * 2
        + [DMA((nz * rp,)), DMA((n_o,)), DMA((8,))],
        compiler_params=pltpu.CompilerParams(collective_id=cid, has_side_effects=True),
        cost_estimate=NO_COST,
        name="gather_inputs",
    )(x, pieces, wo, gm, expert)


def halo_forward(kv, gx, nz, nb, back, cid):
    def kernel(x_ref, g_ref, o_ref, go, ks, kr, gs, ls):
        me = Layer(nb)
        u, b = me.u, me.b
        bar = pltpu.get_barrier_semaphore()
        for d in range(1, nz):
            signal(bar, lax.rem(u + d, nz), b)
        for i in range(1, me.nc):
            signal(bar, u, me.peer(i))
        signal(bar, u, me.sib)
        pl.semaphore_wait(bar, nz - 1 + me.nc)

        def copy(d):
            src = x_ref if d == 1 else o_ref.at[d - 2]
            return remote(src, o_ref.at[d - 1], ks.at[d - 1], kr.at[d - 1], u + 1, b)

        def relay(d):
            if d > 1:
                pl.when(u >= d - 1)(lambda: copy(d - 1).wait_recv())
            pl.when((u >= d - 1) & (u + 1 < nz))(lambda: copy(d).start())

        relay(1)
        g = Gather(me, g_ref, go, gs)
        g.start()
        own = keep(me, g_ref, go, ls)
        for d in range(2, back + 1):
            relay(d)
        g.rest()
        g.finish()
        own.wait()
        pl.when(u >= back)(lambda: copy(back).wait_recv())
        for d in range(1, back + 1):
            pl.when((u >= d - 1) & (u + 1 < nz))(lambda d=d: copy(d).wait_send())

    sh = jax.ShapeDtypeStruct
    return pl.pallas_call(
        kernel,
        out_shape=(sh((back,) + kv.shape, kv.dtype), sh((nb,) + gx.shape, gx.dtype)),
        in_specs=[ANY] * 2,
        out_specs=(ANY,) * 2,
        scratch_shapes=[DMA((back,))] * 2 + [Gather.scratch(nb), DMA],
        compiler_params=pltpu.CompilerParams(collective_id=cid, has_side_effects=True),
        cost_estimate=NO_COST,
        name="halo_forward",
    )(kv, gx)


def pair_of(me, p_ref, sib_in, snd, land, sems):
    def one(h):
        return Reduce(
            me, lambda j, rows: p_ref[h, me.far(j), rows].astype(f32),
            lambda j: p_ref.at[h, me.unit(j) * 2 + 1 - me.core],
            sib_in.at[h], snd.at[h], land.at[h], sems.at[h])
    return one(0), one(1)


def write_to(ref, *lead):
    def write(rows, value):
        ref[(*lead, rows)] = value.astype(ref.dtype)
    return write


def add_to(ref, other, at):
    def write(rows, value):
        ref[rows] = value + other[at, rows].astype(f32)
    return write


def reduce_product(lhs, rhs, nb, cid):
    rows = lhs.shape[0] // nb
    cols = rhs.shape[1]

    def kernel(l_ref, r_ref, o_ref, *scratch):
        me = Layer(nb)
        me.enter()

        def block(t):
            part = l_ref[pl.ds(pl.multiple_of(t * rows, rows), rows), :]
            return jnp.dot(part, r_ref[...], preferred_element_type=f32)

        red = made(me, block, *scratch)
        red.phase2()
        red.end(write_to(o_ref))
        red.sent()

    return pl.pallas_call(
        kernel,
        out_shape=jax.ShapeDtypeStruct((rows, cols), f32),
        in_specs=[VMEM, VMEM],
        out_specs=VMEM,
        scratch_shapes=made_scratch(nb, rows, cols),
        compiler_params=pltpu.CompilerParams(
            collective_id=cid, has_side_effects=True, vmem_limit_bytes=48 * MIB
        ),
        cost_estimate=NO_COST,
        name="reduce_product",
    )(lhs, rhs)


def middle(x, ypart, nb, cid):
    _, _, rows, cols = ypart.shape

    def kernel(x_ref, y_ref, xo, o_ref, z_ref, gs, ls, *pair):
        me = Layer(nb)
        me.enter()
        g = Gather(me, x_ref, xo, gs)
        g.start()
        r0, r1 = pair_of(me, y_ref, *pair)
        for r in (r1, r0):
            for j in r.order:
                r.start(j)
        own = keep(me, x_ref, xo, ls)
        for j in r1.order[:-1]:
            r1.phase1(j)
        g.rest()
        r1.phase2()
        for j in r0.order[:-1]:
            r0.phase1(j)
        r0.phase2()
        r1.end(write_to(z_ref))
        g.finish()
        r0.end(write_to(o_ref))
        r0.sent()
        r1.sent()
        own.wait()

    sh = jax.ShapeDtypeStruct
    return pl.pallas_call(
        kernel,
        out_shape=(sh((nb,) + x.shape, x.dtype), sh((rows, cols), f32), sh((rows, cols), bf16)),
        in_specs=[ANY, VMEM],
        out_specs=(ANY, VMEM, VMEM),
        scratch_shapes=[Gather.scratch(nb), DMA]
        + Reduce.scratch(nb, rows, cols, 2),
        compiler_params=pltpu.CompilerParams(
            collective_id=cid, has_side_effects=True, vmem_limit_bytes=56 * MIB
        ),
        cost_estimate=NO_COST,
        name="middle",
    )(x, ypart)


def halo_back(dkv, yfar, nz, nb, rp, back, cid):
    R = dkv.shape[1]

    def kernel(d_ref, y_ref, kin, yo, ks, kr, ys):
        me = Layer(nb)
        first = (me.b // rp) * rp
        part = lax.rem(me.b, rp)
        bar = pltpu.get_barrier_semaphore()
        others = [(zo, p) for zo in range(nz) for p in range(rp) if zo or p]
        for zo, p in others:
            signal(bar, lax.rem(me.u + zo, nz), first + lax.rem(part + p, rp))
        pl.semaphore_wait(bar, len(others))

        def copy(d, p):
            k = d * rp + p
            return remote(d_ref.at[d], kin.at[d * rp + part], ks.at[k], kr.at[d * rp + part], me.u - d, first + p)

        def arrival(d, p):
            k = d * rp + p
            return remote(d_ref.at[d], kin.at[k], ks.at[k], kr.at[k], me.u, me.sib)

        for d in range(back + 1):
            for p in range(rp):
                if d:
                    pl.when(me.u >= d)(lambda d=d, p=p: copy(d, p).start())
                elif rp > 1:
                    pl.when(part != p)(lambda d=d, p=p: copy(d, p).start())
        mate = remote(y_ref, yo, ys.at[0], ys.at[1], me.across(1), me.b)
        mate.start()
        for d in range(back + 1):
            for p in range(rp):
                if d:
                    pl.when(me.u >= d)(lambda d=d, p=p: copy(d, p).wait_send())
                    pl.when(me.u + d < nz)(lambda d=d, p=p: arrival(d, p).wait_recv())
                elif rp > 1:
                    pl.when(part != p)(lambda d=d, p=p: copy(d, p).wait_send())
                    pl.when(part != p)(lambda d=d, p=p: arrival(d, p).wait_recv())
        mate.wait()

    return pl.pallas_call(
        kernel,
        out_shape=(
            jax.ShapeDtypeStruct(((back + 1) * rp, R, LANES), bf16), jax.ShapeDtypeStruct(yfar.shape, bf16),
        ),
        in_specs=[ANY] * 2,
        out_specs=(ANY,) * 2,
        scratch_shapes=[DMA(((back + 1) * rp,))] * 2 + [DMA((2,))],
        compiler_params=pltpu.CompilerParams(collective_id=cid, has_side_effects=True),
        cost_estimate=NO_COST,
        name="halo_back",
    )(dkv, yfar)


def reduce_last(lhs, rhs, pieces, nz, nb, rp, cid):
    rows = lhs.shape[0] // nb
    cols = rhs.shape[0]
    _, count, shard, width = pieces.shape
    n_o = nz * rp
    wide = (count - nb) // rp
    n = nz * nb

    def kernel(l_ref, r_ref, p_ref, o_ref, pin, win, land, tmp, total, zs, zr, ps, pr, ws, wr, ls, *scratch):
        me = Layer(nb)
        u = me.u
        lin = u * nb + me.b
        part = lax.rem(me.b, rp)
        bar = pltpu.get_barrier_semaphore()

        @pl.loop(1, n)
        def _(i):
            t = lax.rem(lin + i, n)
            signal(bar, t // nb, lax.rem(t, nb))

        pl.semaphore_wait(bar, n - 1)

        chunk = count // 2
        part_of = lambda c: pl.ds(c * chunk, chunk)

        def hop(way, o, c):
            to = u - 1 if way == 0 else u + 1
            return remote(tmp.at[way, o, part_of(c)], land.at[way, o, part_of(c)],
                          zs.at[way, o, c], zr.at[way, o, c], to, me.b)

        def ends(way, o):
            def run():
                for c in range(2):
                    tmp[way, o, part_of(c)] = p_ref[o, part_of(c)]
                    hop(way, o, c).start()
            return run

        def passes(way, o):
            def run():
                for c in range(2):
                    hop(way, o, c).wait_recv()

                    @pl.loop(c * chunk, (c + 1) * chunk)
                    def _(t):
                        tmp[way, o, t] = (p_ref[o, t].astype(f32) + land[way, o, t].astype(f32)).astype(bf16)

                    hop(way, o, c).start()
            return run

        def down(o):
            return u > o

        def up(o):
            return u < o

        ways = [(0, o) for o in range(nz - 1)], [(1, o) for o in range(nz - 1, 0, -1)]
        for way, o in ways[0] + ways[1]:
            pl.when(u == (0 if way else nz - 1))(ends(way, o))

        def relay(way, o):
            inner = (u > 0) & (u < nz - 1) & (up(o) if way else down(o))
            return inner, passes(way, o)

        low = 2 * u < nz - 1

        def relays(lo, hi, near):
            for way in range(2):
                mine = low if (way == 1) == near else jnp.logical_not(low)
                for way_o in ways[way][lo:hi]:
                    inner, run = relay(*way_o)
                    pl.when(mine & inner)(run)

        def block(t):
            rows_t = l_ref[pl.ds(pl.multiple_of(t * rows, rows), rows), :]
            return lax.dot_general(rows_t, r_ref[...], NT, preferred_element_type=f32)

        red = made(me, block, *scratch, waits=False)
        relays(0, 1, True)
        for j in red.order[:-1]:
            red.phase1(j)
        relays(1, nz, True)
        red.phase2()
        relays(0, nz, False)

        def here(way):
            def run():
                for c in range(2):
                    at = tmp.at[way, u, part_of(c)]
                    remote(at, at, zs.at[way, u, c], zr.at[way, u, c], u, me.sib).wait_recv()
            pl.when((u > 0) if way else (u < nz - 1))(run)

        here(0)
        here(1)

        @pl.loop(0, count)
        def _(t):
            tile = p_ref[u, t].astype(f32)
            tile = tile + jnp.where(u < nz - 1, land[0, u, t].astype(f32), 0.0)
            total[t] = (tile + jnp.where(u > 0, land[1, u, t].astype(f32), 0.0)).astype(bf16)

        out = []
        for i in range(1, nb):
            t = lax.rem(me.b + i, nb)
            c = remote(total.at[t], pin.at[me.b], ps.at[i], pr.at[i], u, t)
            c.start()
            out.append(c)
        own = pltpu.make_async_copy(total.at[me.b], pin.at[me.b], ls.at[0])
        own.start()

        def weight(p):
            t = (me.b // rp) * n_o + u * rp + p
            src = total.at[pl.ds(nb + p * wide, wide)]
            return t, remote(src, win.at[part], ws.at[p], wr.at[part], t // nb, lax.rem(t, nb))

        stay = lambda p: pltpu.make_async_copy(total.at[pl.ds(nb + p * wide, wide)], win.at[part], ls.at[1])
        for p in range(rp):
            t, c = weight(p)
            pl.when(t != lin)(c.start)
            pl.when(t == lin)(stay(p).start)
        red.end(write_to(o_ref))
        red.sent()
        for way, o in ways[0] + ways[1]:
            for c in range(2):
                pl.when(up(o) if way else down(o))(lambda way=way, o=o, c=c: hop(way, o, c).wait_send())
        for c in out:
            c.wait()
        own.wait()
        for p in range(rp):
            t, c = weight(p)
            pl.when(t != lin)(c.wait_send)
            pl.when(t == lin)(stay(p).wait)
        hg = lin // n_o
        layer = lax.rem(lin, n_o) // rp
        for p in range(rp):
            c = remote(total.at[pl.ds(nb, wide)], win.at[p], ws.at[0], wr.at[p], u, me.sib)
            pl.when(layer * nb + hg * rp + p != lin)(c.wait_recv)

    sh = jax.ShapeDtypeStruct
    return pl.pallas_call(
        kernel,
        out_shape=(
            sh((rows, cols), f32), sh((nb, shard, width), bf16), sh((rp, wide, shard, width), bf16),
        ),
        in_specs=[VMEM, VMEM, VMEM],
        out_specs=(VMEM, ANY, ANY),
        scratch_shapes=[pltpu.VMEM((2, nz, count, shard, width), bf16)] * 2
        + [pltpu.VMEM((count, shard, width), bf16)]
        + [DMA((2, nz, 2))] * 2
        + [DMA((nb,))] * 2
        + [DMA((rp,))] * 2
        + [DMA((2,))]
        + made_scratch(nb, rows, cols),
        compiler_params=pltpu.CompilerParams(
            collective_id=cid, has_side_effects=True, vmem_limit_bytes=56 * MIB
        ),
        cost_estimate=NO_COST,
        name="reduce_last",
    )(lhs, rhs, pieces)


def turn(a, c, s1, s2):
    return a * c + pltpu.roll(a, LANES - HW // 2, 1) * s1 + pltpu.roll(a, HW // 2, 1) * s2


def turn_back(a, c, s1, s2):
    return a * c - pltpu.roll(a, LANES - HW // 2, 1) * s1 - pltpu.roll(a, HW // 2, 1) * s2


def swap(a):
    return pltpu.roll(a, HW, 1)


def low_half():
    return lax.broadcasted_iota(jnp.int32, (1, LANES), 1) < HW


def row_block(step, width):
    return pl.BlockSpec((step, width), lambda i: (i, 0))


def whole_block(a):
    zeros = (0,) * a.ndim
    return pl.BlockSpec(a.shape, lambda i: zeros)


def prepare(w_query, w_key, w_value, extra, gains, w_inner, w_outer, cotangent, routes):
    S = w_query.shape[0]
    T = routes.shape[0]
    dz = w_inner.shape[1]
    W = 3 * FF
    half = W // 2

    ins = (w_query, w_key, w_value, extra[0], gains, w_inner, w_outer, cotangent, routes)

    def kernel(*refs):
        n, m = len(ins), len(outs)
        hbm, (isem, osem), vmem = refs[:n + m], refs[n + m:n + m + 2], refs[n + m + 2:]
        loads = [pltpu.make_async_copy(hbm[k], vmem[k], isem.at[k]) for k in range(n)]
        for c in loads:
            c.start()
        q_ref, k_ref, v_ref, x_ref, n_ref, i_ref, o_ref, c_ref, r_ref = vmem[:n]
        p_ref, g_ref, a_ref, b_ref, f_ref = vmem[n:]
        saves = [pltpu.make_async_copy(vmem[n + k], hbm[n + k], osem.at[k]) for k in range(m)]
        for c in loads:
            c.wait()
        low = low_half()
        lane = lax.broadcasted_iota(jnp.int32, (1, LANES), 1)

        def low64(ref, at):
            a = ref[:, at // LANES * LANES:at // LANES * LANES + LANES].astype(f32)
            return swap(a) if at % LANES else a

        spread = lax.broadcasted_iota(jnp.int32, (S, S), 0) == lax.broadcasted_iota(jnp.int32, (S, S), 1)
        tail = x_ref[...].astype(f32)
        for i in range(2):
            column = jnp.sum(jnp.where(spread, n_ref[i:i + 1, :], 0.0), axis=1, keepdims=True)
            tail = jnp.where(lane == r_first + i, column, tail)
        for h in range(KV):
            at = h * QCOLS
            two = lambda a, b: jnp.where(low, a, swap(b)).astype(bf16)
            p_ref[h, :, :LANES] = two(low64(q_ref, at), low64(q_ref, at + HW))
            p_ref[h, :, LANES:2 * LANES] = two(low64(q_ref, at + 2 * HW), low64(k_ref, h * HW))
            p_ref[h, :, 2 * LANES:] = jnp.where(low, low64(v_ref, h * HW), tail).astype(bf16)
        saves[0].start()
        g_ref[:, :D] = c_ref[...]
        named = r_ref[:, 0:1] + HW == lane
        for j in range(1, TOPK):
            named = named | (r_ref[:, j:j + 1] + HW == lane)
        g_ref[:, D:] = jnp.where(named, 1.0, 0.0).astype(bf16)
        saves[1].start()
        odd = lax.rem(lax.axis_index("ulysses"), 2)
        same, outer = i_ref[odd], o_ref[odd].astype(f32).T.astype(bf16)
        a_ref[...] = same[:, :half]
        b_ref[:, :2 * FF - half] = same[:, half:]
        b_ref[:, 2 * FF - half:] = outer
        f_ref[:, :2 * FF] = i_ref[1 - odd]
        f_ref[:, 2 * FF:] = o_ref[1 - odd].astype(f32).T.astype(bf16)
        for c in saves[2:]:
            c.start()
        for c in saves:
            c.wait()

    r_first = extra[1]
    sh = lambda *shape: jax.ShapeDtypeStruct(shape, bf16)
    outs = (sh(KV, S, AUX), sh(T, D + LANES), sh(dz, half), sh(dz, half), sh(dz, W))
    return pl.pallas_call(
        kernel,
        out_shape=outs,
        in_specs=[ANY] * len(ins),
        out_specs=(ANY,) * len(outs),
        scratch_shapes=[DMA((len(ins),)), DMA((len(outs),))]
        + [pltpu.VMEM(a.shape, a.dtype) for a in (*ins, *outs)],
        compiler_params=pltpu.CompilerParams(vmem_limit_bytes=48 * MIB),
        cost_estimate=NO_COST,
        name="prepare",
    )(*ins)


def project(x, gain, packed, c, s1, s2):
    R = x.shape[0]
    step = 256

    def kernel(x_ref, g_ref, w_ref, c_ref, a_ref, b_ref, q_ref, kv_ref, h_ref):
        v = x_ref[...].astype(f32)
        inv = lax.rsqrt(jnp.mean(v * v, axis=1, keepdims=True) + EPS)
        h = (v * inv * g_ref[...]).astype(bf16)
        h_ref[...] = h
        out = jnp.dot(h, w_ref[...], preferred_element_type=f32)
        tables = (c_ref[...], a_ref[...], b_ref[...])
        low = low_half()
        t0 = turn(out[:, :LANES], *tables)
        t1 = turn(out[:, LANES:2 * LANES], *tables)
        scale = lambda a: (jnp.where(low, a, 0.0) * (1.0 / math.sqrt(HW))).astype(bf16)
        q_ref[0] = scale(t0)
        q_ref[1] = scale(swap(t0))
        q_ref[2] = scale(t1)
        kv_ref[...] = jnp.where(low, swap(t1), swap(out[:, 2 * LANES:])).astype(bf16)

    sh = jax.ShapeDtypeStruct
    return pl.pallas_call(
        kernel,
        grid=(R // step,),
        out_shape=(sh((GROUP, R, LANES), bf16), sh((R, LANES), bf16), sh((R, D), bf16)),
        in_specs=[row_block(step, D), whole_block(gain), whole_block(packed)] + [row_block(step, LANES)] * 3,
        out_specs=(
            pl.BlockSpec((GROUP, step, LANES), lambda i: (0, i, 0)),
            row_block(step, LANES),
            row_block(step, D),
        ),
        compiler_params=pltpu.CompilerParams(vmem_limit_bytes=32 * MIB),
        cost_estimate=NO_COST,
        name="project",
    )(x, gain, packed, c, s1, s2)


BQ = 256
BK = 512
NT = (((1,), (1,)), ((), ()))
NN = (((1,), (0,)), ((), ()))
TN = (((0,), (0,)), ((), ()))


def mm(a, b, dims=NN):
    return lax.dot_general(a, b, dims, preferred_element_type=f32)


def seen(meta, st, i, kb, nq):
    qpos = meta[nq] + i * BQ + lax.broadcasted_iota(jnp.int32, (BQ, 1), 0)
    kpos = kb * BK + lax.broadcasted_iota(jnp.int32, (1, BK), 1)
    return ((kpos <= qpos) & (kpos >= st))[None]


def attend(q, kv, starts, meta):
    _, Rq, _ = q.shape
    nq = Rq // BQ
    M = GROUP * BQ

    def kernel(meta, q_ref, kv_ref, st_ref, o_ref, l_ref):
        i = pl.program_id(0)
        qv = q_ref[...].reshape(M, LANES)
        st = st_ref[...]
        last = (meta[nq] + i * BQ + BQ - 1) // BK + 1

        def step(kb, carry):
            m, l, acc = carry
            keys = kv_ref[pl.ds(pl.multiple_of(kb * BK, BK), BK), :]
            s = mm(qv, keys, NT).reshape(GROUP, BQ, BK)
            s = jnp.where(seen(meta, st, i, kb, nq), s, NEG)
            m2 = jnp.maximum(m, jnp.max(s, axis=2, keepdims=True))
            w = jnp.exp(s - m2)
            f = jnp.exp(m - m2)
            l = l * f + jnp.sum(w, axis=2, keepdims=True)
            pv = mm(w.astype(bf16).reshape(M, BK), keys)
            return m2, l, acc * f + pv.reshape(GROUP, BQ, LANES)

        init = (
            jnp.full((GROUP, BQ, 1), NEG, f32),
            jnp.zeros((GROUP, BQ, 1), f32),
            jnp.zeros((GROUP, BQ, LANES), f32),
        )
        m, l, acc = lax.fori_loop(meta[i], last, step, init)
        o = acc / l
        o_ref[:, :LANES] = jnp.where(low_half(), swap(o[0]), o[1]).astype(bf16)
        o_ref[:, LANES:] = swap(o[2])[:, :HW].astype(bf16)
        l_ref[...] = m + jnp.log(l)

    sh = jax.ShapeDtypeStruct
    blk = lambda w: pl.BlockSpec((GROUP, BQ, w), lambda i, m: (0, i, 0))
    return pl.pallas_call(
        kernel,
        grid_spec=pltpu.PrefetchScalarGridSpec(
            num_scalar_prefetch=1,
            grid=(nq,),
            in_specs=[
                blk(LANES),
                pl.BlockSpec(kv.shape, lambda i, m: (0, 0)),
                pl.BlockSpec((BQ, 1), lambda i, m: (i, 0)),
            ],
            out_specs=(pl.BlockSpec((BQ, QCOLS), lambda i, m: (i, 0)), blk(1)),
        ),
        out_shape=(sh((Rq, QCOLS), bf16), sh((GROUP, Rq, 1), f32)),
        compiler_params=pltpu.CompilerParams(vmem_limit_bytes=48 * MIB),
        cost_estimate=NO_COST,
        name="attend",
    )(meta, q, kv, starts)


def attend_back(q, kv, starts, meta, lse, mixed, dattn, wo):
    _, Rq, _ = q.shape
    nq = Rq // BQ
    M = GROUP * BQ
    K = kv.shape[0]

    def kernel(meta, q_ref, kv_ref, st_ref, l_ref, o_ref, g_ref, w_ref, dq_ref, dkv_ref, dw_ref):
        i = pl.program_id(0)

        @pl.when(i == 0)
        def _():
            dkv_ref[...] = jnp.zeros_like(dkv_ref)
            dw_ref[...] = jnp.zeros_like(dw_ref)

        g = g_ref[...]
        mixed = o_ref[...]
        dm = mm(g, w_ref[...], NT).astype(bf16).astype(f32)
        dw_ref[...] += mm(mixed, g, TN)
        low = low_half()
        d0 = dm[:, :LANES]
        d1 = jnp.concatenate([dm[:, LANES:], jnp.zeros((BQ, LANES - HW), f32)], axis=1)
        m0 = mixed[:, :LANES].astype(f32)
        m1 = jnp.concatenate([mixed[:, LANES:].astype(f32), jnp.zeros((BQ, LANES - HW), f32)], axis=1)
        total = lambda a: jnp.sum(a, axis=1, keepdims=True)
        e0, e1 = d0 * m0, d1 * m1
        first = total(jnp.where(low, e0, 0.0))
        delta = jnp.stack([first, total(jnp.where(low, 0.0, e0)), total(e1)])
        high = lambda a: jnp.where(low, 0.0, a).astype(bf16)
        do = jnp.concatenate([high(swap(d0)), high(d0), high(swap(d1))], axis=0)
        qv = q_ref[...].reshape(M, LANES)
        lse = l_ref[...]
        st = st_ref[...]
        last = (meta[nq] + i * BQ + BQ - 1) // BK + 1

        def step(kb, dq):
            at = pl.ds(pl.multiple_of(kb * BK, BK), BK)
            keys = kv_ref[at, :]
            s = mm(qv, keys, NT).reshape(GROUP, BQ, BK)
            p = jnp.where(seen(meta, st, i, kb, nq), jnp.exp(s - lse), 0.0)
            dp = mm(do, keys, NT).reshape(GROUP, BQ, BK)
            ds = (p * (dp - delta)).astype(bf16).reshape(M, BK)
            pb = p.astype(bf16).reshape(M, BK)
            dkv_ref[at, :] += mm(ds, qv, TN) + mm(pb, do, TN)
            return dq + mm(ds, keys)

        dq = lax.fori_loop(meta[i], last, step, jnp.zeros((M, LANES), f32))
        dq_ref[...] = (dq * (1.0 / math.sqrt(HW))).astype(bf16).reshape(GROUP, BQ, LANES)

    sh = jax.ShapeDtypeStruct
    blk = lambda w: pl.BlockSpec((GROUP, BQ, w), lambda i, m: (0, i, 0))
    rows = lambda w: pl.BlockSpec((BQ, w), lambda i, m: (i, 0))
    full = lambda *shape: pl.BlockSpec(shape, lambda i, m: (0, 0))
    return pl.pallas_call(
        kernel,
        grid_spec=pltpu.PrefetchScalarGridSpec(
            num_scalar_prefetch=1,
            grid=(nq,),
            in_specs=[
                blk(LANES), full(*kv.shape), rows(1), blk(1), rows(QCOLS), rows(D), full(QCOLS, D),
            ],
            out_specs=(blk(LANES), full(K, LANES), full(QCOLS, D)),
        ),
        out_shape=(sh((GROUP, Rq, LANES), bf16), sh((K, LANES), f32), sh((QCOLS, D), f32)),
        compiler_params=pltpu.CompilerParams(vmem_limit_bytes=48 * MIB),
        cost_estimate=NO_COST,
        name="attend_back",
    )(meta, q, kv, starts, lse, mixed, dattn, wo)


def weight_grads(dq, dkv, kin, ok, tables, h1, packed, tail):
    _, Rq, _ = dq.shape
    step = 256
    arrivals = kin.shape[0]

    def kernel(ok_ref, dq_ref, dkv_ref, kin_ref, c_ref, a_ref, b_ref, h_ref, w_ref, t_ref, o_ref, p_ref, acc):
        i = pl.program_id(0)

        @pl.when(i == 0)
        def _():
            acc[...] = jnp.zeros_like(acc)

        kv = dkv_ref[...]
        for k in range(arrivals):
            kv = kv + jnp.where(ok_ref[k] > 0, kin_ref[k].astype(f32), 0.0)
        kv = kv.astype(bf16).astype(f32)
        low = low_half()
        tables = (c_ref[...], a_ref[...], b_ref[...])
        q = [dq_ref[h].astype(f32) for h in range(GROUP)]
        kv = swap(kv)
        t0 = turn_back(jnp.where(low, q[0], swap(q[1])), *tables)
        t1 = turn_back(jnp.where(low, q[2], kv), *tables)
        out = jnp.concatenate([t0, t1, jnp.where(low, kv, 0.0)], axis=1).astype(bf16)
        o_ref[...] = out
        acc[...] += mm(h_ref[...], out, TN)

        @pl.when(i == Rq // step - 1)
        def _():
            w = w_ref[...].astype(f32)
            dw = acc[...]
            t = t_ref[...]
            lane = lax.broadcasted_iota(jnp.int32, (1, LANES), 1)
            gain = jnp.sum(jnp.where(lane == ok_ref[arrivals], w[:, 2 * LANES:], 0.0), axis=1, keepdims=True)
            d_gain = jnp.sum(w * dw, axis=1, keepdims=True) / gain
            t = t + jnp.where(lane == ok_ref[arrivals] + 1, d_gain, 0.0)
            p_ref[:, :2 * LANES] = dw[:, :2 * LANES].astype(bf16)
            p_ref[:, 2 * LANES:] = jnp.where(low, dw[:, 2 * LANES:], t).astype(bf16)

    sh = jax.ShapeDtypeStruct
    heads = lambda n: pl.BlockSpec((n, step, LANES), lambda i: (0, i, 0))
    return pl.pallas_call(
        kernel,
        grid=(Rq // step,),
        out_shape=(sh((Rq, AUX), bf16), sh((D, AUX), bf16)),
        in_specs=[pl.BlockSpec(memory_space=pltpu.SMEM), heads(GROUP), row_block(step, LANES), heads(arrivals)]
        + [row_block(step, LANES)] * 3
        + [row_block(step, D), whole_block(packed), whole_block(tail)],
        out_specs=(row_block(step, AUX), pl.BlockSpec((D, AUX), lambda i: (0, 0))),
        scratch_shapes=[pltpu.VMEM((D, AUX), f32)],
        compiler_params=pltpu.CompilerParams(vmem_limit_bytes=48 * MIB),
        cost_estimate=NO_COST,
        name="weight_grads",
    )(ok, dq, dkv, kin, *tables, h1, packed, tail)


def experts(h2_own, g_own, g_oth, router, hot, weights, sent, leave, nz, nb, cid):
    T = h2_own.shape[0]
    nc = nb // 2
    step = 2 * T
    units = 2 * nc
    dz = D // nz
    C = D + LANES
    W = 3 * FF
    nw = len(weights)
    ng = len(leave)
    resident = nb <= 8

    def kernel(x_ref, g0_ref, g1_ref, r_ref, e_ref, *rest):
        win = rest[:nw]
        y_ref, s_ref = rest[nw:nw + 2]
        rest = rest[nw + 2:]
        din, gin = rest[:ng], rest[ng]
        rest = rest[ng + 1:]
        h_all, hbuf, part, gbuf, ybuf, wc, acc, zbuf, gs, zs, sem, gsem, ysem, *pair = rest
        me = Layer(nb)
        me.enter(sorted({1, sent[0]}))
        own, oth = h_all.at[0], h_all.at[1]
        mate = remote(x_ref, oth.at[me.b], zs.at[0], zs.at[1], me.across(1), me.b)
        mate.start()
        ga = Gather(me, x_ref, own, gs.at[0])
        gb = Gather(me, oth.at[me.b], oth, gs.at[1])
        ga.start()
        mine = pltpu.make_async_copy(x_ref, own.at[me.b], zs.at[2])
        mine.start()
        rows_at = lambda d: pl.ds(pl.multiple_of(me.across(d) * dz, dz), dz)
        loads = [
            pltpu.make_async_copy(win[k], wc.at[rows_at(d), pl.ds(c, a.shape[1])], sem.at[k])
            for k, (a, d, c) in enumerate(weights)
        ]
        for c in loads:
            c.start()

        def place(u):
            other = (u >= 2) & (u < nc + 2)
            j = jnp.where(u < 2, u, jnp.where(other, u - 2, 2 * nc + 1 - u))
            return jnp.where(other, 1, 0), j

        def cot(u, h):
            _, j = place(u)
            rows = pl.ds(pl.multiple_of(me.unit(j) * step, step), step)
            slot = lax.rem(u, 2)
            return pltpu.make_async_copy((g1_ref if h else g0_ref).at[rows], gbuf.at[slot], gsem.at[slot])

        def cot_start(u):
            h, _ = place(u)
            pl.when(h == 0)(lambda: cot(u, 0).start())
            pl.when(h == 1)(lambda: cot(u, 1).start())

        def result(u):
            h, j = place(u)
            slot = lax.rem(u, 2)
            return pltpu.make_async_copy(
                ybuf.at[slot], y_ref.at[h, pl.ds(pl.multiple_of(me.unit(j) * 2, 2), 2)], ysem.at[slot])

        cot_start(jnp.int32(0))
        acc[...] = jnp.zeros_like(acc)
        ra, rb = pair_of(me, part, *pair)
        back = remote(zbuf.at[0], zbuf.at[1], zs.at[3], zs.at[4], me.across(1), me.b)
        ga.relay1()
        for c in loads:
            c.wait()
        mine.wait()

        def at(k, f):
            def run(u):
                pl.when(u == k)(f)
            return run

        def arrive(u):
            def first():
                ga.relay2()
                mate.wait_recv()
                gb.start()

            def second():
                ga.relay3()
                gb.relay1()

            at(1, first)(u)
            at(2, second)(u)
            at(3, gb.relay2)(u)
            at(4, gb.relay3)(u)
            for k in range(units):
                h = 1 if 2 <= k < nc + 2 else 0
                j = k if k < 2 else (k - 2 if h else 2 * nc + 1 - k)
                at(k, lambda h=h, j=j: (gb if h else ga).passed(j))(u)

        def depart(u):
            for k in range(units):
                h = 1 if 2 <= k < nc + 2 else 0
                j = k if k < 2 else (k - 2 if h else 2 * nc + 1 - k)
                at(k, lambda h=h, j=j: (rb if h else ra).start(j))(u)

            def mates():
                for j in rb.order[:-1]:
                    rb.phase1(j)

            at(nc + 1, mates)(u)

            def ours():
                rb.phase2()
                ra.phase1(3)
                ra.phase1(1)

            if nc == 4:
                at(nc + 2, ours)(u)

            def across():
                rb.end(write_to(zbuf, 0))
                back.start()

            at(units - 1, across)(u)

        @pl.loop(0, units)
        def _(u):
            h, j = place(u)
            slot = lax.rem(u, 2)
            pl.when(u + 1 < units)(lambda: cot_start(u + 1))
            arrive(u)
            cot(u, 0).wait()
            pl.when(u >= 2)(lambda: result(u - 2).wait())
            two = pl.ds(pl.multiple_of(me.unit(j) * 2, 2), 2)
            if resident:
                x = h_all[h, two].reshape(step, D)
            else:
                c = pltpu.make_async_copy(h_all.at[h, two], hbuf, zs.at[5])
                c.start()
                c.wait()
                x = hbuf[...].reshape(step, D)
            hot = e_ref[...]
            mask = gbuf[slot, :, D:].astype(f32) > 0
            logits = mm(x, r_ref[...])
            top = jnp.max(jnp.where(mask, logits, NEG), axis=1, keepdims=True)
            w = jnp.where(mask, jnp.exp(jnp.where(mask, logits - top, 0.0)), 0.0)
            gate = jnp.sum(w * hot, axis=1, keepdims=True) / jnp.sum(w, axis=1, keepdims=True)
            gu = mm(x, wc[:, :2 * FF])
            a, up = gu[:, :FF], gu[:, FF:]
            sg = jax.nn.sigmoid(a)
            silu = a * sg
            act = (silu * up).astype(bf16)
            g = gbuf[slot, :, :D]
            ybuf[slot] = (gate * mm(act, wc[:, 2 * FF:], NT)).astype(bf16).reshape(2, T, D)
            result(u).start()
            raw = mm(g, wc[:, 2 * FF:])
            acc[:, 2 * FF:] += mm((gate * g.astype(f32)).astype(bf16), act, TN)
            dgate = jnp.sum(act.astype(f32) * raw, axis=1, keepdims=True)
            dact = gate * raw
            dgu = jnp.concatenate(
                [dact * up * (sg * (1.0 + a * (1.0 - sg))), dact * silu], axis=1).astype(bf16)
            acc[:, :2 * FF] += mm(x, dgu, TN)
            part[h, two, :, :D] = mm(dgu, wc[:, :2 * FF], NT).astype(bf16).reshape(2, T, D)
            hi = dgate.astype(bf16).astype(f32)
            part[h, two, :, D:] = (hi * hot + swap((dgate - hi) * hot)).astype(bf16).reshape(2, T, LANES)
            depart(u)

        for j in (2,) if nc == 4 else ra.order[:-1]:
            ra.phase1(j)
        wc[...] = acc[...].astype(bf16)
        grad = lambda d, c, width: wc.at[rows_at(d), pl.ds(c, width)]
        going = remote(grad(*sent), gin, zs.at[6], zs.at[7], me.across(sent[0]), me.b)
        going.start()
        saves = [pltpu.make_async_copy(grad(*p), din[k], sem.at[k]) for k, p in enumerate(leave)]
        for c in saves:
            c.start()
        ra.phase2()
        back.wait_recv()
        ra.end(add_to(s_ref, zbuf, 1))
        back.wait_send()
        mate.wait_send()
        for r in (ga, gb, ra, rb):
            r.sent()
        for c in saves:
            c.wait()
        going.wait()
        result(jnp.int32(units - 2)).wait()
        result(jnp.int32(units - 1)).wait()

    sh = jax.ShapeDtypeStruct
    v = lambda shape, kind=bf16: pltpu.VMEM(shape, kind)
    return pl.pallas_call(
        kernel,
        out_shape=(sh((2, nb, T, D), bf16), sh((T, C), f32))
        + tuple(sh((dz, width), bf16) for _, _, width in leave)
        + (sh((dz, sent[2]), bf16),)
        + (() if resident else (sh((2, nb, T, D), bf16),)),
        in_specs=[ANY] * 3 + [VMEM] * 2 + [ANY] * nw,
        out_specs=(ANY, VMEM) + (ANY,) * (ng + 1 + int(not resident)),
        scratch_shapes=([v((2, nb, T, D))] if resident else [])
        + [
            v((2, T, D)), v((2, nb, T, C)), v((2, step, C)), v((2, 2, T, D)),
            v((D, W)), v((D, W), f32), v((2, T, C)),
            Gather.scratch(nb, 2), DMA((8,)), DMA((max(nw, ng),)), DMA((2,)), DMA((2,)),
        ]
        + Reduce.scratch(nb, T, C, 2),
        compiler_params=pltpu.CompilerParams(
            collective_id=cid, has_side_effects=True, vmem_limit_bytes=60 * MIB
        ),
        cost_estimate=NO_COST,
        name="experts",
    )(h2_own, g_own, g_oth, router, hot, *[a for a, _, _ in weights])


def finish(dh1, x, gain, dresid, pin, win, resid, ysum, yfar, grads, places):
    T = x.shape[0]
    groups, rp, S, _ = pin.shape
    senders = win.shape[0]
    m = len(grads)
    dz = grads[0].shape[0]

    def kernel(d_ref, x_ref, g_ref, r_ref, p_ref, w_ref, s_ref, y_ref, f_ref, *rest):
        srcs = rest[:m]
        t_ref, q_ref, k_ref, v_ref, m_ref, o_ref, out_ref, in_ref, ex_ref = rest[m:]
        odd = lax.rem(lax.axis_index("ulysses"), 2)
        for e in range(2):
            at = odd if e == 0 else 1 - odd
            for c in range(0, 3 * FF, FF // 2):
                total = 0.0
                for r, (d, lo, width) in zip(srcs, places):
                    if d % 2 == e and lo <= c < lo + width:
                        total = total + r[:, c - lo:c - lo + FF // 2].astype(f32)
                if c < 2 * FF:
                    in_ref[at, :, c:c + FF // 2] = total
                else:
                    ex_ref[at, c - 2 * FF:c - 2 * FF + FF // 2, :] = total.T
        v = x_ref[...].astype(f32)
        inv = lax.rsqrt(jnp.mean(v * v, axis=1, keepdims=True) + EPS)
        n = v * inv
        w = d_ref[...] * g_ref[...]
        t_ref[...] = r_ref[...] + inv * (w - n * jnp.mean(w * n, axis=1, keepdims=True))
        out_ref[...] = s_ref[...] + y_ref[...] + f_ref[...].astype(f32)
        for k in range(D // AUX):
            parts = [w_ref[p, k].astype(f32) for p in range(senders)]
            o_ref[:, k * AUX:(k + 1) * AUX] = functools.reduce(lambda a, b: a + b, parts)
        small = 0.0
        for h in range(groups):
            row = 0.0
            for p in range(rp):
                row = row + p_ref[h, p].astype(f32)
            q_ref[:, h * QCOLS:(h + 1) * QCOLS] = row[:, :QCOLS]
            k_ref[:, h * HW:(h + 1) * HW] = row[:, QCOLS:QCOLS + HW]
            v_ref[:, h * HW:(h + 1) * HW] = row[:, QCOLS + HW:ROUTER_AT]
            small = small + row[:, 2 * LANES:]
        m_ref[...] = small

    sh = lambda *shape: jax.ShapeDtypeStruct(shape, f32)
    return pl.pallas_call(
        kernel,
        out_shape=(sh(T, D), sh(S, HEADS * HW), sh(S, KV * HW), sh(S, KV * HW), sh(S, LANES), sh(S, D), sh(T, D),
                   sh(2, dz, 2 * FF), sh(2, FF, dz)),
        in_specs=[VMEM] * (9 + m),
        out_specs=(VMEM,) * 9,
        compiler_params=pltpu.CompilerParams(vmem_limit_bytes=60 * MIB),
        cost_estimate=NO_COST,
        name="finish",
    )(dh1, x, gain, dresid, pin, win, resid, ysum, yfar, *grads)


def locate(rows, lengths):
    passed = rows[:, None] >= jnp.cumsum(lengths)
    return jnp.sum(jnp.where(passed, lengths, 0), axis=-1)


def norm_rows(v, gain):
    inverse = lax.rsqrt(jnp.mean(v * v, axis=-1, keepdims=True) + EPS)
    normed = v * inverse
    return normed, inverse, normed * gain


def norm_back(upstream, normed, inverse, gain):
    d_normed = upstream * gain
    d_gain = jnp.sum(upstream * normed, axis=0)
    d_values = inverse * (d_normed - normed * jnp.mean(d_normed * normed, axis=-1, keepdims=True))
    return d_values, d_gain


def rows_of(a, start, count):
    return a if a.shape[0] == count else lax.dynamic_slice_in_dim(a, start, count, 0)


def widen(a, start, count):
    if a.shape[0] == count:
        return a
    return lax.dynamic_update_slice_in_dim(jnp.zeros((count,) + a.shape[1:], a.dtype), a, start, 0)


def on_device(tokens, lengths, routes, gain_attn, w_query, w_key, w_value, w_output, gain_moe,
              w_router, w_inner, w_outer, cotangent):
    nz = lax.axis_size("ulysses")
    nb = lax.axis_size("blk")
    z = lax.axis_index("ulysses")
    b = lax.axis_index("blk")
    T = tokens.shape[0]
    R = nb * T
    rp = nb // KV
    Rq = R // rp
    part = b % rp
    at = part * Rq
    n = nz * nb
    S = D // n
    E = w_router.shape[1]
    longest = min(LENMAX, n * T // 2)
    back = min(nz - 1, (longest - 1 + R - 1) // R)
    n_o = QCOLS // S
    odd = z % 2

    lanes = jnp.arange(LANES, dtype=jnp.int32)
    extra = (jnp.pad(w_router, ((0, 0), (HW, LANES - HW - E))), HW + E)
    gains = jnp.stack([gain_attn, gain_moe]).astype(f32)
    pieces, cot_mask, same_a, same_b, other = prepare(
        w_query, w_key, w_value, extra, gains, w_inner, w_outer, cotangent, routes)
    W = 3 * FF
    half = W // 2
    early = min(2, nz - 1)
    xg, packed, wo, g_own, g_far, first = gather_inputs(
        tokens, pieces, w_output, cot_mask, same_a if early % 2 == 0 else other[:, :half], early, nz, nb, 0)
    xg = xg.reshape(R, D)
    packed = packed.reshape(D, AUX)
    router = packed[:, 2 * LANES:]
    gains = packed[:, ROUTER_AT + E:ROUTER_AT + E + 2].astype(f32).T
    gain1, gain2 = gains[0:1], gains[1:2]

    flip = lambda d: [(k, k ^ d) for k in range(nz)]
    give = lambda w, d: lax.ppermute(w, "ulysses", flip(d))
    named = jnp.any(routes[:, :, None] + HW == lanes[None, None, :], axis=1)
    second, packed = lax.optimization_barrier((same_b if early % 2 == 0 else other[:, half:], packed))
    second = give(second, early)
    weights = [(same_a, 0, 0), (same_b, 0, half), (first, early, 0)]

    rows = z * R + jnp.arange(R, dtype=jnp.int32)
    opening = locate(rows, lengths)
    pair = lanes % HW
    frequency = THETA ** (-((pair % (HW // 2)).astype(f32) * 2.0 / HW))
    angles = (rows - opening).astype(f32)[:, None] * frequency[None, :]
    cos, sin = jnp.cos(angles), jnp.sin(angles)
    tables = (cos, jnp.where(pair < HW // 2, -sin, 0.0), jnp.where(pair < HW // 2, 0.0, sin))

    q, kv, h1 = project(xg, gain1, packed, *tables)
    if rp > 1:
        q = lax.dynamic_slice_in_dim(q, at, Rq, 1)
    kv, second = lax.optimization_barrier((kv, second))
    weights.append((second, early, half))
    far, g_oth = halo_forward(kv, g_far, nz, nb, back, 1)
    g_own, g_oth = g_own.reshape(R, D + LANES), g_oth.reshape(R, D + LANES)
    wo = wo.reshape(QCOLS, D)
    same_a, same_b, other, far = lax.optimization_barrier((same_a, same_b, other, far))
    for d in range(1, nz):
        if d % 2 and d != early:
            weights.append((give(other, d), d, 0))
        elif d != early:
            weights += [(give(same_a, d), d, 0), (give(same_b, d), d, half)]
    kv_all = jnp.concatenate([far[d - 1] for d in range(back, 0, -1)] + [kv], axis=0)
    base = (z - back) * R
    starts = rows_of(opening, at, Rq) - base
    meta = jnp.concatenate([starts[::BQ] // BK, (back * R + at)[None]]).astype(jnp.int32)
    starts = starts[:, None]
    mixed, lse = attend(q, kv_all, starts, meta)
    attn = reduce_product(widen(mixed, at, R), wo, nb, 2)

    resid = tokens.astype(f32) + attn
    n2, inv2, scaled2 = norm_rows(resid, gain2)
    h2_own = scaled2.astype(bf16)
    hot = (lanes == HW + b * EXP_DEV + odd).astype(f32)[None, :]
    sent = (early, 0, FF)
    leave = [(0, 0, W), (early, FF, W - FF), (nz - 1, 0, half), (nz - 1, half, half)]
    leave += [(d, 0, W) for d in range(1, nz - 1) if d != early]
    y, summed, *grads = experts(h2_own, g_own, g_oth, router, hot, weights, sent, leave, nz, nb, 3)
    grads, got = grads[:len(leave)], grads[len(leave)]

    upstream = cotangent.astype(f32)
    dgates = summed[:, D:] + jnp.roll(summed[:, D:], HW, 1)
    logits = mm(h2_own, router)
    top = jnp.max(jnp.where(named, logits, NEG), axis=1, keepdims=True)
    w = jnp.where(named, jnp.exp(jnp.where(named, logits - top, 0.0)), 0.0)
    gates = w / jnp.sum(w, axis=1, keepdims=True)
    dlogits = gates * (dgates - jnp.sum(gates * dgates, axis=1, keepdims=True))
    dlogits = dlogits.astype(bf16)
    dh2 = summed[:, :D] + mm(dlogits, router, NT)
    d_norm2, d_gain2 = norm_back(dh2, n2, inv2, gain2)
    dresid = upstream + d_norm2
    grads = [grads[0]] + [give(a, d) for a, (d, _, _) in zip(grads[1:], leave[1:])]
    dattn, ysum, yfar = middle(dresid.astype(bf16), y, nb, 5)
    dattn = dattn.reshape(R, D)
    tail = mm(h2_own, dlogits, TN) + jnp.where(lanes == HW + E, d_gain2[:, None], 0.0)

    dq, dkv, dwo = attend_back(q, kv_all, starts, meta, lse, mixed, rows_of(dattn, at, Rq), wo)
    dkv, *grads = lax.optimization_barrier((dkv, *grads))
    dkv = dkv.reshape(back + 1, R, LANES)
    dkv_out = jnp.stack([dkv[back - d] for d in range(back + 1)]).astype(bf16)
    kin, yfar = halo_back(dkv_out, yfar, nz, nb, rp, back, 6)
    ok = [(z + d < nz) if d else (part != p) for d in range(back + 1) for p in range(rp)]
    ok = jnp.stack([jnp.asarray(o).astype(jnp.int32) for o in ok] + [jnp.int32(HW + E)])
    if rp > 1:
        kin = lax.dynamic_slice_in_dim(kin, at, Rq, 1)
    turned, dw = weight_grads(
        dq, rows_of(dkv[back], at, Rq), kin, ok, [rows_of(t, at, Rq) for t in tables],
        rows_of(h1, at, Rq), packed, tail)
    wide = D // AUX
    dwo = dwo.astype(bf16).reshape(nz, rp, S, wide, AUX)
    dwo = jnp.transpose(dwo, (0, 1, 3, 2, 4)).reshape(nz, rp * wide, S, AUX)
    last = jnp.concatenate([dw.reshape(nz, nb, S, AUX), dwo], axis=1)
    dh1, pin, win = reduce_last(widen(turned, at, R), packed, last, nz, nb, rp, 7)
    d_tokens, d_query, d_key, d_value, small, d_output, out, d_inner, d_outer = finish(
        dh1, tokens, gain1, dresid, pin.reshape(KV, rp, S, AUX), win, resid, ysum, yfar,
        grads + [got], leave + [sent])
    return (
        out, d_tokens, small[:, HW + E + 1], d_query, d_key, d_value, d_output,
        small[:, HW + E], small[:, HW:HW + E], d_inner, d_outer,
    )


def solution(mesh):
    both = ("ulysses", "blk")
    rows = P(both, None)
    weights = (P(both), rows, rows, rows, rows, P(both), rows, P("blk", "ulysses", None), P("blk", None, "ulysses"))
    return jax.shard_map(
        on_device,
        mesh=mesh,
        in_specs=(rows, P(), rows) + weights + (rows,),
        out_specs=(rows, rows) + weights,
        check_vma=False,
    )
```

```python
import functools
import math

import jax
import jax.numpy as jnp
from jax import lax
from jax.experimental import pallas as pl
from jax.experimental.pallas import tpu as pltpu
from jax.sharding import PartitionSpec as P

D = 1536
HEADS = 24
KV = 8
HW = 64
GROUP = HEADS // KV
FF = 512
TOPK = 8
EXP_DEV = 2
LENMAX = 4096
EPS = 1e-05
THETA = 10000.0
NEG = -1e30
LANES = 128
AUX = 384
ROUTER_AT = 320
QCOLS = GROUP * HW

f32 = jnp.float32
bf16 = jnp.bfloat16
MESH = pl.DeviceIdType.MESH
ANY = pl.BlockSpec(memory_space=pl.ANY)
VMEM = pl.BlockSpec(memory_space=pltpu.VMEM)
DMA = pltpu.SemaphoreType.DMA
MIB = 1 << 20
NO_COST = pl.CostEstimate(flops=0, bytes_accessed=0, transcendentals=0)


def dev(u, b):
    return {"ulysses": u, "blk": b}


def remote(src, dst, ss, rs, u, b):
    return pltpu.make_async_remote_copy(
        src_ref=src, dst_ref=dst, send_sem=ss, recv_sem=rs,
        device_id=dev(u, b), device_id_type=MESH,
    )


def signal(sem, u, b):
    pl.semaphore_signal(sem, inc=1, device_id=dev(u, b), device_id_type=MESH)


class Layer:
    def __init__(self, nb):
        self.u = lax.axis_index("ulysses")
        self.b = lax.axis_index("blk")
        self.nb = nb
        self.nc = nb // 2
        self.chip = self.b // 2
        self.core = lax.rem(self.b, 2)
        self.sib = self.chip * 2 + 1 - self.core

    def peer(self, i):
        return lax.rem(self.chip + i, self.nc) * 2 + self.core

    def unit(self, j):
        if self.nc != 4:
            return lax.rem(self.chip + self.nc - j, self.nc)
        x, y = lax.rem(self.chip, 2), self.chip // 2
        jx, jy = j % 2, j // 2
        return x + jx - 2 * x * jx + 2 * (y + jy - 2 * y * jy)

    def far(self, j):
        return self.unit(j) * 2 + self.core

    def across(self, d):
        at = self.u
        for k in range(d.bit_length()):
            if (d >> k) & 1:
                at = at + (1 << k) - (2 << k) * lax.rem(self.u // (1 << k), 2)
        return at

    def enter(self, flips=()):
        bar = pltpu.get_barrier_semaphore()
        for i in range(1, self.nc):
            signal(bar, self.u, self.peer(i))
        signal(bar, self.u, self.sib)
        for d in flips:
            signal(bar, self.across(d), self.b)
        pl.semaphore_wait(bar, self.nc + len(flips))


class Gather:
    def __init__(self, me, src, dst, sems):
        self.me, self.src, self.dst, self.sems = me, src, dst, sems
        self.quad = me.nc == 4
        half = dst.shape[1] // 2
        self.a, self.b = pl.ds(0, half), pl.ds(half, half)

    @staticmethod
    def scratch(nb, *lead):
        return DMA(lead + (2, 10 if nb == 8 else nb))

    def copy(self, k):
        me, src, dst = self.me, self.src, self.dst
        send = lambda s, d, to: remote(s, d, self.sems.at[0, k], self.sems.at[1, k], me.u, to)
        same = lambda at, to: send(dst.at[at], dst.at[at], to)
        part = lambda at, rows, to: send(dst.at[at, rows], dst.at[at, rows], to)
        if self.quad:
            if k < 4:
                rows = self.b if k % 2 else self.a
                return send(src.at[rows], dst.at[me.b, rows], me.far(1 + k // 2))
            if k < 6:
                return part(me.far(k - 3), self.b if k == 5 else self.a, me.far(6 - k))
            if k == 6:
                return send(src, dst.at[me.b], me.sib)
            return same(me.far(k - 6), me.sib)
        if k < me.nc:
            return send(src, dst.at[me.b], me.peer(k))
        if k == me.nc:
            return send(src, dst.at[me.b], me.sib)
        return same(me.far(k - me.nc), me.sib)

    def start(self):
        if self.quad:
            for k in (0, 3, 1, 2, 6):
                self.copy(k).start()
        else:
            for k in range(1, self.me.nc + 1):
                self.copy(k).start()

    def relay1(self):
        if self.quad:
            self.copy(0).wait_recv()
            self.copy(4).start()
            self.copy(3).wait_recv()
            self.copy(5).start()

    def relay2(self):
        if self.quad:
            self.copy(1).wait_recv()
            self.copy(7).start()
            self.copy(2).wait_recv()
            self.copy(8).start()
        else:
            for k in range(1, self.me.nc):
                self.copy(k).wait_recv()
                self.copy(self.me.nc + k).start()

    def relay3(self):
        if self.quad:
            self.copy(4).wait_recv()
            self.copy(5).wait_recv()
            self.copy(9).start()

    def passed(self, j):
        self.copy((6 if self.quad else self.me.nc) + j).wait_recv()

    def sent(self):
        for k in range(10) if self.quad else range(1, 2 * self.me.nc):
            self.copy(k).wait_send()

    def rest(self):
        self.relay1()
        self.relay2()
        self.relay3()

    def finish(self):
        for j in range(self.me.nc):
            self.passed(j)
        self.sent()


class Reduce:
    def __init__(self, me, get, source, sib_in, snd, land, sems):
        self.me, self.get, self.source = me, get, source
        self.sib_in, self.snd, self.land, self.sems = sib_in, snd, land, sems
        self.quad = me.nc == 4
        self.rows = sib_in.shape[1]
        half = self.rows // 2
        self.a, self.b = pl.ds(0, half), pl.ds(half, half)
        self.order = (3, 1, 2, 0) if self.quad else (*range(1, me.nc), 0)

    @staticmethod
    def scratch(nb, rows, cols, *lead):
        nc = nb // 2
        shape = lead + ((6, rows // 2, cols) if nc == 4 else (nc, rows, cols))
        return [
            pltpu.VMEM(lead + (nc, rows, cols), bf16), pltpu.VMEM(shape, bf16), pltpu.VMEM(shape, bf16),
            DMA(lead + (2, 10 if nc == 4 else 2 * nc)),
        ]

    def copy(self, k):
        me = self.me
        ss, rs = self.sems.at[0, k], self.sems.at[1, k]
        if k < me.nc:
            return remote(self.source(k), self.sib_in.at[k], ss, rs, me.u, me.sib)
        k = k - me.nc
        to = me.far((1, 1, 2, 2, 2, 1)[k] if self.quad else k)
        return remote(self.snd.at[k], self.land.at[k], ss, rs, me.u, to)

    def start(self, j):
        self.copy(j).start()

    def part(self, j, rows):
        return self.get(j, rows) + self.sib_in[j, rows].astype(f32)

    def send(self, k, value):
        self.snd[k] = value.astype(bf16)
        self.copy(self.me.nc + k).start()

    def phase1(self, j):
        self.copy(j).wait_recv()
        if not self.quad:
            self.send(j, self.part(j, pl.ds(0, self.rows)))
            return
        if j != 2:
            self.send(0 if j == 1 else 1, self.part(j, self.a))
        if j != 1:
            self.send(2 if j == 2 else 3, self.part(j, self.b))

    def landed(self, k):
        self.copy(self.me.nc + k).wait_recv()
        return self.land[k].astype(f32)

    def phase2(self):
        if self.quad:
            self.send(4, self.part(2, self.a) + self.landed(1))
            self.send(5, self.part(1, self.b) + self.landed(3))

    def end(self, write):
        self.copy(0).wait_recv()
        if self.quad:
            write(self.a, self.part(0, self.a) + self.landed(0) + self.landed(4))
            write(self.b, self.part(0, self.b) + self.landed(2) + self.landed(5))
        else:
            total = self.part(0, pl.ds(0, self.rows))
            for j in range(1, self.me.nc):
                total = total + self.landed(j)
            write(pl.ds(0, self.rows), total)

    def sent(self):
        for k in range(10) if self.quad else (*range(self.me.nc + 1), *range(self.me.nc + 1, 2 * self.me.nc)):
            if self.quad or k != self.me.nc:
                self.copy(k).wait_send()


def made(me, block, mine, sib_out, sib_in, snd, land, sems, waits=True):
    red = Reduce(me, lambda j, rows: mine[j, rows], lambda j: sib_out.at[j], sib_in, snd, land, sems)
    for j in red.order:
        sib_out[j] = block(me.unit(j) * 2 + 1 - me.core).astype(bf16)
        red.start(j)
    for j in red.order:
        mine[j] = block(me.far(j))
        if j and waits:
            red.phase1(j)
    return red


def made_scratch(nb, rows, cols):
    nc = nb // 2
    return [pltpu.VMEM((nc, rows, cols), f32), pltpu.VMEM((nc, rows, cols), bf16)] + Reduce.scratch(nb, rows, cols)


def keep(me, src, dst, sem):
    c = pltpu.make_async_copy(src, dst.at[me.b], sem)
    c.start()
    return c


def gather_inputs(x, pieces, wo, gm, expert, swap_d, nz, nb, cid):
    groups, shard, _ = pieces.shape
    rp = nb // groups
    n_o = QCOLS // shard
    n = nz * nb

    def kernel(x_ref, p_ref, w_ref, g_ref, e_ref, xo, po, wo_out, go, gx, eo, gs, ps, pr, zs, zr, ws, wr, ls):
        me = Layer(nb)
        lin = me.u * nb + me.b
        u, b = me.u, me.b
        bar = pltpu.get_barrier_semaphore()

        @pl.loop(1, n)
        def _(i):
            t = lax.rem(lin + i, n)
            signal(bar, t // nb, lax.rem(t, nb))

        pl.semaphore_wait(bar, n - 1)

        def piece(i):
            tb = lax.rem(b + i, nb)
            return remote(p_ref.at[tb // rp], po.at[u, b], ps.at[i], pr.at[i], u, tb)

        for i in range(1, nb):
            piece(i).start()
        own = pltpu.make_async_copy(p_ref.at[b // rp], po.at[u, b], ls.at[0])
        own.start()
        g = Gather(me, x_ref, xo, gs.at[0])
        g.start()
        cot = Gather(me, g_ref, go, gs.at[1])
        for i in range(1, nb):
            piece(i).wait()
        own.wait()

        def up(k):
            o = u - k + 1
            return remote(po.at[o], po.at[o], zs.at[0, k], zr.at[0, k], u + 1, b)

        def down(k):
            o = u + k - 1
            return remote(po.at[o], po.at[o], zs.at[1, k], zr.at[1, k], u - 1, b)

        def here(way, k):
            remote(po.at[u], po.at[u], zs.at[way, k], zr.at[way, k], u, me.sib).wait_recv()

        def relay(k):
            if k > 1:
                pl.when(u >= k - 1)(lambda: here(0, k - 1))
                pl.when(u + k - 1 < nz)(lambda: here(1, k - 1))
            pl.when((u >= k - 1) & (u + 1 < nz))(lambda: up(k).start())
            pl.when((u + k - 1 < nz) & (u > 0))(lambda: down(k).start())

        relay(1)
        hg = lin // n_o
        slot = lax.rem(lin, n_o)

        def weight(zo, p):
            tz, tb = lax.rem(u + zo, nz), hg * rp + p
            return tb, remote(w_ref, wo_out.at[slot], ws.at[zo * rp + p], wr.at[slot], tz, tb)

        g.relay1()
        for k in range(2, nz):
            relay(k)
            if k == 2:
                g.relay2()
                cot.start()
        stay = pltpu.make_async_copy(w_ref, wo_out.at[slot], ls.at[1])
        for zo in range(nz):
            for p in range(rp):
                tb, c = weight(zo, p)
                if zo:
                    c.start()
                else:
                    pl.when(tb != b)(c.start)
                    pl.when(tb == b)(stay.start)
        mate = remote(g_ref, gx, ls.at[4], ls.at[5], me.across(1), b)
        mate.start()
        half = remote(e_ref, eo, ls.at[6], ls.at[7], me.across(swap_d), b)
        half.start()
        xk = keep(me, x_ref, xo, ls.at[2])
        gk = keep(me, g_ref, go, ls.at[3])
        g.relay3()
        cot.rest()
        g.finish()
        cot.finish()
        pl.when(u >= nz - 1)(lambda: here(0, nz - 1))
        pl.when(u + nz - 1 < nz)(lambda: here(1, nz - 1))
        for k in range(1, nz):
            pl.when((u >= k - 1) & (u + 1 < nz))(lambda k=k: up(k).wait_send())
            pl.when((u + k - 1 < nz) & (u > 0))(lambda k=k: down(k).wait_send())
        for zo in range(nz):
            for p in range(rp):
                tb, c = weight(zo, p)
                if zo:
                    c.wait_send()
                else:
                    pl.when(tb != b)(c.wait_send)
                    pl.when(tb == b)(stay.wait)
        for j in range(n_o):
            src = (b // rp) * n_o + j
            c = remote(w_ref, wo_out.at[j], ws.at[0], wr.at[j], u, me.sib)
            pl.when(src != lin)(c.wait_recv)
        for c in (mate, half, xk, gk):
            c.wait()

    sh = jax.ShapeDtypeStruct
    return pl.pallas_call(
        kernel,
        out_shape=(
            sh((nb,) + x.shape, x.dtype), sh((nz, nb, shard, AUX), bf16), sh((n_o, shard, D), bf16),
            sh((nb,) + gm.shape, gm.dtype), sh(gm.shape, gm.dtype), sh(expert.shape, bf16),
        ),
        in_specs=[ANY] * 5,
        out_specs=(ANY,) * 6,
        scratch_shapes=[Gather.scratch(nb, 2)]
        + [DMA((nb,))] * 2
        + [DMA((2, nz))] * 2
        + [DMA((nz * rp,)), DMA((n_o,)), DMA((8,))],
        compiler_params=pltpu.CompilerParams(collective_id=cid, has_side_effects=True),
        cost_estimate=NO_COST,
        name="gather_inputs",
    )(x, pieces, wo, gm, expert)


def halo_forward(kv, gx, nz, nb, back, cid):
    def kernel(x_ref, g_ref, o_ref, go, ks, kr, gs, ls):
        me = Layer(nb)
        u, b = me.u, me.b
        bar = pltpu.get_barrier_semaphore()
        for d in range(1, nz):
            signal(bar, lax.rem(u + d, nz), b)
        for i in range(1, me.nc):
            signal(bar, u, me.peer(i))
        signal(bar, u, me.sib)
        pl.semaphore_wait(bar, nz - 1 + me.nc)

        def copy(d):
            src = x_ref if d == 1 else o_ref.at[d - 2]
            return remote(src, o_ref.at[d - 1], ks.at[d - 1], kr.at[d - 1], u + 1, b)

        def here(d):
            remote(x_ref, o_ref.at[d - 1], ks.at[d - 1], kr.at[d - 1], u, me.sib).wait_recv()

        def relay(d):
            if d > 1:
                pl.when(u >= d - 1)(lambda: here(d - 1))
            pl.when((u >= d - 1) & (u + 1 < nz))(lambda: copy(d).start())

        relay(1)
        g = Gather(me, g_ref, go, gs)
        g.start()
        own = keep(me, g_ref, go, ls)
        for d in range(2, back + 1):
            relay(d)
        g.rest()
        g.finish()
        own.wait()
        pl.when(u >= back)(lambda: here(back))
        for d in range(1, back + 1):
            pl.when((u >= d - 1) & (u + 1 < nz))(lambda d=d: copy(d).wait_send())

    sh = jax.ShapeDtypeStruct
    return pl.pallas_call(
        kernel,
        out_shape=(sh((back,) + kv.shape, kv.dtype), sh((nb,) + gx.shape, gx.dtype)),
        in_specs=[ANY] * 2,
        out_specs=(ANY,) * 2,
        scratch_shapes=[DMA((back,))] * 2 + [Gather.scratch(nb), DMA],
        compiler_params=pltpu.CompilerParams(collective_id=cid, has_side_effects=True),
        cost_estimate=NO_COST,
        name="halo_forward",
    )(kv, gx)


def pair_of(me, p_ref, sib_in, snd, land, sems):
    def one(h):
        return Reduce(
            me, lambda j, rows: p_ref[h, me.far(j), rows].astype(f32),
            lambda j: p_ref.at[h, me.unit(j) * 2 + 1 - me.core],
            sib_in.at[h], snd.at[h], land.at[h], sems.at[h])
    return one(0), one(1)


def write_to(ref, *lead):
    def write(rows, value):
        ref[(*lead, rows)] = value.astype(ref.dtype)
    return write


def add_to(ref, other, at):
    def write(rows, value):
        ref[rows] = value + other[at, rows].astype(f32)
    return write


def reduce_product(lhs, rhs, nb, cid):
    rows = lhs.shape[0] // nb
    cols = rhs.shape[1]

    def kernel(l_ref, r_ref, o_ref, *scratch):
        me = Layer(nb)
        me.enter()

        def block(t):
            part = l_ref[pl.ds(pl.multiple_of(t * rows, rows), rows), :]
            return jnp.dot(part, r_ref[...], preferred_element_type=f32)

        red = made(me, block, *scratch)
        red.phase2()
        red.end(write_to(o_ref))
        red.sent()

    return pl.pallas_call(
        kernel,
        out_shape=jax.ShapeDtypeStruct((rows, cols), f32),
        in_specs=[VMEM, VMEM],
        out_specs=VMEM,
        scratch_shapes=made_scratch(nb, rows, cols),
        compiler_params=pltpu.CompilerParams(
            collective_id=cid, has_side_effects=True, vmem_limit_bytes=48 * MIB
        ),
        cost_estimate=NO_COST,
        name="reduce_product",
    )(lhs, rhs)


def middle(x, ypart, nb, cid):
    _, _, rows, cols = ypart.shape

    def kernel(x_ref, y_ref, xo, o_ref, z_ref, gs, ls, *pair):
        me = Layer(nb)
        me.enter()
        g = Gather(me, x_ref, xo, gs)
        g.start()
        r0, r1 = pair_of(me, y_ref, *pair)
        for r in (r1, r0):
            for j in r.order:
                r.start(j)
        own = keep(me, x_ref, xo, ls)
        for j in r1.order[:-1]:
            r1.phase1(j)
        g.rest()
        r1.phase2()
        for j in r0.order[:-1]:
            r0.phase1(j)
        r0.phase2()
        r1.end(write_to(z_ref))
        g.finish()
        r0.end(write_to(o_ref))
        r0.sent()
        r1.sent()
        own.wait()

    sh = jax.ShapeDtypeStruct
    return pl.pallas_call(
        kernel,
        out_shape=(sh((nb,) + x.shape, x.dtype), sh((rows, cols), f32), sh((rows, cols), bf16)),
        in_specs=[ANY, VMEM],
        out_specs=(ANY, VMEM, VMEM),
        scratch_shapes=[Gather.scratch(nb), DMA]
        + Reduce.scratch(nb, rows, cols, 2),
        compiler_params=pltpu.CompilerParams(
            collective_id=cid, has_side_effects=True, vmem_limit_bytes=56 * MIB
        ),
        cost_estimate=NO_COST,
        name="middle",
    )(x, ypart)


def halo_back(dkv, yfar, nz, nb, rp, back, cid):
    R = dkv.shape[1]

    def kernel(d_ref, y_ref, kin, yo, ks, kr, ys):
        me = Layer(nb)
        first = (me.b // rp) * rp
        part = lax.rem(me.b, rp)
        bar = pltpu.get_barrier_semaphore()
        others = [(zo, p) for zo in range(nz) for p in range(rp) if zo or p]
        for zo, p in others:
            signal(bar, lax.rem(me.u + zo, nz), first + lax.rem(part + p, rp))
        pl.semaphore_wait(bar, len(others))

        def copy(d, p):
            k = d * rp + p
            return remote(d_ref.at[d], kin.at[d * rp + part], ks.at[k], kr.at[d * rp + part], me.u - d, first + p)

        def arrival(d, p):
            k = d * rp + p
            return remote(d_ref.at[d], kin.at[k], ks.at[k], kr.at[k], me.u, me.sib)

        for d in range(back + 1):
            for p in range(rp):
                if d:
                    pl.when(me.u >= d)(lambda d=d, p=p: copy(d, p).start())
                elif rp > 1:
                    pl.when(part != p)(lambda d=d, p=p: copy(d, p).start())
        mate = remote(y_ref, yo, ys.at[0], ys.at[1], me.across(1), me.b)
        mate.start()
        for d in range(back + 1):
            for p in range(rp):
                if d:
                    pl.when(me.u >= d)(lambda d=d, p=p: copy(d, p).wait_send())
                    pl.when(me.u + d < nz)(lambda d=d, p=p: arrival(d, p).wait_recv())
                elif rp > 1:
                    pl.when(part != p)(lambda d=d, p=p: copy(d, p).wait_send())
                    pl.when(part != p)(lambda d=d, p=p: arrival(d, p).wait_recv())
        mate.wait()

    return pl.pallas_call(
        kernel,
        out_shape=(
            jax.ShapeDtypeStruct(((back + 1) * rp, R, LANES), bf16), jax.ShapeDtypeStruct(yfar.shape, bf16),
        ),
        in_specs=[ANY] * 2,
        out_specs=(ANY,) * 2,
        scratch_shapes=[DMA(((back + 1) * rp,))] * 2 + [DMA((2,))],
        compiler_params=pltpu.CompilerParams(collective_id=cid, has_side_effects=True),
        cost_estimate=NO_COST,
        name="halo_back",
    )(dkv, yfar)


def reduce_last(lhs, rhs, pieces, nz, nb, rp, cid):
    rows = lhs.shape[0] // nb
    cols = rhs.shape[0]
    _, count, shard, width = pieces.shape
    n_o = nz * rp
    wide = (count - nb) // rp
    n = nz * nb

    def kernel(l_ref, r_ref, p_ref, o_ref, pin, win, land, tmp, total, zs, zr, ps, pr, ws, wr, ls, *scratch):
        me = Layer(nb)
        u = me.u
        lin = u * nb + me.b
        part = lax.rem(me.b, rp)
        bar = pltpu.get_barrier_semaphore()

        @pl.loop(1, n)
        def _(i):
            t = lax.rem(lin + i, n)
            signal(bar, t // nb, lax.rem(t, nb))

        pl.semaphore_wait(bar, n - 1)

        chunk = count // 2
        part_of = lambda c: pl.ds(c * chunk, chunk)

        def hop(way, o, c):
            to = u - 1 if way == 0 else u + 1
            return remote(tmp.at[way, o, part_of(c)], land.at[way, o, part_of(c)],
                          zs.at[way, o, c], zr.at[way, o, c], to, me.b)

        def ends(way, o):
            def run():
                for c in range(2):
                    tmp[way, o, part_of(c)] = p_ref[o, part_of(c)]
                    hop(way, o, c).start()
            return run

        def passes(way, o):
            def run():
                for c in range(2):
                    hop(way, o, c).wait_recv()

                    @pl.loop(c * chunk, (c + 1) * chunk)
                    def _(t):
                        tmp[way, o, t] = (p_ref[o, t].astype(f32) + land[way, o, t].astype(f32)).astype(bf16)

                    hop(way, o, c).start()
            return run

        def down(o):
            return u > o

        def up(o):
            return u < o

        ways = [(0, o) for o in range(nz - 1)], [(1, o) for o in range(nz - 1, 0, -1)]
        for way, o in ways[0] + ways[1]:
            pl.when(u == (0 if way else nz - 1))(ends(way, o))

        def relay(way, o):
            inner = (u > 0) & (u < nz - 1) & (up(o) if way else down(o))
            return inner, passes(way, o)

        low = 2 * u < nz - 1

        def relays(lo, hi, near):
            for way in range(2):
                mine = low if (way == 1) == near else jnp.logical_not(low)
                for way_o in ways[way][lo:hi]:
                    inner, run = relay(*way_o)
                    pl.when(mine & inner)(run)

        def block(t):
            rows_t = l_ref[pl.ds(pl.multiple_of(t * rows, rows), rows), :]
            return lax.dot_general(rows_t, r_ref[...], NT, preferred_element_type=f32)

        red = made(me, block, *scratch, waits=False)
        relays(0, 1, True)
        for j in red.order[:-1]:
            red.phase1(j)
        relays(1, nz, True)
        red.phase2()
        relays(0, nz, False)

        def here(way):
            def run():
                for c in range(2):
                    at = tmp.at[way, u, part_of(c)]
                    remote(at, at, zs.at[way, u, c], zr.at[way, u, c], u, me.sib).wait_recv()
            pl.when((u > 0) if way else (u < nz - 1))(run)

        here(0)
        here(1)

        @pl.loop(0, count)
        def _(t):
            tile = p_ref[u, t].astype(f32)
            tile = tile + jnp.where(u < nz - 1, land[0, u, t].astype(f32), 0.0)
            total[t] = (tile + jnp.where(u > 0, land[1, u, t].astype(f32), 0.0)).astype(bf16)

        out = []
        for i in range(1, nb):
            t = lax.rem(me.b + i, nb)
            c = remote(total.at[t], pin.at[me.b], ps.at[i], pr.at[i], u, t)
            c.start()
            out.append(c)
        own = pltpu.make_async_copy(total.at[me.b], pin.at[me.b], ls.at[0])
        own.start()

        def weight(p):
            t = (me.b // rp) * n_o + u * rp + p
            src = total.at[pl.ds(nb + p * wide, wide)]
            return t, remote(src, win.at[part], ws.at[p], wr.at[part], t // nb, lax.rem(t, nb))

        stay = lambda p: pltpu.make_async_copy(total.at[pl.ds(nb + p * wide, wide)], win.at[part], ls.at[1])
        for p in range(rp):
            t, c = weight(p)
            pl.when(t != lin)(c.start)
            pl.when(t == lin)(stay(p).start)
        red.end(write_to(o_ref))
        red.sent()
        for way, o in ways[0] + ways[1]:
            for c in range(2):
                pl.when(up(o) if way else down(o))(lambda way=way, o=o, c=c: hop(way, o, c).wait_send())
        for c in out:
            c.wait()
        own.wait()
        for p in range(rp):
            t, c = weight(p)
            pl.when(t != lin)(c.wait_send)
            pl.when(t == lin)(stay(p).wait)
        hg = lin // n_o
        layer = lax.rem(lin, n_o) // rp
        for p in range(rp):
            c = remote(total.at[pl.ds(nb, wide)], win.at[p], ws.at[0], wr.at[p], u, me.sib)
            pl.when(layer * nb + hg * rp + p != lin)(c.wait_recv)

    sh = jax.ShapeDtypeStruct
    return pl.pallas_call(
        kernel,
        out_shape=(
            sh((rows, cols), f32), sh((nb, shard, width), bf16), sh((rp, wide, shard, width), bf16),
        ),
        in_specs=[VMEM, VMEM, VMEM],
        out_specs=(VMEM, ANY, ANY),
        scratch_shapes=[pltpu.VMEM((2, nz, count, shard, width), bf16)] * 2
        + [pltpu.VMEM((count, shard, width), bf16)]
        + [DMA((2, nz, 2))] * 2
        + [DMA((nb,))] * 2
        + [DMA((rp,))] * 2
        + [DMA((2,))]
        + made_scratch(nb, rows, cols),
        compiler_params=pltpu.CompilerParams(
            collective_id=cid, has_side_effects=True, vmem_limit_bytes=56 * MIB
        ),
        cost_estimate=NO_COST,
        name="reduce_last",
    )(lhs, rhs, pieces)


def turn(a, c, s1, s2):
    return a * c + pltpu.roll(a, LANES - HW // 2, 1) * s1 + pltpu.roll(a, HW // 2, 1) * s2


def turn_back(a, c, s1, s2):
    return a * c - pltpu.roll(a, LANES - HW // 2, 1) * s1 - pltpu.roll(a, HW // 2, 1) * s2


def swap(a):
    return pltpu.roll(a, HW, 1)


def low_half():
    return lax.broadcasted_iota(jnp.int32, (1, LANES), 1) < HW


def row_block(step, width):
    return pl.BlockSpec((step, width), lambda i: (i, 0))


def whole_block(a):
    zeros = (0,) * a.ndim
    return pl.BlockSpec(a.shape, lambda i: zeros)


def prepare(w_query, w_key, w_value, extra, gains, w_inner, w_outer, cotangent, routes):
    S = w_query.shape[0]
    T = routes.shape[0]
    dz = w_inner.shape[1]
    W = 3 * FF
    half = W // 2

    ins = (w_query, w_key, w_value, extra[0], gains, w_inner, w_outer, cotangent, routes)

    def kernel(*refs):
        n, m = len(ins), len(outs)
        hbm, (isem, osem), vmem = refs[:n + m], refs[n + m:n + m + 2], refs[n + m + 2:]
        loads = [pltpu.make_async_copy(hbm[k], vmem[k], isem.at[k]) for k in range(n)]
        for c in loads:
            c.start()
        q_ref, k_ref, v_ref, x_ref, n_ref, i_ref, o_ref, c_ref, r_ref = vmem[:n]
        p_ref, g_ref, a_ref, b_ref, f_ref = vmem[n:]
        saves = [pltpu.make_async_copy(vmem[n + k], hbm[n + k], osem.at[k]) for k in range(m)]
        for c in loads:
            c.wait()
        low = low_half()
        lane = lax.broadcasted_iota(jnp.int32, (1, LANES), 1)

        def low64(ref, at):
            a = ref[:, at // LANES * LANES:at // LANES * LANES + LANES].astype(f32)
            return swap(a) if at % LANES else a

        spread = lax.broadcasted_iota(jnp.int32, (S, S), 0) == lax.broadcasted_iota(jnp.int32, (S, S), 1)
        tail = x_ref[...].astype(f32)
        for i in range(2):
            column = jnp.sum(jnp.where(spread, n_ref[i:i + 1, :], 0.0), axis=1, keepdims=True)
            tail = jnp.where(lane == r_first + i, column, tail)
        for h in range(KV):
            at = h * QCOLS
            two = lambda a, b: jnp.where(low, a, swap(b)).astype(bf16)
            p_ref[h, :, :LANES] = two(low64(q_ref, at), low64(q_ref, at + HW))
            p_ref[h, :, LANES:2 * LANES] = two(low64(q_ref, at + 2 * HW), low64(k_ref, h * HW))
            p_ref[h, :, 2 * LANES:] = jnp.where(low, low64(v_ref, h * HW), tail).astype(bf16)
        saves[0].start()
        g_ref[:, :D] = c_ref[...]
        named = r_ref[:, 0:1] + HW == lane
        for j in range(1, TOPK):
            named = named | (r_ref[:, j:j + 1] + HW == lane)
        g_ref[:, D:] = jnp.where(named, 1.0, 0.0).astype(bf16)
        saves[1].start()
        odd = lax.rem(lax.axis_index("ulysses"), 2)
        same, outer = i_ref[odd], o_ref[odd].astype(f32).T.astype(bf16)
        a_ref[...] = same[:, :half]
        b_ref[:, :2 * FF - half] = same[:, half:]
        b_ref[:, 2 * FF - half:] = outer
        f_ref[:, :2 * FF] = i_ref[1 - odd]
        f_ref[:, 2 * FF:] = o_ref[1 - odd].astype(f32).T.astype(bf16)
        for c in saves[2:]:
            c.start()
        for c in saves:
            c.wait()

    r_first = extra[1]
    sh = lambda *shape: jax.ShapeDtypeStruct(shape, bf16)
    outs = (sh(KV, S, AUX), sh(T, D + LANES), sh(dz, half), sh(dz, half), sh(dz, W))
    return pl.pallas_call(
        kernel,
        out_shape=outs,
        in_specs=[ANY] * len(ins),
        out_specs=(ANY,) * len(outs),
        scratch_shapes=[DMA((len(ins),)), DMA((len(outs),))]
        + [pltpu.VMEM(a.shape, a.dtype) for a in (*ins, *outs)],
        compiler_params=pltpu.CompilerParams(vmem_limit_bytes=48 * MIB),
        cost_estimate=NO_COST,
        name="prepare",
    )(*ins)


def project(x, gain, packed, c, s1, s2):
    R = x.shape[0]
    step = 256

    def kernel(x_ref, g_ref, w_ref, c_ref, a_ref, b_ref, q_ref, kv_ref, h_ref):
        v = x_ref[...].astype(f32)
        inv = lax.rsqrt(jnp.mean(v * v, axis=1, keepdims=True) + EPS)
        h = (v * inv * g_ref[...]).astype(bf16)
        h_ref[...] = h
        out = jnp.dot(h, w_ref[...], preferred_element_type=f32)
        tables = (c_ref[...], a_ref[...], b_ref[...])
        low = low_half()
        t0 = turn(out[:, :LANES], *tables)
        t1 = turn(out[:, LANES:2 * LANES], *tables)
        scale = lambda a: (jnp.where(low, a, 0.0) * (1.0 / math.sqrt(HW))).astype(bf16)
        q_ref[0] = scale(t0)
        q_ref[1] = scale(swap(t0))
        q_ref[2] = scale(t1)
        kv_ref[...] = jnp.where(low, swap(t1), swap(out[:, 2 * LANES:])).astype(bf16)

    sh = jax.ShapeDtypeStruct
    return pl.pallas_call(
        kernel,
        grid=(R // step,),
        out_shape=(sh((GROUP, R, LANES), bf16), sh((R, LANES), bf16), sh((R, D), bf16)),
        in_specs=[row_block(step, D), whole_block(gain), whole_block(packed)] + [row_block(step, LANES)] * 3,
        out_specs=(
            pl.BlockSpec((GROUP, step, LANES), lambda i: (0, i, 0)),
            row_block(step, LANES),
            row_block(step, D),
        ),
        compiler_params=pltpu.CompilerParams(vmem_limit_bytes=32 * MIB),
        cost_estimate=NO_COST,
        name="project",
    )(x, gain, packed, c, s1, s2)


BQ = 256
BK = 512
NT = (((1,), (1,)), ((), ()))
NN = (((1,), (0,)), ((), ()))
TN = (((0,), (0,)), ((), ()))


def mm(a, b, dims=NN):
    return lax.dot_general(a, b, dims, preferred_element_type=f32)


def seen(meta, st, i, kb, nq):
    qpos = meta[nq] + i * BQ + lax.broadcasted_iota(jnp.int32, (BQ, 1), 0)
    kpos = kb * BK + lax.broadcasted_iota(jnp.int32, (1, BK), 1)
    return ((kpos <= qpos) & (kpos >= st))[None]


def attend(q, kv, starts, meta):
    _, Rq, _ = q.shape
    nq = Rq // BQ
    M = GROUP * BQ

    def kernel(meta, q_ref, kv_ref, st_ref, o_ref, l_ref):
        i = pl.program_id(0)
        qv = q_ref[...].reshape(M, LANES)
        st = st_ref[...]
        last = (meta[nq] + i * BQ + BQ - 1) // BK + 1

        def step(kb, carry):
            m, l, acc = carry
            keys = kv_ref[pl.ds(pl.multiple_of(kb * BK, BK), BK), :]
            s = mm(qv, keys, NT).reshape(GROUP, BQ, BK)
            s = jnp.where(seen(meta, st, i, kb, nq), s, NEG)
            m2 = jnp.maximum(m, jnp.max(s, axis=2, keepdims=True))
            w = jnp.exp(s - m2)
            f = jnp.exp(m - m2)
            l = l * f + jnp.sum(w, axis=2, keepdims=True)
            pv = mm(w.astype(bf16).reshape(M, BK), keys)
            return m2, l, acc * f + pv.reshape(GROUP, BQ, LANES)

        init = (
            jnp.full((GROUP, BQ, 1), NEG, f32),
            jnp.zeros((GROUP, BQ, 1), f32),
            jnp.zeros((GROUP, BQ, LANES), f32),
        )
        m, l, acc = lax.fori_loop(meta[i], last, step, init)
        o = acc / l
        o_ref[:, :LANES] = jnp.where(low_half(), swap(o[0]), o[1]).astype(bf16)
        o_ref[:, LANES:] = swap(o[2])[:, :HW].astype(bf16)
        l_ref[...] = m + jnp.log(l)

    sh = jax.ShapeDtypeStruct
    blk = lambda w: pl.BlockSpec((GROUP, BQ, w), lambda i, m: (0, i, 0))
    return pl.pallas_call(
        kernel,
        grid_spec=pltpu.PrefetchScalarGridSpec(
            num_scalar_prefetch=1,
            grid=(nq,),
            in_specs=[
                blk(LANES),
                pl.BlockSpec(kv.shape, lambda i, m: (0, 0)),
                pl.BlockSpec((BQ, 1), lambda i, m: (i, 0)),
            ],
            out_specs=(pl.BlockSpec((BQ, QCOLS), lambda i, m: (i, 0)), blk(1)),
        ),
        out_shape=(sh((Rq, QCOLS), bf16), sh((GROUP, Rq, 1), f32)),
        compiler_params=pltpu.CompilerParams(vmem_limit_bytes=48 * MIB),
        cost_estimate=NO_COST,
        name="attend",
    )(meta, q, kv, starts)


def attend_back(q, kv, starts, meta, lse, mixed, dattn, wo):
    _, Rq, _ = q.shape
    nq = Rq // BQ
    M = GROUP * BQ
    K = kv.shape[0]

    def kernel(meta, q_ref, kv_ref, st_ref, l_ref, o_ref, g_ref, w_ref, dq_ref, dkv_ref, dw_ref):
        i = pl.program_id(0)

        @pl.when(i == 0)
        def _():
            dkv_ref[...] = jnp.zeros_like(dkv_ref)
            dw_ref[...] = jnp.zeros_like(dw_ref)

        g = g_ref[...]
        mixed = o_ref[...]
        dm = mm(g, w_ref[...], NT).astype(bf16).astype(f32)
        dw_ref[...] += mm(mixed, g, TN)
        low = low_half()
        d0 = dm[:, :LANES]
        d1 = jnp.concatenate([dm[:, LANES:], jnp.zeros((BQ, LANES - HW), f32)], axis=1)
        m0 = mixed[:, :LANES].astype(f32)
        m1 = jnp.concatenate([mixed[:, LANES:].astype(f32), jnp.zeros((BQ, LANES - HW), f32)], axis=1)
        total = lambda a: jnp.sum(a, axis=1, keepdims=True)
        e0, e1 = d0 * m0, d1 * m1
        first = total(jnp.where(low, e0, 0.0))
        delta = jnp.stack([first, total(jnp.where(low, 0.0, e0)), total(e1)])
        high = lambda a: jnp.where(low, 0.0, a).astype(bf16)
        do = jnp.concatenate([high(swap(d0)), high(d0), high(swap(d1))], axis=0)
        qv = q_ref[...].reshape(M, LANES)
        lse = l_ref[...]
        st = st_ref[...]
        last = (meta[nq] + i * BQ + BQ - 1) // BK + 1

        def step(kb, dq):
            at = pl.ds(pl.multiple_of(kb * BK, BK), BK)
            keys = kv_ref[at, :]
            s = mm(qv, keys, NT).reshape(GROUP, BQ, BK)
            p = jnp.where(seen(meta, st, i, kb, nq), jnp.exp(s - lse), 0.0)
            dp = mm(do, keys, NT).reshape(GROUP, BQ, BK)
            ds = (p * (dp - delta)).astype(bf16).reshape(M, BK)
            pb = p.astype(bf16).reshape(M, BK)
            dkv_ref[at, :] += mm(ds, qv, TN) + mm(pb, do, TN)
            return dq + mm(ds, keys)

        dq = lax.fori_loop(meta[i], last, step, jnp.zeros((M, LANES), f32))
        dq_ref[...] = (dq * (1.0 / math.sqrt(HW))).astype(bf16).reshape(GROUP, BQ, LANES)

    sh = jax.ShapeDtypeStruct
    blk = lambda w: pl.BlockSpec((GROUP, BQ, w), lambda i, m: (0, i, 0))
    rows = lambda w: pl.BlockSpec((BQ, w), lambda i, m: (i, 0))
    full = lambda *shape: pl.BlockSpec(shape, lambda i, m: (0, 0))
    return pl.pallas_call(
        kernel,
        grid_spec=pltpu.PrefetchScalarGridSpec(
            num_scalar_prefetch=1,
            grid=(nq,),
            in_specs=[
                blk(LANES), full(*kv.shape), rows(1), blk(1), rows(QCOLS), rows(D), full(QCOLS, D),
            ],
            out_specs=(blk(LANES), full(K, LANES), full(QCOLS, D)),
        ),
        out_shape=(sh((GROUP, Rq, LANES), bf16), sh((K, LANES), f32), sh((QCOLS, D), f32)),
        compiler_params=pltpu.CompilerParams(vmem_limit_bytes=48 * MIB),
        cost_estimate=NO_COST,
        name="attend_back",
    )(meta, q, kv, starts, lse, mixed, dattn, wo)


def weight_grads(dq, dkv, kin, ok, tables, h1, packed, tail):
    _, Rq, _ = dq.shape
    step = 256
    arrivals = kin.shape[0]

    def kernel(ok_ref, dq_ref, dkv_ref, kin_ref, c_ref, a_ref, b_ref, h_ref, w_ref, t_ref, o_ref, p_ref, acc):
        i = pl.program_id(0)

        @pl.when(i == 0)
        def _():
            acc[...] = jnp.zeros_like(acc)

        kv = dkv_ref[...]
        for k in range(arrivals):
            kv = kv + jnp.where(ok_ref[k] > 0, kin_ref[k].astype(f32), 0.0)
        kv = kv.astype(bf16).astype(f32)
        low = low_half()
        tables = (c_ref[...], a_ref[...], b_ref[...])
        q = [dq_ref[h].astype(f32) for h in range(GROUP)]
        kv = swap(kv)
        t0 = turn_back(jnp.where(low, q[0], swap(q[1])), *tables)
        t1 = turn_back(jnp.where(low, q[2], kv), *tables)
        out = jnp.concatenate([t0, t1, jnp.where(low, kv, 0.0)], axis=1).astype(bf16)
        o_ref[...] = out
        acc[...] += mm(h_ref[...], out, TN)

        @pl.when(i == Rq // step - 1)
        def _():
            w = w_ref[...].astype(f32)
            dw = acc[...]
            t = t_ref[...]
            lane = lax.broadcasted_iota(jnp.int32, (1, LANES), 1)
            gain = jnp.sum(jnp.where(lane == ok_ref[arrivals], w[:, 2 * LANES:], 0.0), axis=1, keepdims=True)
            d_gain = jnp.sum(w * dw, axis=1, keepdims=True) / gain
            t = t + jnp.where(lane == ok_ref[arrivals] + 1, d_gain, 0.0)
            p_ref[:, :2 * LANES] = dw[:, :2 * LANES].astype(bf16)
            p_ref[:, 2 * LANES:] = jnp.where(low, dw[:, 2 * LANES:], t).astype(bf16)

    sh = jax.ShapeDtypeStruct
    heads = lambda n: pl.BlockSpec((n, step, LANES), lambda i: (0, i, 0))
    return pl.pallas_call(
        kernel,
        grid=(Rq // step,),
        out_shape=(sh((Rq, AUX), bf16), sh((D, AUX), bf16)),
        in_specs=[pl.BlockSpec(memory_space=pltpu.SMEM), heads(GROUP), row_block(step, LANES), heads(arrivals)]
        + [row_block(step, LANES)] * 3
        + [row_block(step, D), whole_block(packed), whole_block(tail)],
        out_specs=(row_block(step, AUX), pl.BlockSpec((D, AUX), lambda i: (0, 0))),
        scratch_shapes=[pltpu.VMEM((D, AUX), f32)],
        compiler_params=pltpu.CompilerParams(vmem_limit_bytes=48 * MIB),
        cost_estimate=NO_COST,
        name="weight_grads",
    )(ok, dq, dkv, kin, *tables, h1, packed, tail)


def experts(h2_own, g_own, g_oth, router, hot, n2, inv2, gain2, cot, weights, sent, leave, nz, nb, cid):
    T = h2_own.shape[0]
    nc = nb // 2
    step = 2 * T
    units = 2 * nc
    dz = D // nz
    C = D + LANES
    W = 3 * FF
    nw = len(weights)
    ng = len(leave)
    resident = nb <= 8

    def kernel(x_ref, g0_ref, g1_ref, r_ref, e_ref, n_ref, v_ref, k_ref, c_ref, *rest):
        win = rest[:nw]
        y_ref, dr_ref, da_ref, dl_ref, dg_ref = rest[nw:nw + 5]
        rest = rest[nw + 5:]
        din, gin = rest[:ng], rest[ng]
        rest = rest[ng + 1:]
        h_all, hbuf, s_ref, part, gbuf, ybuf, wc, acc, zbuf, gs, zs, sem, gsem, ysem, *pair = rest
        me = Layer(nb)
        me.enter(sorted({1, sent[0]}))
        own, oth = h_all.at[0], h_all.at[1]
        mate = remote(x_ref, oth.at[me.b], zs.at[0], zs.at[1], me.across(1), me.b)
        mate.start()
        ga = Gather(me, x_ref, own, gs.at[0])
        gb = Gather(me, oth.at[me.b], oth, gs.at[1])
        ga.start()
        mine = pltpu.make_async_copy(x_ref, own.at[me.b], zs.at[2])
        mine.start()
        rows_at = lambda d: pl.ds(pl.multiple_of(me.across(d) * dz, dz), dz)
        loads = [
            pltpu.make_async_copy(win[k], wc.at[rows_at(d), pl.ds(c, a.shape[1])], sem.at[k])
            for k, (a, d, c) in enumerate(weights)
        ]
        for c in loads:
            c.start()

        def place(u):
            other = (u >= 2) & (u < nc + 2)
            j = jnp.where(u < 2, u, jnp.where(other, u - 2, 2 * nc + 1 - u))
            return jnp.where(other, 1, 0), j

        def cot(u, h):
            _, j = place(u)
            rows = pl.ds(pl.multiple_of(me.unit(j) * step, step), step)
            slot = lax.rem(u, 2)
            return pltpu.make_async_copy((g1_ref if h else g0_ref).at[rows], gbuf.at[slot], gsem.at[slot])

        def cot_start(u):
            h, _ = place(u)
            pl.when(h == 0)(lambda: cot(u, 0).start())
            pl.when(h == 1)(lambda: cot(u, 1).start())

        def result(u):
            h, j = place(u)
            slot = lax.rem(u, 2)
            return pltpu.make_async_copy(
                ybuf.at[slot], y_ref.at[h, pl.ds(pl.multiple_of(me.unit(j) * 2, 2), 2)], ysem.at[slot])

        cot_start(jnp.int32(0))
        acc[...] = jnp.zeros_like(acc)
        ra, rb = pair_of(me, part, *pair)
        back = remote(zbuf.at[0], zbuf.at[1], zs.at[3], zs.at[4], me.across(1), me.b)
        ga.relay1()
        for c in loads:
            c.wait()
        mine.wait()

        def at(k, f):
            def run(u):
                pl.when(u == k)(f)
            return run

        def arrive(u):
            def first():
                ga.relay2()
                mate.wait_recv()
                gb.start()

            def second():
                ga.relay3()
                gb.relay1()

            at(1, first)(u)
            at(2, second)(u)
            at(3, gb.relay2)(u)
            at(4, gb.relay3)(u)
            for k in range(units):
                h = 1 if 2 <= k < nc + 2 else 0
                j = k if k < 2 else (k - 2 if h else 2 * nc + 1 - k)
                at(k, lambda h=h, j=j: (gb if h else ga).passed(j))(u)

        def depart(u):
            for k in range(units):
                h = 1 if 2 <= k < nc + 2 else 0
                j = k if k < 2 else (k - 2 if h else 2 * nc + 1 - k)
                at(k, lambda h=h, j=j: (rb if h else ra).start(j))(u)

            def mates():
                for j in rb.order[:-1]:
                    rb.phase1(j)

            at(nc + 1, mates)(u)

            def ours():
                rb.phase2()
                ra.phase1(3)
                ra.phase1(1)

            if nc == 4:
                at(nc + 2, ours)(u)

            def across():
                rb.end(write_to(zbuf, 0))
                back.start()

            at(units - 1, across)(u)

        @pl.loop(0, units)
        def _(u):
            h, j = place(u)
            slot = lax.rem(u, 2)
            pl.when(u + 1 < units)(lambda: cot_start(u + 1))
            arrive(u)
            cot(u, 0).wait()
            pl.when(u >= 2)(lambda: result(u - 2).wait())
            two = pl.ds(pl.multiple_of(me.unit(j) * 2, 2), 2)
            if resident:
                x = h_all[h, two].reshape(step, D)
            else:
                c = pltpu.make_async_copy(h_all.at[h, two], hbuf, zs.at[5])
                c.start()
                c.wait()
                x = hbuf[...].reshape(step, D)
            hot = e_ref[...]
            mask = gbuf[slot, :, D:].astype(f32) > 0
            logits = mm(x, r_ref[...])
            top = jnp.max(jnp.where(mask, logits, NEG), axis=1, keepdims=True)
            w = jnp.where(mask, jnp.exp(jnp.where(mask, logits - top, 0.0)), 0.0)
            gate = jnp.sum(w * hot, axis=1, keepdims=True) / jnp.sum(w, axis=1, keepdims=True)
            gu = mm(x, wc[:, :2 * FF])
            a, up = gu[:, :FF], gu[:, FF:]
            sg = jax.nn.sigmoid(a)
            silu = a * sg
            act = (silu * up).astype(bf16)
            g = gbuf[slot, :, :D]
            ybuf[slot] = (gate * mm(act, wc[:, 2 * FF:], NT)).astype(bf16).reshape(2, T, D)
            result(u).start()
            raw = mm(g, wc[:, 2 * FF:])
            acc[:, 2 * FF:] += mm((gate * g.astype(f32)).astype(bf16), act, TN)
            dgate = jnp.sum(act.astype(f32) * raw, axis=1, keepdims=True)
            dact = gate * raw
            dgu = jnp.concatenate(
                [dact * up * (sg * (1.0 + a * (1.0 - sg))), dact * silu], axis=1).astype(bf16)
            acc[:, :2 * FF] += mm(x, dgu, TN)
            part[h, two, :, :D] = mm(dgu, wc[:, :2 * FF], NT).astype(bf16).reshape(2, T, D)
            hi = dgate.astype(bf16).astype(f32)
            part[h, two, :, D:] = (hi * hot + swap((dgate - hi) * hot)).astype(bf16).reshape(2, T, LANES)
            depart(u)

        for j in (2,) if nc == 4 else ra.order[:-1]:
            ra.phase1(j)
        wc[...] = acc[...].astype(bf16)
        grad = lambda d, c, width: wc.at[rows_at(d), pl.ds(c, width)]
        going = remote(grad(*sent), gin, zs.at[6], zs.at[7], me.across(sent[0]), me.b)
        going.start()
        saves = [pltpu.make_async_copy(grad(*p), din[k], sem.at[k]) for k, p in enumerate(leave)]
        for c in saves:
            c.start()
        ra.phase2()
        back.wait_recv()
        ra.end(add_to(s_ref, zbuf, 1))
        again = pltpu.make_async_copy(x_ref, hbuf.at[0], zs.at[5])
        again.start()
        again.wait()
        dgates = s_ref[:, D:] + swap(s_ref[:, D:])
        mask = c_ref[:, D:].astype(f32) > 0
        logits = mm(hbuf[0], r_ref[...])
        top = jnp.max(jnp.where(mask, logits, NEG), axis=1, keepdims=True)
        w = jnp.where(mask, jnp.exp(jnp.where(mask, logits - top, 0.0)), 0.0)
        gates = w / jnp.sum(w, axis=1, keepdims=True)
        dlogits = gates * (dgates - jnp.sum(gates * dgates, axis=1, keepdims=True))
        dlogits = dlogits.astype(bf16)
        dl_ref[...] = dlogits
        n = n_ref[...]
        dh2 = s_ref[:, :D] + mm(dlogits, r_ref[...], NT)
        dg_ref[...] = jnp.sum(dh2 * n, axis=0, keepdims=True)
        d_normed = dh2 * k_ref[...]
        dv = v_ref[...] * (d_normed - n * jnp.mean(d_normed * n, axis=1, keepdims=True))
        dresid = c_ref[:, :D].astype(f32) + dv
        dr_ref[...] = dresid
        da_ref[...] = dresid.astype(bf16)
        back.wait_send()
        mate.wait_send()
        for r in (ga, gb, ra, rb):
            r.sent()
        for c in saves:
            c.wait()
        going.wait()
        result(jnp.int32(units - 2)).wait()
        result(jnp.int32(units - 1)).wait()

    sh = jax.ShapeDtypeStruct
    v = lambda shape, kind=bf16: pltpu.VMEM(shape, kind)
    return pl.pallas_call(
        kernel,
        out_shape=(
            sh((2, nb, T, D), bf16), sh((T, D), f32), sh((T, D), bf16), sh((T, LANES), bf16), sh((1, D), f32),
        )
        + tuple(sh((dz, width), bf16) for _, _, width in leave)
        + (sh((dz, sent[2]), bf16),)
        + (() if resident else (sh((2, nb, T, D), bf16),)),
        in_specs=[ANY] * 3 + [VMEM] * 6 + [ANY] * nw,
        out_specs=(ANY,) + (VMEM,) * 4 + (ANY,) * (ng + 1 + int(not resident)),
        scratch_shapes=([v((2, nb, T, D))] if resident else [])
        + [
            v((2, T, D)), v((T, C), f32), v((2, nb, T, C)), v((2, step, C)), v((2, 2, T, D)),
            v((D, W)), v((D, W), f32), v((2, T, C)),
            Gather.scratch(nb, 2), DMA((8,)), DMA((max(nw, ng),)), DMA((2,)), DMA((2,)),
        ]
        + Reduce.scratch(nb, T, C, 2),
        compiler_params=pltpu.CompilerParams(
            collective_id=cid, has_side_effects=True, vmem_limit_bytes=60 * MIB
        ),
        cost_estimate=NO_COST,
        name="experts",
    )(h2_own, g_own, g_oth, router, hot, n2, inv2, gain2, cot, *[a for a, _, _ in weights])


def finish(dh1, x, gain, dresid, pin, win, resid, ysum, yfar, grads, places):
    T = x.shape[0]
    groups, rp, S, _ = pin.shape
    senders = win.shape[0]
    m = len(grads)
    dz = grads[0].shape[0]

    def kernel(d_ref, x_ref, g_ref, r_ref, p_ref, w_ref, s_ref, y_ref, f_ref, *rest):
        srcs = rest[:m]
        t_ref, q_ref, k_ref, v_ref, m_ref, o_ref, out_ref, in_ref, ex_ref = rest[m:]
        odd = lax.rem(lax.axis_index("ulysses"), 2)
        for e in range(2):
            at = odd if e == 0 else 1 - odd
            for c in range(0, 3 * FF, FF // 2):
                total = 0.0
                for r, (d, lo, width) in zip(srcs, places):
                    if d % 2 == e and lo <= c < lo + width:
                        total = total + r[:, c - lo:c - lo + FF // 2].astype(f32)
                if c < 2 * FF:
                    in_ref[at, :, c:c + FF // 2] = total
                else:
                    ex_ref[at, c - 2 * FF:c - 2 * FF + FF // 2, :] = total.T
        v = x_ref[...].astype(f32)
        inv = lax.rsqrt(jnp.mean(v * v, axis=1, keepdims=True) + EPS)
        n = v * inv
        w = d_ref[...] * g_ref[...]
        t_ref[...] = r_ref[...] + inv * (w - n * jnp.mean(w * n, axis=1, keepdims=True))
        out_ref[...] = s_ref[...] + y_ref[...] + f_ref[...].astype(f32)
        for k in range(D // AUX):
            parts = [w_ref[p, k].astype(f32) for p in range(senders)]
            o_ref[:, k * AUX:(k + 1) * AUX] = functools.reduce(lambda a, b: a + b, parts)
        small = 0.0
        for h in range(groups):
            row = 0.0
            for p in range(rp):
                row = row + p_ref[h, p].astype(f32)
            q_ref[:, h * QCOLS:(h + 1) * QCOLS] = row[:, :QCOLS]
            k_ref[:, h * HW:(h + 1) * HW] = row[:, QCOLS:QCOLS + HW]
            v_ref[:, h * HW:(h + 1) * HW] = row[:, QCOLS + HW:ROUTER_AT]
            small = small + row[:, 2 * LANES:]
        m_ref[...] = small

    sh = lambda *shape: jax.ShapeDtypeStruct(shape, f32)
    return pl.pallas_call(
        kernel,
        out_shape=(sh(T, D), sh(S, HEADS * HW), sh(S, KV * HW), sh(S, KV * HW), sh(S, LANES), sh(S, D), sh(T, D),
                   sh(2, dz, 2 * FF), sh(2, FF, dz)),
        in_specs=[VMEM] * (9 + m),
        out_specs=(VMEM,) * 9,
        compiler_params=pltpu.CompilerParams(vmem_limit_bytes=60 * MIB),
        cost_estimate=NO_COST,
        name="finish",
    )(dh1, x, gain, dresid, pin, win, resid, ysum, yfar, *grads)


def locate(rows, lengths):
    passed = rows[:, None] >= jnp.cumsum(lengths)
    return jnp.sum(jnp.where(passed, lengths, 0), axis=-1)


def norm_rows(v, gain):
    inverse = lax.rsqrt(jnp.mean(v * v, axis=-1, keepdims=True) + EPS)
    normed = v * inverse
    return normed, inverse, normed * gain


def rows_of(a, start, count):
    return a if a.shape[0] == count else lax.dynamic_slice_in_dim(a, start, count, 0)


def widen(a, start, count):
    if a.shape[0] == count:
        return a
    return lax.dynamic_update_slice_in_dim(jnp.zeros((count,) + a.shape[1:], a.dtype), a, start, 0)


def on_device(tokens, lengths, routes, gain_attn, w_query, w_key, w_value, w_output, gain_moe,
              w_router, w_inner, w_outer, cotangent):
    nz = lax.axis_size("ulysses")
    nb = lax.axis_size("blk")
    z = lax.axis_index("ulysses")
    b = lax.axis_index("blk")
    T = tokens.shape[0]
    R = nb * T
    rp = nb // KV
    Rq = R // rp
    part = b % rp
    at = part * Rq
    n = nz * nb
    S = D // n
    E = w_router.shape[1]
    longest = min(LENMAX, n * T // 2)
    back = min(nz - 1, (longest - 1 + R - 1) // R)
    n_o = QCOLS // S
    odd = z % 2

    lanes = jnp.arange(LANES, dtype=jnp.int32)
    extra = (jnp.pad(w_router, ((0, 0), (HW, LANES - HW - E))), HW + E)
    gains = jnp.stack([gain_attn, gain_moe]).astype(f32)
    pieces, cot_mask, same_a, same_b, other = prepare(
        w_query, w_key, w_value, extra, gains, w_inner, w_outer, cotangent, routes)
    W = 3 * FF
    half = W // 2
    early = min(2, nz - 1)
    xg, packed, wo, g_own, g_far, first = gather_inputs(
        tokens, pieces, w_output, cot_mask, same_a if early % 2 == 0 else other[:, :half], early, nz, nb, 0)
    xg = xg.reshape(R, D)
    packed = packed.reshape(D, AUX)
    router = packed[:, 2 * LANES:]
    gains = packed[:, ROUTER_AT + E:ROUTER_AT + E + 2].astype(f32).T
    gain1, gain2 = gains[0:1], gains[1:2]

    flip = lambda d: [(k, k ^ d) for k in range(nz)]
    give = lambda w, d: lax.ppermute(w, "ulysses", flip(d))
    second, packed = lax.optimization_barrier((same_b if early % 2 == 0 else other[:, half:], packed))
    second = give(second, early)
    weights = [(same_a, 0, 0), (same_b, 0, half), (first, early, 0)]

    rows = z * R + jnp.arange(R, dtype=jnp.int32)
    opening = locate(rows, lengths)
    pair = lanes % HW
    frequency = THETA ** (-((pair % (HW // 2)).astype(f32) * 2.0 / HW))
    angles = (rows - opening).astype(f32)[:, None] * frequency[None, :]
    cos, sin = jnp.cos(angles), jnp.sin(angles)
    tables = (cos, jnp.where(pair < HW // 2, -sin, 0.0), jnp.where(pair < HW // 2, 0.0, sin))

    q, kv, h1 = project(xg, gain1, packed, *tables)
    if rp > 1:
        q = lax.dynamic_slice_in_dim(q, at, Rq, 1)
    kv, second = lax.optimization_barrier((kv, second))
    weights.append((second, early, half))
    far, g_oth = halo_forward(kv, g_far, nz, nb, back, 1)
    g_own, g_oth = g_own.reshape(R, D + LANES), g_oth.reshape(R, D + LANES)
    wo = wo.reshape(QCOLS, D)
    same_a, same_b, other, far = lax.optimization_barrier((same_a, same_b, other, far))
    for d in range(1, nz):
        if d % 2 and d != early:
            weights.append((give(other, d), d, 0))
        elif d != early:
            weights += [(give(same_a, d), d, 0), (give(same_b, d), d, half)]
    kv_all = jnp.concatenate([far[d - 1] for d in range(back, 0, -1)] + [kv], axis=0)
    base = (z - back) * R
    starts = rows_of(opening, at, Rq) - base
    meta = jnp.concatenate([starts[::BQ] // BK, (back * R + at)[None]]).astype(jnp.int32)
    starts = starts[:, None]
    mixed, lse = attend(q, kv_all, starts, meta)
    attn = reduce_product(widen(mixed, at, R), wo, nb, 2)

    resid = tokens.astype(f32) + attn
    n2, inv2, scaled2 = norm_rows(resid, gain2)
    h2_own = scaled2.astype(bf16)
    hot = (lanes == HW + b * EXP_DEV + odd).astype(f32)[None, :]
    sent = (early, 0, FF)
    leave = [(0, 0, W), (early, FF, W - FF), (nz - 1, 0, half), (nz - 1, half, half)]
    leave += [(d, 0, W) for d in range(1, nz - 1) if d != early]
    y, dresid, dattn, dlogits, d_gain2, *grads = experts(
        h2_own, g_own, g_oth, router, hot, n2, inv2, gain2, cot_mask, weights, sent, leave, nz, nb, 3)
    grads, got = grads[:len(leave)], grads[len(leave)]

    grads = [grads[0]] + [give(a, d) for a, (d, _, _) in zip(grads[1:], leave[1:])]
    dattn, ysum, yfar = middle(dattn, y, nb, 5)
    dattn = dattn.reshape(R, D)
    tail = mm(h2_own, dlogits, TN) + jnp.where(lanes == HW + E, d_gain2[0][:, None], 0.0)

    dq, dkv, dwo = attend_back(q, kv_all, starts, meta, lse, mixed, rows_of(dattn, at, Rq), wo)
    dkv, *grads = lax.optimization_barrier((dkv, *grads))
    dkv = dkv.reshape(back + 1, R, LANES)
    dkv_out = jnp.stack([dkv[back - d] for d in range(back + 1)]).astype(bf16)
    kin, yfar = halo_back(dkv_out, yfar, nz, nb, rp, back, 6)
    ok = [(z + d < nz) if d else (part != p) for d in range(back + 1) for p in range(rp)]
    ok = jnp.stack([jnp.asarray(o).astype(jnp.int32) for o in ok] + [jnp.int32(HW + E)])
    if rp > 1:
        kin = lax.dynamic_slice_in_dim(kin, at, Rq, 1)
    turned, dw = weight_grads(
        dq, rows_of(dkv[back], at, Rq), kin, ok, [rows_of(t, at, Rq) for t in tables],
        rows_of(h1, at, Rq), packed, tail)
    wide = D // AUX
    dwo = dwo.astype(bf16).reshape(nz, rp, S, wide, AUX)
    dwo = jnp.transpose(dwo, (0, 1, 3, 2, 4)).reshape(nz, rp * wide, S, AUX)
    last = jnp.concatenate([dw.reshape(nz, nb, S, AUX), dwo], axis=1)
    dh1, pin, win = reduce_last(widen(turned, at, R), packed, last, nz, nb, rp, 7)
    d_tokens, d_query, d_key, d_value, small, d_output, out, d_inner, d_outer = finish(
        dh1, tokens, gain1, dresid, pin.reshape(KV, rp, S, AUX), win, resid, ysum, yfar,
        grads + [got], leave + [sent])
    return (
        out, d_tokens, small[:, HW + E + 1], d_query, d_key, d_value, d_output,
        small[:, HW + E], small[:, HW:HW + E], d_inner, d_outer,
    )


def solution(mesh):
    both = ("ulysses", "blk")
    rows = P(both, None)
    weights = (P(both), rows, rows, rows, rows, P(both), rows, P("blk", "ulysses", None), P("blk", None, "ulysses"))
    return jax.shard_map(
        on_device,
        mesh=mesh,
        in_specs=(rows, P(), rows) + weights + (rows,),
        out_specs=(rows, rows) + weights,
        check_vma=False,
    )
```
